32 devices in a mesh: dp: 4 (over x, core), ctx: 8 (over z, y).
Axes of the slice: x: 2, y: 2, z: 4, core: 2. Of those that a mesh axis runs over, the one named last changes fastest.
Arguments:
- tokens: bfloat16 [8, 1024, 2048], P('dp', 'ctx'), may hold values from -6 to 6
- cotangent: bfloat16 [8, 1024, 2048], P('dp', 'ctx'), may hold values from -6 to 6
- counts: int32 [4], P('dp'), may hold values from 1 to 2, as said below
- query_weight: bfloat16 [2048, 2048], P('dp', 'ctx'), may hold values from -0.125 to 0.125
- key_weight: bfloat16 [2048, 2048], P('dp', 'ctx'), may hold values from -0.125 to 0.125
- value_weight: bfloat16 [2048, 2048], P('dp', 'ctx'), may hold values from -0.125 to 0.125
- output_weight: bfloat16 [2048, 2048], P('dp', 'ctx'), may hold values from -1.5 to 1.5
- gate_weight: bfloat16 [2048, 8192], P('dp', 'ctx'), may hold values from -0.125 to 0.125
- up_weight: bfloat16 [2048, 8192], P('dp', 'ctx'), may hold values from -0.125 to 0.125
- down_weight: bfloat16 [8192, 2048], P('dp', 'ctx'), may hold values from -0.0625 to 0.0625
Outputs:
- mixed: bfloat16 [8, 1024, 2048], P('dp', 'ctx')
- token_grad: float32 [8, 1024, 2048], P('dp', 'ctx')
- grad_query_weight: float32 [2048, 2048], P('dp', 'ctx')
- grad_key_weight: float32 [2048, 2048], P('dp', 'ctx')
- grad_value_weight: float32 [2048, 2048], P('dp', 'ctx')
- grad_output_weight: float32 [2048, 2048], P('dp', 'ctx')
- grad_gate_weight: float32 [2048, 8192], P('dp', 'ctx')
- grad_up_weight: float32 [2048, 8192], P('dp', 'ctx')
- grad_down_weight: float32 [8192, 2048], P('dp', 'ctx')
The draws below stay inside these ranges and needn't reach their ends.
Inputs may be any that keep to these rules, and one draw needn't show every extreme that they name: Group g holds sequences in its slots 0 to counts[g] - 1; some group holds 2 and some group holds 1.
All inputs are finite; a program needn't handle non-finite values.
Results may differ from the reference program's by a relative error of at most 0.02.
Values may be sent and summed in bfloat16 or wider, within the bound.
No kernel may reach another device: no remote copies, remote signals or barrier semaphores. Data moves between devices by JAX's collectives and lax.ppermute only.
A program may use at most 704 MiB of HBM per device.

```python
import math
import jax
import jax.numpy as jnp
from jax import lax

D = 2048
HEADS = 16
HEAD_DIM = 128
FF = 8192
MB_MAX = 2
L = 1024
GROUPS = 4
SLOTS = 8
N_CTX = 8


def draw_counts(key, part):
    key = jax.random.fold_in(key, 7)
    first_key, second_key = jax.random.split(key)
    drawn = jax.random.randint(first_key, (GROUPS,), 1, MB_MAX + 1)
    order = jax.random.permutation(second_key, GROUPS)
    drawn = drawn.at[order[0]].set(MB_MAX)
    drawn = drawn.at[order[1]].set(1)
    return drawn.astype(jnp.int32)


def steps_of(own_key, shape, cuts, least, largest):
    level = 1.0
    for axis_at, shards_of in cuts:
        draws = jax.random.uniform(jax.random.fold_in(jax.random.fold_in(own_key, 6), axis_at), (shards_of,), jnp.float32, least / len(cuts), largest / len(cuts))
        level = level * jnp.repeat(jnp.exp(draws), shape[axis_at] // shards_of).reshape((-1,) + (1,) * (len(shape) - 1 - axis_at))
    return level


def normal_values(rng, extent, width, limit, shards=(), kind=jnp.bfloat16):
    array = jax.random.normal(rng, extent, jnp.float32) * width
    if len(shards) > 0:
        array = steps_of(rng, extent, shards, -0.22, 0.18) * array
    return jnp.clip(array, min=-limit, max=limit).astype(kind)


def setup_inputs(seed: int = 0) -> dict:
    key_of = jax.random.split(jax.random.key(seed), 11)
    return {
        "tokens": normal_values(key_of[0], (SLOTS, L, D), 1.0, 6.0, ((0, 4), (1, 8))),
        "cotangent": normal_values(key_of[1], (SLOTS, L, D), 1.0, 6.0, ((0, 4), (1, 8))),
        "counts": draw_counts(jax.random.fold_in(key_of[10], 71), 0),
        "query_weight": normal_values(key_of[3], (D, HEADS * HEAD_DIM), D ** -0.5, 0.125, ((0, 4), (1, 8))),
        "key_weight": normal_values(key_of[4], (D, HEADS * HEAD_DIM), D ** -0.5, 0.125, ((0, 4), (1, 8))),
        "value_weight": normal_values(key_of[5], (D, HEADS * HEAD_DIM), D ** -0.5, 0.125, ((0, 4), (1, 8))),
        "output_weight": normal_values(key_of[6], (HEADS * HEAD_DIM, D), (max(1, 8 * HEADS * HEAD_DIM // L)) ** -0.5, 1.5, ((0, 4), (1, 8))),
        "gate_weight": normal_values(key_of[7], (D, FF), D ** -0.5, 0.125, ((0, 4), (1, 8))),
        "up_weight": normal_values(key_of[8], (D, FF), D ** -0.5, 0.125, ((0, 4), (1, 8))),
        "down_weight": normal_values(key_of[9], (FF, D), FF ** -0.5, 0.0625, ((0, 4), (1, 8))),
    }


epsilon = 1e-05
rope_base = 10000.0
highest = lax.Precision.HIGHEST

@jax.custom_vjp
def low(v):
    return lax.optimization_barrier(v.astype(jnp.bfloat16)).astype(jnp.float32)

@jax.custom_vjp
def low_back(v):
    return v

def low_keep(v):
    return (low(v), None)

def low_pass(kept, grad):
    return (grad,)

def back_keep(v):
    return (v, None)

def back_low(kept, grad):
    return (low(grad),)
low.defvjp(low_keep, low_pass)
low_back.defvjp(back_keep, back_low)

def product(left, right):
    return jnp.dot(left, right, precision=highest)

def layer_norm(values):
    centred = values - lax.optimization_barrier(jnp.mean(values, axis=-1, keepdims=True))
    variance = lax.optimization_barrier(jnp.mean(centred * centred, axis=-1, keepdims=True))
    return centred * lax.rsqrt(variance + epsilon)

def paired_positions(row_index, tok_rows, blocks):
    half_block = tok_rows // 2
    device = row_index // tok_rows
    offset = row_index % tok_rows
    return jnp.where(offset < half_block, device * half_block + offset, (2 * blocks - 1 - device) * half_block + offset - half_block)

def rope_tables(positions):
    half_dim = HEAD_DIM // 2
    frequency = rope_base ** (-jnp.arange(half_dim, dtype=jnp.float32) / half_dim)
    angles = positions.astype(jnp.float32)[:, None] * frequency[None, :]
    return (jnp.cos(angles)[:, None, :], jnp.sin(angles)[:, None, :])

def rotate(values, cosine_table, sine_table):
    half_dim = values.shape[-1] // 2
    first_half = values[..., :half_dim]
    second_half = values[..., half_dim:]
    return jnp.concatenate([first_half * cosine_table - second_half * sine_table, second_half * cosine_table + first_half * sine_table], axis=-1)

def attention(queries, keys, values, positions):
    row_count = queries.shape[0]
    block_rows = math.gcd(row_count, 512)
    score_scale = HEAD_DIM ** (-0.5)
    key_heads = keys.reshape(row_count, HEADS, HEAD_DIM)
    value_heads = values.reshape(row_count, HEADS, HEAD_DIM)

    def one_block(block_item):
        query_block, block_positions = block_item
        query_heads = query_block.reshape(block_rows, HEADS, HEAD_DIM)
        scores = low_back(jnp.einsum('qhd,khd->hqk', query_heads, key_heads, precision=highest)) * score_scale
        allowed = block_positions[None, :, None] >= positions[None, None, :]
        scores = jnp.where(allowed, scores, -1e+30)
        shifted = jnp.exp(scores - lax.optimization_barrier(jnp.max(scores, axis=-1, keepdims=True)))
        soft_weights = low(shifted / lax.optimization_barrier(jnp.sum(shifted, axis=-1, keepdims=True)))
        attended = jnp.einsum('hqk,khd->qhd', soft_weights, value_heads, precision=highest)
        return attended.reshape(block_rows, HEADS * HEAD_DIM)
    block_outs = lax.map(jax.checkpoint(one_block), (queries.reshape(row_count // block_rows, block_rows, HEADS * HEAD_DIM), positions.reshape(row_count // block_rows, block_rows)))
    return block_outs.reshape(row_count, HEADS * HEAD_DIM)

def forward(inputs, weights, positions):
    query_weight, key_weight, value_weight, output_weight, gate_weight, up_weight, down_weight = weights
    row_count = inputs.shape[0]
    cosine_table, sine_table = rope_tables(positions)
    norm_in = low(layer_norm(inputs))
    query_proj = low_back(product(norm_in, query_weight)).reshape(row_count, HEADS, HEAD_DIM)
    key_proj = low_back(product(norm_in, key_weight)).reshape(row_count, HEADS, HEAD_DIM)
    queries = low(rotate(query_proj, cosine_table, sine_table)).reshape(row_count, HEADS * HEAD_DIM)
    keys = low(rotate(key_proj, cosine_table, sine_table)).reshape(row_count, HEADS * HEAD_DIM)
    values = low_back(low(product(norm_in, value_weight)))
    attended = low_back(low(attention(queries, keys, values, positions)))
    after_attn = inputs + low_back(product(attended, output_weight))
    norm_mid = low(layer_norm(after_attn))
    gate_proj = low_back(product(norm_mid, gate_weight))
    up_proj = low_back(product(norm_mid, up_weight))
    hidden = low(jax.nn.silu(gate_proj) * up_proj)
    return after_attn + low_back(product(hidden, down_weight))

def reference(tokens, cotangent, counts, query_weight, key_weight, value_weight, output_weight, gate_weight, up_weight, down_weight):
    float_weights = tuple((weight.astype(jnp.float32) for weight in (query_weight, key_weight, value_weight, output_weight, gate_weight, up_weight, down_weight)))
    slot_index = jnp.arange(SLOTS, dtype=jnp.int32)
    live_mask = (slot_index % MB_MAX < counts[slot_index // MB_MAX]).astype(jnp.float32)
    positions = paired_positions(jnp.arange(L, dtype=jnp.int32), L // N_CTX, N_CTX)

    def slot_step(running, block_item):
        slot_tokens, slot_cotangent, slot_live = block_item
        layer_out, layer_back = jax.vjp(lambda inputs, *weights: forward(inputs, weights, positions), slot_tokens.astype(jnp.float32), *float_weights)
        gradients = layer_back(slot_cotangent.astype(jnp.float32) * slot_live)
        updated = tuple((before + after for before, after in zip(running, gradients[1:])))
        return (updated, (layer_out * slot_live, gradients[0]))
    initial = tuple((jnp.zeros_like(weight) for weight in float_weights))
    totals, (layer_outs, token_grad) = lax.scan(slot_step, initial, (tokens, cotangent, live_mask))
    return (layer_outs.astype(jnp.bfloat16), token_grad, totals[0], totals[1], totals[2], totals[3], totals[4], totals[5], totals[6])
```

```python
import functools

import jax
import jax.numpy as jnp
from jax import lax
from jax.experimental import pallas as pl
from jax.experimental.pallas import tpu as pltpu
from jax.sharding import Mesh
from jax.sharding import PartitionSpec as P

HEADS = 16
HEAD_DIM = 128
FF = 8192


epsilon = 1e-05
rope_base = 10000.0


def layer_norm(values):
    centred = values - jnp.mean(values, axis=-1, keepdims=True)
    variance = jnp.mean(centred * centred, axis=-1, keepdims=True)
    return centred * lax.rsqrt(variance + epsilon)


def paired_positions(row_index, tok_rows, blocks):
    half_block = tok_rows // 2
    device = row_index // tok_rows
    offset = row_index % tok_rows
    return jnp.where(
        offset < half_block,
        device * half_block + offset,
        (2 * blocks - 1 - device) * half_block + offset - half_block,
    )


def rope_tables(positions):
    half_dim = HEAD_DIM // 2
    frequency = rope_base ** (-jnp.arange(half_dim, dtype=jnp.float32) / half_dim)
    angles = positions.astype(jnp.float32)[:, None] * frequency[None, :]
    return (jnp.cos(angles)[:, None, :], jnp.sin(angles)[:, None, :])


def rotate(values, cosine_table, sine_table):
    half_dim = values.shape[-1] // 2
    first_half = values[..., :half_dim]
    second_half = values[..., half_dim:]
    return jnp.concatenate(
        [
            first_half * cosine_table - second_half * sine_table,
            second_half * cosine_table + first_half * sine_table,
        ],
        axis=-1,
    )


def outer_sum(left, right):
    return lax.dot_general(
        left, right, (((0,), (0,)), ((), ())), preferred_element_type=jnp.float32
    )


def back_product(grad_rows, weight):
    return lax.dot_general(
        grad_rows, weight, (((1,), (1,)), ((), ())), preferred_element_type=jnp.float32
    )


def block_start(block, tile_span, blocks):
    upper_side = (block >= blocks // tile_span).astype(jnp.int32)
    lead_tile = jnp.where(
        upper_side == 0, block * tile_span, 2 * blocks - (block + 1) * tile_span
    ).astype(jnp.int32)
    return (lead_tile, upper_side)


def tile_starts(tiles, lead_tile, upper_side):
    zero_index = jnp.zeros((), jnp.int32)
    return (lead_tile, upper_side) + (zero_index,) * (tiles.ndim - 2)


def take_block(tiles, lead_tile, upper_side, tile_span):
    piece = lax.dynamic_slice(
        tiles, tile_starts(tiles, lead_tile, upper_side), (tile_span, 1) + tiles.shape[2:]
    )
    return piece.reshape((tile_span * tiles.shape[2],) + tiles.shape[3:])


def add_block(tiles, part, lead_tile, upper_side, tile_span):
    starts = tile_starts(tiles, lead_tile, upper_side)
    piece_shape = (tile_span, 1) + tiles.shape[2:]
    before = lax.dynamic_slice(tiles, starts, piece_shape)
    return lax.dynamic_update_slice(tiles, before + part.reshape(piece_shape), starts)


def block_scores(query_half, query_pos, key_block, key_pos):
    scores = jnp.einsum(
        "qhd,khd->hqk", query_half, key_block, preferred_element_type=jnp.float32
    ) * HEAD_DIM ** (-0.5)
    allowed = query_pos[:, None] >= key_pos[None, :]
    return jnp.where(allowed[None, :, :], scores, -1e30)


def attend_half(query_half, query_pos, tables, needed, tile_span, blocks):
    key_tiles, value_tiles, pos_tiles = tables
    row_count = query_half.shape[0]

    def scores_at(block):
        lead_tile, upper_side = block_start(block, tile_span, blocks)
        key_block = take_block(key_tiles, lead_tile, upper_side, tile_span)
        key_pos = take_block(pos_tiles, lead_tile, upper_side, tile_span)
        return (block_scores(query_half, query_pos, key_block, key_pos), lead_tile, upper_side)

    def total_step(block, carried):
        highest, total_mass = carried
        scores = scores_at(block)[0]
        new_highest = jnp.maximum(highest, jnp.max(scores, axis=-1))
        total_mass = total_mass * jnp.exp(highest - new_highest) + jnp.sum(
            jnp.exp(scores - new_highest[..., None]), axis=-1
        )
        return (new_highest, total_mass)

    start_high = jnp.full((HEADS, row_count), -1e30, jnp.float32)
    highest, total_mass = lax.fori_loop(
        0, needed, total_step, (start_high, jnp.zeros((HEADS, row_count), jnp.float32))
    )
    log_total = highest + jnp.log(total_mass)

    def value_step(block, output_rows):
        scores, lead_tile, upper_side = scores_at(block)
        soft_low = jnp.exp(scores - log_total[..., None]).astype(jnp.bfloat16)
        value_block = take_block(value_tiles, lead_tile, upper_side, tile_span)
        return output_rows + jnp.einsum(
            "hqk,khd->qhd", soft_low, value_block, preferred_element_type=jnp.float32
        )

    output_rows = lax.fori_loop(
        0, needed, value_step, jnp.zeros((row_count, HEADS, HEAD_DIM), jnp.float32)
    )
    return (output_rows, log_total)


def attend_half_back(
    query_half,
    query_pos,
    grad_half,
    log_total,
    centre,
    tables,
    needed,
    tile_span,
    blocks,
    key_grad,
    value_grad,
):
    key_tiles, value_tiles, pos_tiles = tables
    score_scale = HEAD_DIM ** (-0.5)

    def back_step(block, state):
        query_grad, key_acc, value_acc = state
        lead_tile, upper_side = block_start(block, tile_span, blocks)
        key_block = take_block(key_tiles, lead_tile, upper_side, tile_span)
        value_block = take_block(value_tiles, lead_tile, upper_side, tile_span)
        key_pos = take_block(pos_tiles, lead_tile, upper_side, tile_span)
        soft = jnp.exp(
            block_scores(query_half, query_pos, key_block, key_pos) - log_total[..., None]
        )
        value_part = jnp.einsum(
            "hqk,qhd->khd", soft.astype(jnp.bfloat16), grad_half, preferred_element_type=jnp.float32
        )
        grad_soft = jnp.einsum(
            "qhd,khd->hqk", grad_half, value_block, preferred_element_type=jnp.float32
        )
        grad_scores = (soft * (grad_soft - centre[..., None]) * score_scale).astype(jnp.bfloat16)
        query_grad = query_grad + jnp.einsum(
            "hqk,khd->qhd", grad_scores, key_block, preferred_element_type=jnp.float32
        )
        key_part = jnp.einsum(
            "hqk,qhd->khd", grad_scores, query_half, preferred_element_type=jnp.float32
        )
        key_acc = add_block(key_acc, key_part, lead_tile, upper_side, tile_span)
        value_acc = add_block(value_acc, value_part, lead_tile, upper_side, tile_span)
        return (query_grad, key_acc, value_acc)

    initial = (jnp.zeros(query_half.shape, jnp.float32), key_grad, value_grad)
    return lax.fori_loop(0, needed, back_step, initial)


def gather_weights(
    query_weight, key_weight, value_weight, output_weight, gate_weight, up_weight, down_weight
):
    row_parts = (
        lax.all_gather(query_weight, "dp", axis=0, tiled=True),
        lax.all_gather(key_weight, "dp", axis=0, tiled=True),
        lax.all_gather(value_weight, "dp", axis=0, tiled=True),
        lax.all_gather(output_weight, "dp", axis=0, tiled=True),
        lax.all_gather(gate_weight, "dp", axis=0, tiled=True),
        lax.all_gather(up_weight, "dp", axis=0, tiled=True),
        lax.all_gather(down_weight, "dp", axis=0, tiled=True),
    )
    return (
        lax.all_gather(row_parts[0], "ctx", axis=1, tiled=True),
        lax.all_gather(row_parts[1], "ctx", axis=1, tiled=True),
        lax.all_gather(row_parts[2], "ctx", axis=1, tiled=True),
        lax.all_gather(row_parts[3], "ctx", axis=1, tiled=True),
        lax.all_gather(row_parts[4], "ctx", axis=1, tiled=True),
        lax.all_gather(row_parts[5], "ctx", axis=1, tiled=True),
        lax.all_gather(row_parts[6], "ctx", axis=1, tiled=True),
    )


def fold_columns(running, operands, grads):
    norm_in_low, attended_low, norm_mid_low, hidden_low = operands
    columns = (
        lax.all_to_all(grads[0], "ctx", split_axis=1, concat_axis=0, tiled=True),
        lax.all_to_all(grads[1], "ctx", split_axis=1, concat_axis=0, tiled=True),
        lax.all_to_all(grads[2], "ctx", split_axis=1, concat_axis=0, tiled=True),
        lax.all_to_all(grads[3], "ctx", split_axis=1, concat_axis=0, tiled=True),
        lax.all_to_all(grads[4], "ctx", split_axis=1, concat_axis=0, tiled=True),
        lax.all_to_all(grads[5], "ctx", split_axis=1, concat_axis=0, tiled=True),
        lax.all_to_all(grads[6], "ctx", split_axis=1, concat_axis=0, tiled=True),
    )
    totals = tuple(running)
    norm_in_piece = lax.all_gather(norm_in_low, "ctx", axis=0, tiled=True)
    attended_piece = lax.all_gather(attended_low, "ctx", axis=0, tiled=True)
    norm_mid_piece = lax.all_gather(norm_mid_low, "ctx", axis=0, tiled=True)
    hidden_piece = lax.all_gather(hidden_low, "ctx", axis=0, tiled=True)
    lefts = (
        norm_in_piece,
        norm_in_piece,
        norm_in_piece,
        attended_piece,
        norm_mid_piece,
        norm_mid_piece,
        hidden_piece,
    )
    return list(
        tuple(
            (total + outer_sum(left, column) for total, left, column in zip(totals, lefts, columns))
        )
    )


def body(
    tokens,
    cotangent,
    counts,
    query_weight,
    key_weight,
    value_weight,
    output_weight,
    gate_weight,
    up_weight,
    down_weight,
):
    slot_count, tok_rows, model_width = tokens.shape
    blocks = lax.axis_size("ctx")
    ctx_index = lax.axis_index("ctx")
    seq_rows = tok_rows * blocks
    half_rows = tok_rows // 2
    proj_width = HEADS * HEAD_DIM
    tile_span = min(512, seq_rows // 2) // half_rows
    first_needed = ctx_index // tile_span + 1
    second_needed = (2 * blocks - 1 - ctx_index) // tile_span + 1
    own_positions = paired_positions(
        ctx_index * tok_rows + jnp.arange(tok_rows, dtype=jnp.int32), tok_rows, blocks
    )
    pos_tiles = paired_positions(jnp.arange(seq_rows, dtype=jnp.int32), tok_rows, blocks).reshape(
        blocks, 2, half_rows
    )
    cosine_table, sine_table = rope_tables(own_positions)

    def rotate_heads(projected):
        return rotate(
            projected.reshape(tok_rows, HEADS, HEAD_DIM), cosine_table, sine_table
        ).reshape(tok_rows, proj_width)

    running = [
        jnp.zeros((model_width, proj_width // blocks), jnp.float32),
        jnp.zeros((model_width, proj_width // blocks), jnp.float32),
        jnp.zeros((model_width, proj_width // blocks), jnp.float32),
        jnp.zeros((proj_width, model_width // blocks), jnp.float32),
        jnp.zeros((model_width, FF // blocks), jnp.float32),
        jnp.zeros((model_width, FF // blocks), jnp.float32),
        jnp.zeros((FF, model_width // blocks), jnp.float32),
    ]
    outputs = []
    token_grads = []
    for slot_index in range(slot_count):
        gathered = gather_weights(
            query_weight,
            key_weight,
            value_weight,
            output_weight,
            gate_weight,
            up_weight,
            down_weight,
        )
        full_query, full_key, full_value, full_output, full_gate, full_up, full_down = gathered
        live_mask = (slot_index < counts[0]).astype(jnp.float32)
        inputs = tokens[slot_index].astype(jnp.float32)
        normed_in, norm_in_back = jax.vjp(layer_norm, inputs)
        norm_in_low = normed_in.astype(jnp.bfloat16)
        query_proj = jnp.dot(norm_in_low, full_query, preferred_element_type=jnp.float32)
        key_proj = jnp.dot(norm_in_low, full_key, preferred_element_type=jnp.float32)
        value_proj = jnp.dot(norm_in_low, full_value, preferred_element_type=jnp.float32)
        query_rot, query_turn_back = jax.vjp(rotate_heads, query_proj)
        key_rot, key_turn_back = jax.vjp(rotate_heads, key_proj)
        query_heads = query_rot.astype(jnp.bfloat16).reshape(tok_rows, HEADS, HEAD_DIM)
        key_rows, value_rows = (
            lax.all_gather(key_rot.astype(jnp.bfloat16), "ctx", axis=0, tiled=True),
            lax.all_gather(value_proj.astype(jnp.bfloat16), "ctx", axis=0, tiled=True),
        )
        tables = (
            key_rows.reshape(blocks, 2, half_rows, HEADS, HEAD_DIM),
            value_rows.reshape(blocks, 2, half_rows, HEADS, HEAD_DIM),
            pos_tiles,
        )
        first_out, first_total = attend_half(
            query_heads[:half_rows],
            own_positions[:half_rows],
            tables,
            first_needed,
            tile_span,
            blocks,
        )
        second_out, second_total = attend_half(
            query_heads[half_rows:],
            own_positions[half_rows:],
            tables,
            second_needed,
            tile_span,
            blocks,
        )
        attended_wide = jnp.concatenate([first_out, second_out], axis=0)
        attended_low = attended_wide.reshape(tok_rows, proj_width).astype(jnp.bfloat16)
        after_attn = inputs + jnp.dot(attended_low, full_output, preferred_element_type=jnp.float32)
        normed_mid, norm_mid_back = jax.vjp(layer_norm, after_attn)
        norm_mid_low = normed_mid.astype(jnp.bfloat16)
        gate_proj = jnp.dot(norm_mid_low, full_gate, preferred_element_type=jnp.float32)
        up_proj = jnp.dot(norm_mid_low, full_up, preferred_element_type=jnp.float32)
        hidden, hidden_back = jax.vjp(
            lambda gate_in, up_in: jax.nn.silu(gate_in) * up_in, gate_proj, up_proj
        )
        hidden_low = hidden.astype(jnp.bfloat16)
        layer_out = after_attn + jnp.dot(hidden_low, full_down, preferred_element_type=jnp.float32)
        outputs.append((layer_out * live_mask).astype(jnp.bfloat16))
        grad_out = cotangent[slot_index].astype(jnp.float32) * live_mask
        grad_out_low = grad_out.astype(jnp.bfloat16)
        grad_gate_in, grad_up_in = hidden_back(back_product(grad_out_low, full_down))
        grad_gate_low = grad_gate_in.astype(jnp.bfloat16)
        grad_up_low = grad_up_in.astype(jnp.bfloat16)
        grad_norm_mid = back_product(grad_gate_low, full_gate) + back_product(grad_up_low, full_up)
        grad_after = grad_out + norm_mid_back(grad_norm_mid)[0]
        grad_after_low = grad_after.astype(jnp.bfloat16)
        grad_attended_low = back_product(grad_after_low, full_output).astype(jnp.bfloat16)
        grad_heads = grad_attended_low.reshape(tok_rows, HEADS, HEAD_DIM)
        centre = jnp.einsum("qhd,qhd->hq", grad_heads.astype(jnp.float32), attended_wide)
        empty_tiles = jnp.zeros((blocks, 2, half_rows, HEADS, HEAD_DIM), jnp.float32)
        first_query, key_acc, value_acc = attend_half_back(
            query_heads[:half_rows],
            own_positions[:half_rows],
            grad_heads[:half_rows],
            first_total,
            centre[:, :half_rows],
            tables,
            first_needed,
            tile_span,
            blocks,
            empty_tiles,
            empty_tiles,
        )
        second_query, key_acc, value_acc = attend_half_back(
            query_heads[half_rows:],
            own_positions[half_rows:],
            grad_heads[half_rows:],
            second_total,
            centre[:, half_rows:],
            tables,
            second_needed,
            tile_span,
            blocks,
            key_acc,
            value_acc,
        )
        grad_query_rot = jnp.concatenate([first_query, second_query], axis=0).reshape(
            tok_rows, proj_width
        )
        key_share, value_share = (
            lax.psum_scatter(
                key_acc.reshape(seq_rows, proj_width).astype(jnp.bfloat16),
                "ctx",
                scatter_dimension=0,
                tiled=True,
            ).astype(jnp.float32),
            lax.psum_scatter(
                value_acc.reshape(seq_rows, proj_width).astype(jnp.bfloat16),
                "ctx",
                scatter_dimension=0,
                tiled=True,
            ).astype(jnp.float32),
        )
        grad_query_low = query_turn_back(grad_query_rot)[0].astype(jnp.bfloat16)
        grad_key_low = key_turn_back(key_share)[0].astype(jnp.bfloat16)
        grad_value_low = value_share.astype(jnp.bfloat16)
        grad_norm_in = (
            back_product(grad_query_low, full_query)
            + back_product(grad_key_low, full_key)
            + back_product(grad_value_low, full_value)
        )
        token_grads.append(grad_after + norm_in_back(grad_norm_in)[0])
        grads = (
            grad_query_low,
            grad_key_low,
            grad_value_low,
            grad_after_low,
            grad_gate_low,
            grad_up_low,
            grad_out_low,
        )
        running = fold_columns(
            running, (norm_in_low, attended_low, norm_mid_low, hidden_low), grads
        )
    row_sums = (
        lax.psum_scatter(
            running[0].astype(jnp.bfloat16), "dp", scatter_dimension=0, tiled=True
        ).astype(jnp.float32),
        lax.psum_scatter(
            running[1].astype(jnp.bfloat16), "dp", scatter_dimension=0, tiled=True
        ).astype(jnp.float32),
        lax.psum_scatter(
            running[2].astype(jnp.bfloat16), "dp", scatter_dimension=0, tiled=True
        ).astype(jnp.float32),
        lax.psum_scatter(
            running[3].astype(jnp.bfloat16), "dp", scatter_dimension=0, tiled=True
        ).astype(jnp.float32),
        lax.psum_scatter(
            running[4].astype(jnp.bfloat16), "dp", scatter_dimension=0, tiled=True
        ).astype(jnp.float32),
        lax.psum_scatter(
            running[5].astype(jnp.bfloat16), "dp", scatter_dimension=0, tiled=True
        ).astype(jnp.float32),
        lax.psum_scatter(
            running[6].astype(jnp.bfloat16), "dp", scatter_dimension=0, tiled=True
        ).astype(jnp.float32),
    )
    return (
        jnp.stack(outputs),
        jnp.stack(token_grads),
        row_sums[0],
        row_sums[1],
        row_sums[2],
        row_sums[3],
        row_sums[4],
        row_sums[5],
        row_sums[6],
    )


PAIRS = ("x", "c", "w", "u", "v")
SWAP = ((0, 1), (1, 0))


def swap(value, axis):
    return lax.ppermute(value, axis, SWAP)


def join(own, other, bit, axis):
    low = jnp.where(bit == 0, own, other)
    high = jnp.where(bit == 0, other, own)
    return jnp.concatenate([low, high], axis=axis)


def low_bits(value):
    return value.astype(jnp.bfloat16)


def wide_bits(value):
    return value.astype(jnp.float32)


def half(value, bit, axis):
    size = value.shape[axis] // 2
    return lax.dynamic_slice_in_dim(value, bit * size, size, axis)


def split_column_weights(weights, c):
    kept = jnp.concatenate([half(weight, c, 1) for weight in weights], axis=1)
    sent = jnp.concatenate([half(weight, 1 - c, 1) for weight in weights], axis=1)
    return join(kept, swap(sent, "c"), c, 0)


def join_column_grads(total, c, counts):
    other = swap(low_bits(half(total, 1 - c, 0)), "c")
    kept = half(total, c, 0)
    grads, at = [], 0
    for count in counts:
        grads.append(join(wide_bits(kept[:, at : at + count]), wide_bits(other[:, at : at + count]), c, 1))
        at += count
    return grads


def split_row_weights(parts, spots):
    _, _, span, columns = parts.shape
    kept, other = half(parts, spots["c"], 1), half(parts, 1 - spots["c"], 1)
    parts = join(kept[:, 0], swap(other, "c")[:, 0], spots["c"], 0).reshape(2, 2, span, columns)
    kept, other = half(parts, spots["u"], 0), half(parts, 1 - spots["u"], 0)
    parts = join(kept[0], swap(other, "u")[0], spots["u"], 2)
    kept, other = half(parts, spots["v"], 0)[0], swap(half(parts, 1 - spots["v"], 0), "v")[0]
    low = jnp.where(spots["v"] == 0, kept, other)
    high = jnp.where(spots["v"] == 0, other, kept)
    return jnp.concatenate(
        [low[:, :columns], high[:, :columns], low[:, columns:], high[:, columns:]], axis=1
    )


def join_row_grads(total, spots):
    total = low_bits(total)
    span, columns = total.shape[0], total.shape[1] // 4
    even = jnp.concatenate([total[:, :columns], total[:, 2 * columns : 3 * columns]], axis=1)
    odd = jnp.concatenate([total[:, columns : 2 * columns], total[:, 3 * columns :]], axis=1)
    kept = jnp.where(spots["v"] == 0, even, odd)
    other = swap(jnp.where(spots["v"] == 0, odd, even), "v")
    parts = join(kept[None], other[None], spots["v"], 0)
    kept, other = half(parts, spots["u"], 2), half(parts, 1 - spots["u"], 2)
    parts = join(kept[None], swap(other, "u")[None], spots["u"], 0)
    kept, other = half(parts, spots["c"], 0), half(parts, 1 - spots["c"], 0)
    return join(kept[0][:, None], swap(other, "c")[0][:, None], spots["c"], 1)


def spread(piece):
    rows, columns = piece.shape
    return lax.all_gather(piece, ("w", "x"), axis=0, tiled=True).reshape(2, 2 * rows, columns)


def spread_by_pairs(piece, spots):
    beside = swap(piece, "w")
    across = swap(piece, "x")
    both = swap(beside, "x")
    own = join(piece, across, spots["x"], 0)
    other = join(beside, both, spots["x"], 0)
    return lax.optimization_barrier(join(own[None], other[None], spots["w"], 0))


def collect(grad):
    _, rows, columns = grad.shape
    return lax.psum_scatter(
        grad.reshape(2 * rows, columns), ("w", "x"), scatter_dimension=0, tiled=True
    )


def collect_by_pairs(grad, spots):
    kept, other = half(grad, spots["x"], 1), half(grad, 1 - spots["x"], 1)
    total = wide_bits(kept) + wide_bits(swap(other, "x"))
    kept, other = half(total, spots["w"], 0)[0], half(total, 1 - spots["w"], 0)[0]
    return kept + wide_bits(swap(low_bits(other), "w"))


def gather_rows(value):
    size = value.shape[0] // 2
    first, second = value[:size], value[size:]
    first_u = swap(first, "u")
    second_v = swap(second, "v")
    first_v = swap(first, "v")
    second_u = swap(second, "u")
    first_uv = swap(first_u, "v")
    second_uv = swap(second_v, "u")
    own = jnp.concatenate(
        [first, first_u, first_v, first_uv, second, second_v, second_u, second_uv], axis=0
    )
    return own, swap(own, "c")


def scatter_rows(total):
    size = total.shape[0] // 8
    first = total[: 4 * size]
    second = total[4 * size :]
    first = low_bits(wide_bits(first[: 2 * size]) + wide_bits(swap(first[2 * size :], "v")))
    second = low_bits(wide_bits(second[: 2 * size]) + wide_bits(swap(second[2 * size :], "u")))
    first = wide_bits(first[:size]) + wide_bits(swap(first[size:], "u"))
    second = wide_bits(second[:size]) + wide_bits(swap(second[size:], "v"))
    return jnp.concatenate([first, second], axis=0)


ACROSS = (((1,), (1,)), ((), ()))
DOWN = (((0,), (0,)), ((), ()))
CHUNK = 256


def dot(left, right, dims=(((1,), (0,)), ((), ()))):
    return lax.dot_general(left, right, dims, preferred_element_type=jnp.float32)


def whole(shape):
    return pl.BlockSpec(shape, lambda *_: (0,) * len(shape))


def kernel_call(kernel, grid, in_specs, out_specs, out_shape, flops, size, scratch=()):
    return pl.pallas_call(
        kernel,
        grid=grid,
        in_specs=in_specs,
        out_specs=out_specs,
        out_shape=out_shape,
        scratch_shapes=scratch,
        compiler_params=pltpu.CompilerParams(vmem_limit_bytes=48 * 2**20),
        cost_estimate=pl.CostEstimate(flops=flops, bytes_accessed=size, transcendentals=0),
    )


def turn(values, cosine, sine):
    return values * cosine + pltpu.roll(values, HEAD_DIM // 2, 1) * sine


def attend_kernel(rows_ref, weight_ref, cos_ref, sin_ref, pos_col_ref, pos_row_ref, turned_ref, out_ref):
    key_pos = pos_row_ref[...]
    rows = rows_ref.shape[0]

    @pl.loop(0, rows // CHUNK)
    def _(i):
        at = pl.ds(pl.multiple_of(i * CHUNK, CHUNK), CHUNK)
        proj = dot(rows_ref[at, :], weight_ref[0])
        cosine, sine = cos_ref[at, :], sin_ref[at, :]
        turned_ref[at, :HEAD_DIM] = low_bits(turn(proj[:, :HEAD_DIM], cosine, sine))
        turned_ref[at, HEAD_DIM : 2 * HEAD_DIM] = low_bits(
            turn(proj[:, HEAD_DIM : 2 * HEAD_DIM], cosine, sine)
        )
        turned_ref[at, 2 * HEAD_DIM :] = low_bits(proj[:, 2 * HEAD_DIM :])

    @pl.loop(0, rows // CHUNK)
    def _(i):
        at = pl.ds(pl.multiple_of(i * CHUNK, CHUNK), CHUNK)
        scores = dot(turned_ref[at, :HEAD_DIM], turned_ref[:, HEAD_DIM : 2 * HEAD_DIM], ACROSS)
        scores = scores * HEAD_DIM ** (-0.5)
        scores = jnp.where(pos_col_ref[at, :] >= key_pos, scores, -1e30)
        shifted = jnp.exp(scores - jnp.max(scores, axis=1, keepdims=True))
        soft = shifted / jnp.sum(shifted, axis=1, keepdims=True)
        out_ref[at, :] = low_bits(dot(low_bits(soft), turned_ref[:, 2 * HEAD_DIM :]))


def attend(rows, weight, tables):
    count, width = rows.shape
    span = weight.shape[2]
    return kernel_call(
        attend_kernel,
        (2,),
        [
            whole(rows.shape),
            pl.BlockSpec((1, width, span), lambda h: (h, 0, 0)),
            *[whole(table.shape) for table in tables],
        ],
        (
            pl.BlockSpec((count, span), lambda h: (0, h)),
            pl.BlockSpec((count, HEAD_DIM), lambda h: (0, h)),
        ),
        (
            jax.ShapeDtypeStruct((count, 2 * span), jnp.bfloat16),
            jax.ShapeDtypeStruct((count, 2 * HEAD_DIM), jnp.bfloat16),
        ),
        2 * count * width * 2 * span + 8 * count * count * HEAD_DIM * 3,
        count * width * 2 + weight.size * 2,
    )(rows, weight, *tables)


def attend_back_kernel(
    grad_ref, weight_ref, turned_ref, cos_ref, sin_ref, pos_col_ref, pos_row_ref, out_ref, key_acc, value_acc
):
    key_pos = pos_col_ref[...]
    rows, width = grad_ref.shape
    scale = HEAD_DIM ** (-0.5)
    keys = turned_ref[:, HEAD_DIM : 2 * HEAD_DIM]
    values = turned_ref[:, 2 * HEAD_DIM :]
    key_acc[...] = jnp.zeros_like(key_acc)
    value_acc[...] = jnp.zeros_like(value_acc)
    for start in range(0, rows, CHUNK):
        at = slice(start, start + CHUNK)
        queries = turned_ref[at, :HEAD_DIM]
        grads = low_bits(
            dot(grad_ref[at, : width // 2], weight_ref[0], ACROSS)
            + dot(grad_ref[at, width // 2 :], weight_ref[1], ACROSS)
        )
        scores = dot(keys, queries, ACROSS) * scale
        scores = jnp.where(pos_row_ref[:, at] >= key_pos, scores, -1e30)
        shifted = jnp.exp(scores - jnp.max(scores, axis=0, keepdims=True))
        soft = shifted / jnp.sum(shifted, axis=0, keepdims=True)
        grad_soft = dot(values, grads, ACROSS)
        centre = jnp.sum(soft * grad_soft, axis=0, keepdims=True)
        grad_scores = low_bits(soft * (grad_soft - centre) * scale)
        value_acc[...] += dot(low_bits(soft), grads)
        key_acc[...] += dot(grad_scores, queries)
        query_grad = dot(grad_scores, keys, DOWN)
        out_ref[at, :HEAD_DIM] = low_bits(turn(query_grad, cos_ref[at, :], -sin_ref[at, :]))
    out_ref[:, HEAD_DIM : 2 * HEAD_DIM] = low_bits(turn(key_acc[...], cos_ref[...], -sin_ref[...]))
    out_ref[:, 2 * HEAD_DIM :] = low_bits(value_acc[...])


def attend_back(grads, weight, turned, tables):
    count, width = grads.shape
    span = turned.shape[1] // 2
    return kernel_call(
        attend_back_kernel,
        (2,),
        [
            whole(grads.shape),
            pl.BlockSpec((2, HEAD_DIM, width // 2), lambda h: (0, h, 0)),
            pl.BlockSpec((count, span), lambda h: (0, h)),
            *[whole(table.shape) for table in tables],
        ],
        pl.BlockSpec((count, span), lambda h: (0, h)),
        jax.ShapeDtypeStruct(turned.shape, jnp.bfloat16),
        2 * count * width * 2 * HEAD_DIM + 20 * count * count * HEAD_DIM * 2,
        count * width * 2 + turned.size * 4,
        [pltpu.VMEM((count, HEAD_DIM), jnp.float32)] * 2,
    )(grads, weight, turned, *tables)


def hidden_kernel(rows_ref, grad_ref, wide_ref, down_ref, hidden_ref, out_ref):
    rows, width = rows_ref.shape
    span = hidden_ref.shape[1]

    @pl.loop(0, rows // CHUNK)
    def _(i):
        at = pl.ds(pl.multiple_of(i * CHUNK, CHUNK), CHUNK)
        both = dot(rows_ref[at, :], wide_ref[0])
        gate, up = both[:, :span], both[:, span:]
        grad_hidden = dot(grad_ref[at, : width // 2], down_ref[0], ACROSS) + dot(
            grad_ref[at, width // 2 :], down_ref[1], ACROSS
        )
        sigma = jax.nn.sigmoid(gate)
        silu = gate * sigma
        hidden_ref[at, :] = low_bits(silu * up)
        out_ref[at, :span] = low_bits(grad_hidden * up * (sigma * (1.0 + gate * (1.0 - sigma))))
        out_ref[at, span:] = low_bits(grad_hidden * silu)


def hidden_pass(rows, grads, wide, down, tile):
    count, width = rows.shape
    span = wide.shape[2] // 2
    tiles = span // tile
    return kernel_call(
        hidden_kernel,
        (2, tiles),
        [
            whole(rows.shape),
            whole(grads.shape),
            pl.BlockSpec((1, width, 2 * tile), lambda w, t: (w, 0, t)),
            pl.BlockSpec((2, tile, width // 2), lambda w, t: (0, tiles * w + t, 0)),
        ],
        (
            pl.BlockSpec((count, tile), lambda w, t: (0, tiles * w + t)),
            pl.BlockSpec((count, 2 * tile), lambda w, t: (0, tiles * w + t)),
        ),
        (
            jax.ShapeDtypeStruct((count, 2 * span), jnp.bfloat16),
            jax.ShapeDtypeStruct((count, 4 * span), jnp.bfloat16),
        ),
        2 * count * width * 6 * span,
        count * width * 8 + wide.size * 3,
    )(rows, grads, wide, down)


def back_kernel(added, left_ref, weight_ref, *refs):
    out_ref = refs[-1]
    rows, depth = left_ref.shape

    @pl.loop(0, rows // CHUNK)
    def _(i):
        at = pl.ds(pl.multiple_of(i * CHUNK, CHUNK), CHUNK)
        total = dot(left_ref[at, : depth // 2], weight_ref[0], ACROSS) + dot(
            left_ref[at, depth // 2 :], weight_ref[1], ACROSS
        )
        if added:
            total += wide_bits(refs[0][at, :])
        out_ref[at, :] = low_bits(total)


def back_rows(left, weight, added=None):
    count, depth = left.shape
    width = weight.shape[1]
    tile = 256
    more = [] if added is None else [added]
    return kernel_call(
        functools.partial(back_kernel, len(more)),
        (width // tile,),
        [
            whole(left.shape),
            pl.BlockSpec((2, tile, depth // 2), lambda i: (0, i, 0)),
            *[pl.BlockSpec((count, tile), lambda i: (0, i)) for _ in more],
        ],
        pl.BlockSpec((count, tile), lambda i: (0, i)),
        jax.ShapeDtypeStruct((count, width), jnp.bfloat16),
        2 * count * width * depth,
        count * (width + depth) * 2 + weight.size * 2,
    )(left, weight, *more)


def ahead_kernel(added, left_ref, weight_ref, *refs):
    out_ref = refs[-1]
    rows = left_ref.shape[0]

    @pl.loop(0, rows // CHUNK)
    def _(i):
        at = pl.ds(pl.multiple_of(i * CHUNK, CHUNK), CHUNK)
        total = dot(left_ref[at, :], weight_ref[0])
        if added:
            total += wide_bits(refs[0][at, :])
        out_ref[at, :] = low_bits(total)


def ahead_rows(left, weight, added=None):
    count, depth = left.shape
    span = weight.shape[2]
    tile = 512
    tiles = span // tile
    more = [] if added is None else [added]
    return kernel_call(
        functools.partial(ahead_kernel, len(more)),
        (2, tiles),
        [
            whole(left.shape),
            pl.BlockSpec((1, depth, tile), lambda w, t: (w, 0, t)),
            *[pl.BlockSpec((count, tile), lambda w, t: (0, w * tiles + t)) for _ in more],
        ],
        pl.BlockSpec((count, tile), lambda w, t: (0, w * tiles + t)),
        jax.ShapeDtypeStruct((count, 2 * span), jnp.bfloat16),
        2 * count * depth * 2 * span,
        count * (2 * span + depth) * 2 + weight.size * 2,
    )(left, weight, *more)


def outer_kernel(left_ref, left_other_ref, right_ref, right_other_ref, out_ref):
    out_ref[0] = low_bits(
        dot(left_ref[...], right_ref[...], DOWN) + dot(left_other_ref[...], right_other_ref[...], DOWN)
    )


def outer_rows(lefts, rights):
    count, depth = lefts[0].shape
    span = rights[0].shape[1] // 2
    tile = 256
    left_spec = pl.BlockSpec((count, tile), lambda w, i: (0, i))
    right_spec = pl.BlockSpec((count, span), lambda w, i: (0, w))
    return kernel_call(
        outer_kernel,
        (2, depth // tile),
        [left_spec, left_spec, right_spec, right_spec],
        pl.BlockSpec((1, tile, span), lambda w, i: (w, i, 0)),
        jax.ShapeDtypeStruct((2, depth, span), jnp.bfloat16),
        2 * 2 * count * depth * 2 * span,
        4 * count * (depth + 2 * span) + depth * span * 4,
    )(*lefts, *rights)


def row_tables(half_block, blocks, spots):
    block_at = jnp.arange(2 * half_block, dtype=jnp.int32)
    pieces = []
    for side, order in (("own", ((0, 0), (1, 0), (0, 1), (1, 1))), ("other", ((0, 0), (0, 1), (1, 0), (1, 1)))):
        far = spots["w"] if side == "own" else 1 - spots["w"]
        for flip_u, flip_v in order:
            block = far * 4 + (spots["u"] ^ flip_u) * 2 + (spots["v"] ^ flip_v)
            pieces.append(paired_positions(block * 2 * half_block + block_at, 2 * half_block, blocks))
    positions = jnp.concatenate(pieces)
    cosine, sine = rope_tables(positions)
    cosine, sine = cosine[:, 0], sine[:, 0]
    return (
        jnp.concatenate([cosine, cosine], axis=1),
        jnp.concatenate([-sine, sine], axis=1),
        positions[:, None],
        positions[None, :],
    )


def paired_body(
    tokens,
    cotangent,
    counts,
    query_weight,
    key_weight,
    value_weight,
    output_weight,
    gate_weight,
    up_weight,
    down_weight,
):
    tok_rows = tokens.shape[1]
    spots = {name: lax.axis_index(name) for name in PAIRS}
    tables = row_tables(tok_rows // 2, 8, spots)

    def own_sequence(stored):
        other = swap(half(stored, 1 - spots["w"], 0), "w")
        return jnp.concatenate([half(stored, spots["w"], 0)[0], other[0]], axis=0)

    def stored_slots(rows):
        other = swap(low_bits(rows[tok_rows:]), "w").astype(rows.dtype)
        return join(rows[None, :tok_rows], other[None], spots["w"], 0)

    live = (spots["w"] < counts[0]).astype(jnp.float32)
    token_rows = own_sequence(tokens)
    grad_rows = own_sequence(cotangent)

    columns = split_column_weights(
        [query_weight, key_weight, value_weight, gate_weight, up_weight], spots["c"]
    )
    tile = 256
    head_columns = 3 * HEAD_DIM
    full_qkv = spread_by_pairs(columns[:, :head_columns], spots)
    gate_at, up_at = head_columns, head_columns + gate_weight.shape[1] // 2
    wide = jnp.concatenate(
        [
            columns[:, at + start : at + start + tile]
            for start in range(0, up_at - gate_at, tile)
            for at in (gate_at, up_at)
        ],
        axis=1,
    )
    full_wide = spread(wide)
    output_span, down_span = output_weight.shape[0] // 4, down_weight.shape[0] // 4
    rows = split_row_weights(
        jnp.concatenate(
            [
                output_weight.reshape(2, 2, output_span, -1),
                down_weight.reshape(2, 2, down_span, -1),
            ],
            axis=2,
        ),
        spots,
    )
    full_output = spread_by_pairs(rows[:output_span], spots)
    full_down = spread_by_pairs(rows[output_span:], spots)

    inputs = token_rows.astype(jnp.float32)
    normed_in, norm_in_back = jax.vjp(layer_norm, inputs)
    norm_in = gather_rows(low_bits(normed_in))
    turned, attended = zip(*[attend(part, full_qkv, tables) for part in norm_in])
    other = swap(ahead_rows(attended[1], full_output), "c")
    after_attn = inputs + scatter_rows(ahead_rows(attended[0], full_output, other))
    normed_mid, norm_mid_back = jax.vjp(layer_norm, after_attn)

    norm_mid = gather_rows(low_bits(normed_mid))
    grad_out = grad_rows.astype(jnp.float32) * live
    grad_all = gather_rows(low_bits(grad_out))
    hidden, grad_wide = zip(
        *[hidden_pass(part, grads, full_wide, full_down, tile) for part, grads in zip(norm_mid, grad_all)]
    )
    other = swap(back_rows(grad_wide[1], full_wide), "c")
    down_total = collect(outer_rows(hidden, grad_all))
    grad_norm_mid = scatter_rows(back_rows(grad_wide[0], full_wide, other))
    wide_total = collect(outer_rows(norm_mid, grad_wide))
    other = swap(ahead_rows(hidden[1], full_down), "c")
    layer_out = after_attn + scatter_rows(ahead_rows(hidden[0], full_down, other))
    mixed = low_bits(layer_out * live)
    grad_after = grad_out + norm_mid_back(grad_norm_mid)[0]

    after_all = gather_rows(low_bits(grad_after))
    grad_qkv = [
        attend_back(part, full_output, kept, tables) for kept, part in zip(turned, after_all)
    ]
    other = swap(back_rows(grad_qkv[1], full_qkv), "c")
    grad_norm_in = scatter_rows(back_rows(grad_qkv[0], full_qkv, other))
    token_grad = grad_after + norm_in_back(grad_norm_in)[0]
    output_total = collect_by_pairs(outer_rows(attended, after_all), spots)
    qkv_total = collect_by_pairs(outer_rows(norm_in, grad_qkv), spots)

    wide_parts = [wide_total[:, at : at + tile] for at in range(0, wide_total.shape[1], tile)]
    wide_total = jnp.concatenate(wide_parts[0::2] + wide_parts[1::2], axis=1)
    span = wide_total.shape[1] // 2
    gate_grad, up_grad = join_column_grads(wide_total, spots["c"], (span, span))
    query_grad, key_grad, value_grad = join_column_grads(qkv_total, spots["c"], (HEAD_DIM,) * 3)
    output_grad = join_row_grads(output_total, spots)
    down_grad = join_row_grads(down_total, spots)
    return (
        stored_slots(mixed),
        stored_slots(token_grad),
        query_grad,
        key_grad,
        value_grad,
        wide_bits(output_grad.reshape(output_weight.shape)),
        gate_grad,
        up_grad,
        wide_bits(down_grad.reshape(down_weight.shape)),
    )


def paired_solution(mesh):
    pairs = Mesh(mesh.devices.reshape((2,) * 5), PAIRS)
    rows, columns = ("x", "c"), ("w", "u", "v")
    slots = P(rows, columns, None)
    weight = P(rows, columns)
    return jax.shard_map(
        paired_body,
        mesh=pairs,
        in_specs=(slots, slots, P(rows)) + (weight,) * 7,
        out_specs=(slots, slots) + (weight,) * 7,
        check_vma=False,
    )


def solution(mesh):
    if mesh.shape["ctx"] == 8 and mesh.shape["dp"] == 4:
        return paired_solution(mesh)
    in_specs = (
        P("dp", "ctx", None),
        P("dp", "ctx", None),
        P("dp"),
        P("dp", "ctx"),
        P("dp", "ctx"),
        P("dp", "ctx"),
        P("dp", "ctx"),
        P("dp", "ctx"),
        P("dp", "ctx"),
        P("dp", "ctx"),
    )
    out_specs = (
        P("dp", "ctx", None),
        P("dp", "ctx", None),
        P("dp", "ctx"),
        P("dp", "ctx"),
        P("dp", "ctx"),
        P("dp", "ctx"),
        P("dp", "ctx"),
        P("dp", "ctx"),
        P("dp", "ctx"),
    )
    return jax.shard_map(body, mesh=mesh, in_specs=in_specs, out_specs=out_specs, check_vma=False)
```

```python
import functools

import jax
import jax.numpy as jnp
from jax import lax
from jax.experimental import pallas as pl
from jax.experimental.pallas import tpu as pltpu
from jax.sharding import Mesh
from jax.sharding import PartitionSpec as P

HEADS = 16
HEAD_DIM = 128
FF = 8192


epsilon = 1e-05
rope_base = 10000.0


def layer_norm(values):
    centred = values - jnp.mean(values, axis=-1, keepdims=True)
    variance = jnp.mean(centred * centred, axis=-1, keepdims=True)
    return centred * lax.rsqrt(variance + epsilon)


def paired_positions(row_index, tok_rows, blocks):
    half_block = tok_rows // 2
    device = row_index // tok_rows
    offset = row_index % tok_rows
    return jnp.where(
        offset < half_block,
        device * half_block + offset,
        (2 * blocks - 1 - device) * half_block + offset - half_block,
    )


def rope_tables(positions):
    half_dim = HEAD_DIM // 2
    frequency = rope_base ** (-jnp.arange(half_dim, dtype=jnp.float32) / half_dim)
    angles = positions.astype(jnp.float32)[:, None] * frequency[None, :]
    return (jnp.cos(angles)[:, None, :], jnp.sin(angles)[:, None, :])


def rotate(values, cosine_table, sine_table):
    half_dim = values.shape[-1] // 2
    first_half = values[..., :half_dim]
    second_half = values[..., half_dim:]
    return jnp.concatenate(
        [
            first_half * cosine_table - second_half * sine_table,
            second_half * cosine_table + first_half * sine_table,
        ],
        axis=-1,
    )


def outer_sum(left, right):
    return lax.dot_general(
        left, right, (((0,), (0,)), ((), ())), preferred_element_type=jnp.float32
    )


def back_product(grad_rows, weight):
    return lax.dot_general(
        grad_rows, weight, (((1,), (1,)), ((), ())), preferred_element_type=jnp.float32
    )


def block_start(block, tile_span, blocks):
    upper_side = (block >= blocks // tile_span).astype(jnp.int32)
    lead_tile = jnp.where(
        upper_side == 0, block * tile_span, 2 * blocks - (block + 1) * tile_span
    ).astype(jnp.int32)
    return (lead_tile, upper_side)


def tile_starts(tiles, lead_tile, upper_side):
    zero_index = jnp.zeros((), jnp.int32)
    return (lead_tile, upper_side) + (zero_index,) * (tiles.ndim - 2)


def take_block(tiles, lead_tile, upper_side, tile_span):
    piece = lax.dynamic_slice(
        tiles, tile_starts(tiles, lead_tile, upper_side), (tile_span, 1) + tiles.shape[2:]
    )
    return piece.reshape((tile_span * tiles.shape[2],) + tiles.shape[3:])


def add_block(tiles, part, lead_tile, upper_side, tile_span):
    starts = tile_starts(tiles, lead_tile, upper_side)
    piece_shape = (tile_span, 1) + tiles.shape[2:]
    before = lax.dynamic_slice(tiles, starts, piece_shape)
    return lax.dynamic_update_slice(tiles, before + part.reshape(piece_shape), starts)


def block_scores(query_half, query_pos, key_block, key_pos):
    scores = jnp.einsum(
        "qhd,khd->hqk", query_half, key_block, preferred_element_type=jnp.float32
    ) * HEAD_DIM ** (-0.5)
    allowed = query_pos[:, None] >= key_pos[None, :]
    return jnp.where(allowed[None, :, :], scores, -1e30)


def attend_half(query_half, query_pos, tables, needed, tile_span, blocks):
    key_tiles, value_tiles, pos_tiles = tables
    row_count = query_half.shape[0]

    def scores_at(block):
        lead_tile, upper_side = block_start(block, tile_span, blocks)
        key_block = take_block(key_tiles, lead_tile, upper_side, tile_span)
        key_pos = take_block(pos_tiles, lead_tile, upper_side, tile_span)
        return (block_scores(query_half, query_pos, key_block, key_pos), lead_tile, upper_side)

    def total_step(block, carried):
        highest, total_mass = carried
        scores = scores_at(block)[0]
        new_highest = jnp.maximum(highest, jnp.max(scores, axis=-1))
        total_mass = total_mass * jnp.exp(highest - new_highest) + jnp.sum(
            jnp.exp(scores - new_highest[..., None]), axis=-1
        )
        return (new_highest, total_mass)

    start_high = jnp.full((HEADS, row_count), -1e30, jnp.float32)
    highest, total_mass = lax.fori_loop(
        0, needed, total_step, (start_high, jnp.zeros((HEADS, row_count), jnp.float32))
    )
    log_total = highest + jnp.log(total_mass)

    def value_step(block, output_rows):
        scores, lead_tile, upper_side = scores_at(block)
        soft_low = jnp.exp(scores - log_total[..., None]).astype(jnp.bfloat16)
        value_block = take_block(value_tiles, lead_tile, upper_side, tile_span)
        return output_rows + jnp.einsum(
            "hqk,khd->qhd", soft_low, value_block, preferred_element_type=jnp.float32
        )

    output_rows = lax.fori_loop(
        0, needed, value_step, jnp.zeros((row_count, HEADS, HEAD_DIM), jnp.float32)
    )
    return (output_rows, log_total)


def attend_half_back(
    query_half,
    query_pos,
    grad_half,
    log_total,
    centre,
    tables,
    needed,
    tile_span,
    blocks,
    key_grad,
    value_grad,
):
    key_tiles, value_tiles, pos_tiles = tables
    score_scale = HEAD_DIM ** (-0.5)

    def back_step(block, state):
        query_grad, key_acc, value_acc = state
        lead_tile, upper_side = block_start(block, tile_span, blocks)
        key_block = take_block(key_tiles, lead_tile, upper_side, tile_span)
        value_block = take_block(value_tiles, lead_tile, upper_side, tile_span)
        key_pos = take_block(pos_tiles, lead_tile, upper_side, tile_span)
        soft = jnp.exp(
            block_scores(query_half, query_pos, key_block, key_pos) - log_total[..., None]
        )
        value_part = jnp.einsum(
            "hqk,qhd->khd", soft.astype(jnp.bfloat16), grad_half, preferred_element_type=jnp.float32
        )
        grad_soft = jnp.einsum(
            "qhd,khd->hqk", grad_half, value_block, preferred_element_type=jnp.float32
        )
        grad_scores = (soft * (grad_soft - centre[..., None]) * score_scale).astype(jnp.bfloat16)
        query_grad = query_grad + jnp.einsum(
            "hqk,khd->qhd", grad_scores, key_block, preferred_element_type=jnp.float32
        )
        key_part = jnp.einsum(
            "hqk,qhd->khd", grad_scores, query_half, preferred_element_type=jnp.float32
        )
        key_acc = add_block(key_acc, key_part, lead_tile, upper_side, tile_span)
        value_acc = add_block(value_acc, value_part, lead_tile, upper_side, tile_span)
        return (query_grad, key_acc, value_acc)

    initial = (jnp.zeros(query_half.shape, jnp.float32), key_grad, value_grad)
    return lax.fori_loop(0, needed, back_step, initial)


def gather_weights(
    query_weight, key_weight, value_weight, output_weight, gate_weight, up_weight, down_weight
):
    row_parts = (
        lax.all_gather(query_weight, "dp", axis=0, tiled=True),
        lax.all_gather(key_weight, "dp", axis=0, tiled=True),
        lax.all_gather(value_weight, "dp", axis=0, tiled=True),
        lax.all_gather(output_weight, "dp", axis=0, tiled=True),
        lax.all_gather(gate_weight, "dp", axis=0, tiled=True),
        lax.all_gather(up_weight, "dp", axis=0, tiled=True),
        lax.all_gather(down_weight, "dp", axis=0, tiled=True),
    )
    return (
        lax.all_gather(row_parts[0], "ctx", axis=1, tiled=True),
        lax.all_gather(row_parts[1], "ctx", axis=1, tiled=True),
        lax.all_gather(row_parts[2], "ctx", axis=1, tiled=True),
        lax.all_gather(row_parts[3], "ctx", axis=1, tiled=True),
        lax.all_gather(row_parts[4], "ctx", axis=1, tiled=True),
        lax.all_gather(row_parts[5], "ctx", axis=1, tiled=True),
        lax.all_gather(row_parts[6], "ctx", axis=1, tiled=True),
    )


def fold_columns(running, operands, grads):
    norm_in_low, attended_low, norm_mid_low, hidden_low = operands
    columns = (
        lax.all_to_all(grads[0], "ctx", split_axis=1, concat_axis=0, tiled=True),
        lax.all_to_all(grads[1], "ctx", split_axis=1, concat_axis=0, tiled=True),
        lax.all_to_all(grads[2], "ctx", split_axis=1, concat_axis=0, tiled=True),
        lax.all_to_all(grads[3], "ctx", split_axis=1, concat_axis=0, tiled=True),
        lax.all_to_all(grads[4], "ctx", split_axis=1, concat_axis=0, tiled=True),
        lax.all_to_all(grads[5], "ctx", split_axis=1, concat_axis=0, tiled=True),
        lax.all_to_all(grads[6], "ctx", split_axis=1, concat_axis=0, tiled=True),
    )
    totals = tuple(running)
    norm_in_piece = lax.all_gather(norm_in_low, "ctx", axis=0, tiled=True)
    attended_piece = lax.all_gather(attended_low, "ctx", axis=0, tiled=True)
    norm_mid_piece = lax.all_gather(norm_mid_low, "ctx", axis=0, tiled=True)
    hidden_piece = lax.all_gather(hidden_low, "ctx", axis=0, tiled=True)
    lefts = (
        norm_in_piece,
        norm_in_piece,
        norm_in_piece,
        attended_piece,
        norm_mid_piece,
        norm_mid_piece,
        hidden_piece,
    )
    return list(
        tuple(
            (total + outer_sum(left, column) for total, left, column in zip(totals, lefts, columns))
        )
    )


def body(
    tokens,
    cotangent,
    counts,
    query_weight,
    key_weight,
    value_weight,
    output_weight,
    gate_weight,
    up_weight,
    down_weight,
):
    slot_count, tok_rows, model_width = tokens.shape
    blocks = lax.axis_size("ctx")
    ctx_index = lax.axis_index("ctx")
    seq_rows = tok_rows * blocks
    half_rows = tok_rows // 2
    proj_width = HEADS * HEAD_DIM
    tile_span = min(512, seq_rows // 2) // half_rows
    first_needed = ctx_index // tile_span + 1
    second_needed = (2 * blocks - 1 - ctx_index) // tile_span + 1
    own_positions = paired_positions(
        ctx_index * tok_rows + jnp.arange(tok_rows, dtype=jnp.int32), tok_rows, blocks
    )
    pos_tiles = paired_positions(jnp.arange(seq_rows, dtype=jnp.int32), tok_rows, blocks).reshape(
        blocks, 2, half_rows
    )
    cosine_table, sine_table = rope_tables(own_positions)

    def rotate_heads(projected):
        return rotate(
            projected.reshape(tok_rows, HEADS, HEAD_DIM), cosine_table, sine_table
        ).reshape(tok_rows, proj_width)

    running = [
        jnp.zeros((model_width, proj_width // blocks), jnp.float32),
        jnp.zeros((model_width, proj_width // blocks), jnp.float32),
        jnp.zeros((model_width, proj_width // blocks), jnp.float32),
        jnp.zeros((proj_width, model_width // blocks), jnp.float32),
        jnp.zeros((model_width, FF // blocks), jnp.float32),
        jnp.zeros((model_width, FF // blocks), jnp.float32),
        jnp.zeros((FF, model_width // blocks), jnp.float32),
    ]
    outputs = []
    token_grads = []
    for slot_index in range(slot_count):
        gathered = gather_weights(
            query_weight,
            key_weight,
            value_weight,
            output_weight,
            gate_weight,
            up_weight,
            down_weight,
        )
        full_query, full_key, full_value, full_output, full_gate, full_up, full_down = gathered
        live_mask = (slot_index < counts[0]).astype(jnp.float32)
        inputs = tokens[slot_index].astype(jnp.float32)
        normed_in, norm_in_back = jax.vjp(layer_norm, inputs)
        norm_in_low = normed_in.astype(jnp.bfloat16)
        query_proj = jnp.dot(norm_in_low, full_query, preferred_element_type=jnp.float32)
        key_proj = jnp.dot(norm_in_low, full_key, preferred_element_type=jnp.float32)
        value_proj = jnp.dot(norm_in_low, full_value, preferred_element_type=jnp.float32)
        query_rot, query_turn_back = jax.vjp(rotate_heads, query_proj)
        key_rot, key_turn_back = jax.vjp(rotate_heads, key_proj)
        query_heads = query_rot.astype(jnp.bfloat16).reshape(tok_rows, HEADS, HEAD_DIM)
        key_rows, value_rows = (
            lax.all_gather(key_rot.astype(jnp.bfloat16), "ctx", axis=0, tiled=True),
            lax.all_gather(value_proj.astype(jnp.bfloat16), "ctx", axis=0, tiled=True),
        )
        tables = (
            key_rows.reshape(blocks, 2, half_rows, HEADS, HEAD_DIM),
            value_rows.reshape(blocks, 2, half_rows, HEADS, HEAD_DIM),
            pos_tiles,
        )
        first_out, first_total = attend_half(
            query_heads[:half_rows],
            own_positions[:half_rows],
            tables,
            first_needed,
            tile_span,
            blocks,
        )
        second_out, second_total = attend_half(
            query_heads[half_rows:],
            own_positions[half_rows:],
            tables,
            second_needed,
            tile_span,
            blocks,
        )
        attended_wide = jnp.concatenate([first_out, second_out], axis=0)
        attended_low = attended_wide.reshape(tok_rows, proj_width).astype(jnp.bfloat16)
        after_attn = inputs + jnp.dot(attended_low, full_output, preferred_element_type=jnp.float32)
        normed_mid, norm_mid_back = jax.vjp(layer_norm, after_attn)
        norm_mid_low = normed_mid.astype(jnp.bfloat16)
        gate_proj = jnp.dot(norm_mid_low, full_gate, preferred_element_type=jnp.float32)
        up_proj = jnp.dot(norm_mid_low, full_up, preferred_element_type=jnp.float32)
        hidden, hidden_back = jax.vjp(
            lambda gate_in, up_in: jax.nn.silu(gate_in) * up_in, gate_proj, up_proj
        )
        hidden_low = hidden.astype(jnp.bfloat16)
        layer_out = after_attn + jnp.dot(hidden_low, full_down, preferred_element_type=jnp.float32)
        outputs.append((layer_out * live_mask).astype(jnp.bfloat16))
        grad_out = cotangent[slot_index].astype(jnp.float32) * live_mask
        grad_out_low = grad_out.astype(jnp.bfloat16)
        grad_gate_in, grad_up_in = hidden_back(back_product(grad_out_low, full_down))
        grad_gate_low = grad_gate_in.astype(jnp.bfloat16)
        grad_up_low = grad_up_in.astype(jnp.bfloat16)
        grad_norm_mid = back_product(grad_gate_low, full_gate) + back_product(grad_up_low, full_up)
        grad_after = grad_out + norm_mid_back(grad_norm_mid)[0]
        grad_after_low = grad_after.astype(jnp.bfloat16)
        grad_attended_low = back_product(grad_after_low, full_output).astype(jnp.bfloat16)
        grad_heads = grad_attended_low.reshape(tok_rows, HEADS, HEAD_DIM)
        centre = jnp.einsum("qhd,qhd->hq", grad_heads.astype(jnp.float32), attended_wide)
        empty_tiles = jnp.zeros((blocks, 2, half_rows, HEADS, HEAD_DIM), jnp.float32)
        first_query, key_acc, value_acc = attend_half_back(
            query_heads[:half_rows],
            own_positions[:half_rows],
            grad_heads[:half_rows],
            first_total,
            centre[:, :half_rows],
            tables,
            first_needed,
            tile_span,
            blocks,
            empty_tiles,
            empty_tiles,
        )
        second_query, key_acc, value_acc = attend_half_back(
            query_heads[half_rows:],
            own_positions[half_rows:],
            grad_heads[half_rows:],
            second_total,
            centre[:, half_rows:],
            tables,
            second_needed,
            tile_span,
            blocks,
            key_acc,
            value_acc,
        )
        grad_query_rot = jnp.concatenate([first_query, second_query], axis=0).reshape(
            tok_rows, proj_width
        )
        key_share, value_share = (
            lax.psum_scatter(
                key_acc.reshape(seq_rows, proj_width).astype(jnp.bfloat16),
                "ctx",
                scatter_dimension=0,
                tiled=True,
            ).astype(jnp.float32),
            lax.psum_scatter(
                value_acc.reshape(seq_rows, proj_width).astype(jnp.bfloat16),
                "ctx",
                scatter_dimension=0,
                tiled=True,
            ).astype(jnp.float32),
        )
        grad_query_low = query_turn_back(grad_query_rot)[0].astype(jnp.bfloat16)
        grad_key_low = key_turn_back(key_share)[0].astype(jnp.bfloat16)
        grad_value_low = value_share.astype(jnp.bfloat16)
        grad_norm_in = (
            back_product(grad_query_low, full_query)
            + back_product(grad_key_low, full_key)
            + back_product(grad_value_low, full_value)
        )
        token_grads.append(grad_after + norm_in_back(grad_norm_in)[0])
        grads = (
            grad_query_low,
            grad_key_low,
            grad_value_low,
            grad_after_low,
            grad_gate_low,
            grad_up_low,
            grad_out_low,
        )
        running = fold_columns(
            running, (norm_in_low, attended_low, norm_mid_low, hidden_low), grads
        )
    row_sums = (
        lax.psum_scatter(
            running[0].astype(jnp.bfloat16), "dp", scatter_dimension=0, tiled=True
        ).astype(jnp.float32),
        lax.psum_scatter(
            running[1].astype(jnp.bfloat16), "dp", scatter_dimension=0, tiled=True
        ).astype(jnp.float32),
        lax.psum_scatter(
            running[2].astype(jnp.bfloat16), "dp", scatter_dimension=0, tiled=True
        ).astype(jnp.float32),
        lax.psum_scatter(
            running[3].astype(jnp.bfloat16), "dp", scatter_dimension=0, tiled=True
        ).astype(jnp.float32),
        lax.psum_scatter(
            running[4].astype(jnp.bfloat16), "dp", scatter_dimension=0, tiled=True
        ).astype(jnp.float32),
        lax.psum_scatter(
            running[5].astype(jnp.bfloat16), "dp", scatter_dimension=0, tiled=True
        ).astype(jnp.float32),
        lax.psum_scatter(
            running[6].astype(jnp.bfloat16), "dp", scatter_dimension=0, tiled=True
        ).astype(jnp.float32),
    )
    return (
        jnp.stack(outputs),
        jnp.stack(token_grads),
        row_sums[0],
        row_sums[1],
        row_sums[2],
        row_sums[3],
        row_sums[4],
        row_sums[5],
        row_sums[6],
    )


PAIRS = ("x", "c", "w", "u", "v")
SWAP = ((0, 1), (1, 0))


def swap(value, axis):
    return lax.ppermute(value, axis, SWAP)


def join(own, other, bit, axis):
    low = jnp.where(bit == 0, own, other)
    high = jnp.where(bit == 0, other, own)
    return jnp.concatenate([low, high], axis=axis)


def low_bits(value):
    return value.astype(jnp.bfloat16)


def wide_bits(value):
    return value.astype(jnp.float32)


def half(value, bit, axis):
    size = value.shape[axis] // 2
    return lax.dynamic_slice_in_dim(value, bit * size, size, axis)


def stage(sends, waits=()):
    values, _ = lax.optimization_barrier((tuple(value for value, _ in sends), tuple(waits)))
    return [swap(value, axis) for value, (_, axis) in zip(values, sends)]


def both_halves(value, bit, axis):
    return half(value, bit, axis), half(value, 1 - bit, axis)


def column_halves(weights, c):
    return tuple(
        jnp.concatenate([half(weight, bit, 1) for weight in weights], axis=1) for bit in (c, 1 - c)
    )


def join_columns(kept, other, c, counts):
    grads, at = [], 0
    for count in counts:
        grads.append(join(wide_bits(kept[:, at : at + count]), wide_bits(other[:, at : at + count]), c, 1))
        at += count
    return grads


def square(own, beside, across, both, spots):
    first = join(own, across, spots["x"], 0)
    second = join(beside, both, spots["x"], 0)
    return join(first[None], second[None], spots["w"], 0)


def spread(piece):
    rows, columns = piece.shape
    return lax.all_gather(piece, ("w", "x"), axis=0, tiled=True).reshape(2, 2 * rows, columns)


def collect(grad):
    _, rows, columns = grad.shape
    return lax.psum_scatter(
        grad.reshape(2 * rows, columns), ("w", "x"), scatter_dimension=0, tiled=True
    )


def weave(own, from_u, from_v, first_uv, second_uv):
    size = own.shape[0] // 2
    return jnp.concatenate(
        [
            own[:size],
            from_u[:size],
            from_v[:size],
            first_uv,
            own[size:],
            from_v[size:],
            from_u[size:],
            second_uv,
        ],
        axis=0,
    )


def corners(from_u, from_v):
    size = from_u.shape[0] // 2
    return [(from_u[:size], "v"), (from_v[size:], "u")]


def fold_sends(total):
    size = total.shape[0] // 8
    return [(total[2 * size : 4 * size], "v"), (total[6 * size :], "u")]


def fold(total, from_v, from_u):
    size = total.shape[0] // 8
    first = wide_bits(total[: 2 * size]) + wide_bits(from_v)
    second = wide_bits(total[4 * size : 6 * size]) + wide_bits(from_u)
    kept = jnp.concatenate([first[:size], second[:size]], axis=0)
    return kept, [(low_bits(first[size:]), "u"), (low_bits(second[size:]), "v")]


def fold_end(kept, from_u, from_v):
    return kept + jnp.concatenate([wide_bits(from_u), wide_bits(from_v)], axis=0)


ACROSS = (((1,), (1,)), ((), ()))
DOWN = (((0,), (0,)), ((), ()))
CHUNK = 256
TALL = 1024


def dot(left, right, dims=(((1,), (0,)), ((), ()))):
    return lax.dot_general(left, right, dims, preferred_element_type=jnp.float32)


def whole(shape):
    return pl.BlockSpec(shape, lambda *_: (0,) * len(shape))


def tie_kernel(value_ref, *refs):
    refs[-1][...] = value_ref[...]


def tie(value, *held):
    return pl.pallas_call(
        tie_kernel,
        in_specs=[whole(value.shape), *[pl.BlockSpec(memory_space=pl.ANY) for _ in held]],
        out_specs=whole(value.shape),
        out_shape=jax.ShapeDtypeStruct(value.shape, value.dtype),
        compiler_params=pltpu.CompilerParams(vmem_limit_bytes=48 * 2**20),
    )(value, *held)


def kernel_call(kernel, grid, in_specs, out_specs, out_shape, flops, size, scratch=()):
    return pl.pallas_call(
        kernel,
        grid=grid,
        in_specs=in_specs,
        out_specs=out_specs,
        out_shape=out_shape,
        scratch_shapes=scratch,
        compiler_params=pltpu.CompilerParams(vmem_limit_bytes=48 * 2**20),
        cost_estimate=pl.CostEstimate(flops=flops, bytes_accessed=size, transcendentals=0),
    )


def turn(values, cosine, sine):
    return values * cosine + pltpu.roll(values, HEAD_DIM // 2, 1) * sine


def attend_kernel(rows_ref, weight_ref, cos_ref, sin_ref, pos_col_ref, pos_row_ref, *refs):
    turned_ref, out_ref = refs[-2:]
    key_pos = pos_row_ref[...]
    rows = rows_ref.shape[0]

    @pl.loop(0, rows // CHUNK)
    def _(i):
        at = pl.ds(pl.multiple_of(i * CHUNK, CHUNK), CHUNK)
        proj = dot(rows_ref[at, :], weight_ref[0])
        cosine, sine = cos_ref[at, :], sin_ref[at, :]
        turned_ref[at, :HEAD_DIM] = low_bits(turn(proj[:, :HEAD_DIM], cosine, sine))
        turned_ref[at, HEAD_DIM : 2 * HEAD_DIM] = low_bits(
            turn(proj[:, HEAD_DIM : 2 * HEAD_DIM], cosine, sine)
        )
        turned_ref[at, 2 * HEAD_DIM :] = low_bits(proj[:, 2 * HEAD_DIM :])

    @pl.loop(0, rows // CHUNK)
    def _(i):
        at = pl.ds(pl.multiple_of(i * CHUNK, CHUNK), CHUNK)
        scores = dot(turned_ref[at, :HEAD_DIM], turned_ref[:, HEAD_DIM : 2 * HEAD_DIM], ACROSS)
        scores = scores * HEAD_DIM ** (-0.5)
        scores = jnp.where(pos_col_ref[at, :] >= key_pos, scores, -1e30)
        shifted = jnp.exp(scores - jnp.max(scores, axis=1, keepdims=True))
        soft = shifted / jnp.sum(shifted, axis=1, keepdims=True)
        out_ref[at, :] = low_bits(dot(low_bits(soft), turned_ref[:, 2 * HEAD_DIM :]))


def attend(rows, weight, tables, *held):
    count, width = rows.shape
    span = weight.shape[2]
    return kernel_call(
        attend_kernel,
        (2,),
        [
            whole(rows.shape),
            pl.BlockSpec((1, width, span), lambda h: (h, 0, 0)),
            *[whole(table.shape) for table in tables],
            *[pl.BlockSpec(memory_space=pl.ANY) for _ in held],
        ],
        (
            pl.BlockSpec((count, span), lambda h: (0, h)),
            pl.BlockSpec((count, HEAD_DIM), lambda h: (0, h)),
        ),
        (
            jax.ShapeDtypeStruct((count, 2 * span), jnp.bfloat16),
            jax.ShapeDtypeStruct((count, 2 * HEAD_DIM), jnp.bfloat16),
        ),
        2 * count * width * 2 * span + 8 * count * count * HEAD_DIM * 3,
        count * width * 2 + weight.size * 2,
    )(rows, weight, *tables, *held)


def attend_back_kernel(
    grad_ref, weight_ref, turned_ref, cos_ref, sin_ref, pos_col_ref, pos_row_ref, *refs
):
    out_ref, key_acc, value_acc = refs[-3:]
    key_pos = pos_col_ref[...]
    rows, width = grad_ref.shape
    scale = HEAD_DIM ** (-0.5)
    keys = turned_ref[:, HEAD_DIM : 2 * HEAD_DIM]
    values = turned_ref[:, 2 * HEAD_DIM :]
    key_acc[...] = jnp.zeros_like(key_acc)
    value_acc[...] = jnp.zeros_like(value_acc)
    for start in range(0, rows, CHUNK):
        at = slice(start, start + CHUNK)
        queries = turned_ref[at, :HEAD_DIM]
        grads = low_bits(
            dot(grad_ref[at, : width // 2], weight_ref[0], ACROSS)
            + dot(grad_ref[at, width // 2 :], weight_ref[1], ACROSS)
        )
        scores = dot(keys, queries, ACROSS) * scale
        scores = jnp.where(pos_row_ref[:, at] >= key_pos, scores, -1e30)
        shifted = jnp.exp(scores - jnp.max(scores, axis=0, keepdims=True))
        soft = shifted / jnp.sum(shifted, axis=0, keepdims=True)
        grad_soft = dot(values, grads, ACROSS)
        centre = jnp.sum(soft * grad_soft, axis=0, keepdims=True)
        grad_scores = low_bits(soft * (grad_soft - centre) * scale)
        value_acc[...] += dot(low_bits(soft), grads)
        key_acc[...] += dot(grad_scores, queries)
        query_grad = dot(grad_scores, keys, DOWN)
        out_ref[at, :HEAD_DIM] = low_bits(turn(query_grad, cos_ref[at, :], -sin_ref[at, :]))
    out_ref[:, HEAD_DIM : 2 * HEAD_DIM] = low_bits(turn(key_acc[...], cos_ref[...], -sin_ref[...]))
    out_ref[:, 2 * HEAD_DIM :] = low_bits(value_acc[...])


def attend_back(grads, weight, turned, tables, *held):
    count, width = grads.shape
    span = turned.shape[1] // 2
    return kernel_call(
        attend_back_kernel,
        (2,),
        [
            whole(grads.shape),
            pl.BlockSpec((2, HEAD_DIM, width // 2), lambda h: (0, h, 0)),
            pl.BlockSpec((count, span), lambda h: (0, h)),
            *[whole(table.shape) for table in tables],
            *[pl.BlockSpec(memory_space=pl.ANY) for _ in held],
        ],
        pl.BlockSpec((count, span), lambda h: (0, h)),
        jax.ShapeDtypeStruct(turned.shape, jnp.bfloat16),
        2 * count * width * 2 * HEAD_DIM + 20 * count * count * HEAD_DIM * 2,
        count * width * 2 + turned.size * 4,
        [pltpu.VMEM((count, HEAD_DIM), jnp.float32)] * 2,
    )(grads, weight, turned, *tables, *held)


def hidden_kernel(rows_ref, grad_ref, wide_ref, down_ref, hidden_ref, out_ref):
    rows, width = rows_ref.shape
    span = hidden_ref.shape[1]

    @pl.loop(0, rows // CHUNK)
    def _(i):
        at = pl.ds(pl.multiple_of(i * CHUNK, CHUNK), CHUNK)
        both = dot(rows_ref[at, :], wide_ref[0])
        gate, up = both[:, :span], both[:, span:]
        grad_hidden = dot(grad_ref[at, : width // 2], down_ref[0], ACROSS) + dot(
            grad_ref[at, width // 2 :], down_ref[1], ACROSS
        )
        sigma = jax.nn.sigmoid(gate)
        silu = gate * sigma
        hidden_ref[at, :] = low_bits(silu * up)
        out_ref[at, :span] = low_bits(grad_hidden * up * (sigma * (1.0 + gate * (1.0 - sigma))))
        out_ref[at, span:] = low_bits(grad_hidden * silu)


def hidden_pass(rows, grads, wide, down, tile):
    count, width = rows.shape
    span = wide.shape[2] // 2
    tiles = span // tile
    return kernel_call(
        hidden_kernel,
        (2, tiles),
        [
            whole(rows.shape),
            whole(grads.shape),
            pl.BlockSpec((1, width, 2 * tile), lambda w, t: (w, 0, t)),
            pl.BlockSpec((2, tile, width // 2), lambda w, t: (0, tiles * w + t, 0)),
        ],
        (
            pl.BlockSpec((count, tile), lambda w, t: (0, tiles * w + t)),
            pl.BlockSpec((count, 2 * tile), lambda w, t: (0, tiles * w + t)),
        ),
        (
            jax.ShapeDtypeStruct((count, 2 * span), jnp.bfloat16),
            jax.ShapeDtypeStruct((count, 4 * span), jnp.bfloat16),
        ),
        2 * count * width * 6 * span,
        count * width * 8 + wide.size * 3,
    )(rows, grads, wide, down)


def back_kernel(counts, *refs):
    out_ref = refs[-1]
    pairs, more = counts
    lefts, weights = refs[:pairs], refs[pairs : 2 * pairs]
    added = refs[2 * pairs : 2 * pairs + more]
    rows, depth = lefts[0].shape

    @pl.loop(0, rows // TALL)
    def _(i):
        at = pl.ds(pl.multiple_of(i * TALL, TALL), TALL)
        total = sum(
            dot(left_ref[at, : depth // 2], weight_ref[0], ACROSS)
            + dot(left_ref[at, depth // 2 :], weight_ref[1], ACROSS)
            for left_ref, weight_ref in zip(lefts, weights)
        )
        for added_ref in added:
            total += wide_bits(added_ref[at, :])
        out_ref[at, :] = low_bits(total)


def back_rows(lefts, weights, added=(), held=()):
    count, depth = lefts[0].shape
    width = weights[0].shape[1]
    tile = 256
    return kernel_call(
        functools.partial(back_kernel, (len(lefts), len(added))),
        (width // tile,),
        [
            *[whole(left.shape) for left in lefts],
            *[pl.BlockSpec((2, tile, depth // 2), lambda i: (0, i, 0)) for _ in weights],
            *[pl.BlockSpec((count, tile), lambda i: (0, i)) for _ in added],
            *[pl.BlockSpec(memory_space=pl.ANY) for _ in held],
        ],
        pl.BlockSpec((count, tile), lambda i: (0, i)),
        jax.ShapeDtypeStruct((count, width), jnp.bfloat16),
        2 * count * width * depth * len(lefts),
        len(lefts) * (count * (width + depth) * 2 + weights[0].size * 2),
    )(*lefts, *weights, *added, *held)


def ahead_kernel(added, left_ref, weight_ref, *refs):
    out_ref = refs[-1]
    rows = left_ref.shape[0]

    @pl.loop(0, rows // TALL)
    def _(i):
        at = pl.ds(pl.multiple_of(i * TALL, TALL), TALL)
        total = dot(left_ref[at, :], weight_ref[0])
        if added:
            total += wide_bits(refs[0][at, :])
        out_ref[at, :] = low_bits(total)


def ahead_rows(left, weight, added=None):
    count, depth = left.shape
    span = weight.shape[2]
    tile = 512
    tiles = span // tile
    more = [] if added is None else [added]
    return kernel_call(
        functools.partial(ahead_kernel, len(more)),
        (2, tiles),
        [
            whole(left.shape),
            pl.BlockSpec((1, depth, tile), lambda w, t: (w, 0, t)),
            *[pl.BlockSpec((count, tile), lambda w, t: (0, w * tiles + t)) for _ in more],
        ],
        pl.BlockSpec((count, tile), lambda w, t: (0, w * tiles + t)),
        jax.ShapeDtypeStruct((count, 2 * span), jnp.bfloat16),
        2 * count * depth * 2 * span,
        count * (2 * span + depth) * 2 + weight.size * 2,
    )(left, weight, *more)


def outer_kernel(left_ref, left_other_ref, right_ref, right_other_ref, out_ref):
    out_ref[0] = low_bits(
        dot(left_ref[...], right_ref[...], DOWN) + dot(left_other_ref[...], right_other_ref[...], DOWN)
    )


def outer_rows(lefts, rights):
    count, depth = lefts[0].shape
    span = rights[0].shape[1] // 2
    tile = 256
    left_spec = pl.BlockSpec((count, tile), lambda w, i: (0, i))
    right_spec = pl.BlockSpec((count, span), lambda w, i: (0, w))
    return kernel_call(
        outer_kernel,
        (2, depth // tile),
        [left_spec, left_spec, right_spec, right_spec],
        pl.BlockSpec((1, tile, span), lambda w, i: (w, i, 0)),
        jax.ShapeDtypeStruct((2, depth, span), jnp.bfloat16),
        2 * 2 * count * depth * 2 * span,
        4 * count * (depth + 2 * span) + depth * span * 4,
    )(*lefts, *rights)


def row_tables(half_block, blocks, spots):
    block_at = jnp.arange(2 * half_block, dtype=jnp.int32)
    pieces = []
    for side, order in (("own", ((0, 0), (1, 0), (0, 1), (1, 1))), ("other", ((0, 0), (0, 1), (1, 0), (1, 1)))):
        far = spots["w"] if side == "own" else 1 - spots["w"]
        for flip_u, flip_v in order:
            block = far * 4 + (spots["u"] ^ flip_u) * 2 + (spots["v"] ^ flip_v)
            pieces.append(paired_positions(block * 2 * half_block + block_at, 2 * half_block, blocks))
    positions = jnp.concatenate(pieces)
    cosine, sine = rope_tables(positions)
    cosine, sine = cosine[:, 0], sine[:, 0]
    return (
        jnp.concatenate([cosine, cosine], axis=1),
        jnp.concatenate([-sine, sine], axis=1),
        positions[:, None],
        positions[None, :],
    )


def paired_body(
    tokens,
    cotangent,
    counts,
    query_weight,
    key_weight,
    value_weight,
    output_weight,
    gate_weight,
    up_weight,
    down_weight,
):
    tok_rows = tokens.shape[1]
    spots = {name: lax.axis_index(name) for name in PAIRS}
    c, w, x, u, v = (spots[name] for name in ("c", "w", "x", "u", "v"))
    tables = row_tables(tok_rows // 2, 8, spots)
    live = (w < counts[0]).astype(jnp.float32)
    tile = 256
    head_columns = 3 * HEAD_DIM
    wide_columns = gate_weight.shape[1] // 2
    output_span, down_span = output_weight.shape[0] // 4, down_weight.shape[0] // 4

    token_kept, token_sent = both_halves(tokens, w, 0)
    cotangent_kept, cotangent_sent = both_halves(cotangent, w, 0)
    columns_kept, columns_sent = column_halves(
        [query_weight, key_weight, value_weight, gate_weight, up_weight], c
    )
    parts = jnp.concatenate(
        [output_weight.reshape(2, 2, output_span, -1), down_weight.reshape(2, 2, down_span, -1)],
        axis=2,
    )
    parts_kept, parts_sent = both_halves(parts, v, 0)
    token_got, columns_got, parts_got = (
        swap(token_sent[0], "w"),
        swap(columns_sent, "c"),
        swap(parts_sent[0], "v"),
    )
    inputs = wide_bits(jnp.concatenate([token_kept[0], token_got], axis=0))
    normed_in, norm_in_back = jax.vjp(layer_norm, inputs)
    norm_own = low_bits(normed_in)
    columns = join(columns_kept, columns_got, c, 0)
    qkv_piece = columns[:, :head_columns]
    wide_piece = jnp.concatenate(
        [
            columns[:, at + start : at + start + tile]
            for start in range(0, wide_columns, tile)
            for at in (head_columns, head_columns + wide_columns)
        ],
        axis=1,
    )
    full_wide = spread(wide_piece)
    parts = join(parts_kept[0], parts_got, v, 2)
    parts_kept, parts_sent = both_halves(parts, c, 0)
    norm_u, norm_v, qkv_w, qkv_x, parts_got = stage(
        [(norm_own, "u"), (norm_own, "v"), (qkv_piece, "w"), (qkv_piece, "x"), (parts_sent[0], "c")]
    )
    parts = join(parts_kept, parts_got[None], c, 0)
    parts_kept, parts_sent = both_halves(parts, u, 0)
    norm_uv, qkv_wx, parts_got, cotangent_got = stage(
        [(norm_u, "v"), (qkv_w, "x"), (parts_sent[0], "u"), (cotangent_sent[0], "w")], [norm_v, qkv_x]
    )
    norm_in = weave(norm_own, norm_u, norm_v, norm_uv[:tok_rows], norm_uv[tok_rows:])
    full_qkv = square(qkv_piece, qkv_w, qkv_x, qkv_wx, spots)
    parts = join(parts_kept[0], parts_got, u, 1)
    output_piece, down_piece = parts[:output_span], parts[output_span:]
    grad_out = wide_bits(jnp.concatenate([cotangent_kept[0], cotangent_got], axis=0)) * live
    grad_own = low_bits(grad_out)

    norm_other, output_w, output_x = stage(
        [(norm_in, "c"), (output_piece, "w"), (output_piece, "x")], [qkv_wx, cotangent_got]
    )
    grad_u, grad_v = stage([(grad_own, "u"), (grad_own, "v")], [qkv_wx])
    first = attend(norm_in, full_qkv, tables)
    second = attend(norm_other, full_qkv, tables)
    output_wx, grad_uv, down_x, down_w = stage(
        [(output_w, "x"), (grad_u, "v"), (down_piece, "x"), (down_piece, "w")],
        [output_x, grad_v, first[0], second[0]],
    )
    norm_in = (norm_in, norm_other)
    turned, attended = zip(first, second)
    full_output = square(output_piece, output_w, output_x, output_wx, spots)
    grad_all = weave(grad_own, grad_u, grad_v, grad_uv[:tok_rows], grad_uv[tok_rows:])
    (other,) = stage([(ahead_rows(attended[1], full_output), "c")])
    total = ahead_rows(attended[0], full_output, other)
    from_v, from_u = stage(fold_sends(total))
    (grad_other,) = stage([(grad_all, "c")], [other])
    grad_all = (grad_all, grad_other)
    kept, sends = fold(total, from_v, from_u)
    from_u, from_v = stage(sends, [down_x])
    (down_wx,) = stage([(down_w, "x")], [from_u])
    full_down = square(down_piece, down_w, down_x, down_wx, spots)
    after_attn = inputs + fold_end(kept, from_u, from_v)
    normed_mid, norm_mid_back = jax.vjp(layer_norm, after_attn)
    mid_own = low_bits(normed_mid)
    mid_u, mid_v = stage([(mid_own, "u"), (mid_own, "v")])
    mid_uv, mid_vu = stage(corners(mid_u, mid_v), [grad_other, down_wx])
    mid_uv = tie(mid_uv, full_wide)
    norm_mid = weave(mid_own, mid_u, mid_v, mid_uv, mid_vu)
    norm_mid = (norm_mid, swap(norm_mid, "c"))

    hidden, grad_wide = zip(
        *[hidden_pass(rows, grads, full_wide, full_down, tile) for rows, grads in zip(norm_mid, grad_all)]
    )
    (other,) = stage([(back_rows([grad_wide[1]], [full_wide]), "c")], [grad_wide[0]])
    wide_outer = outer_rows(norm_mid, grad_wide)
    wide_total = collect(wide_outer)
    other, _ = lax.optimization_barrier((other, wide_outer))
    total = back_rows([grad_wide[0]], [full_wide], [other])
    from_v, from_u = stage(fold_sends(total))
    down_outer = outer_rows(hidden, grad_all)
    down_kept, down_sent = both_halves(down_outer, x, 1)
    kept, sends = fold(total, from_v, from_u)
    from_u, from_v = stage(sends, [down_outer])
    (down_got,) = stage([(down_sent, "x")], [from_u])
    ahead = ahead_rows(hidden[1], full_down)
    grad_norm_mid = fold_end(kept, from_u, from_v)
    grad_after = grad_out + norm_mid_back(grad_norm_mid)[0]
    after_own = low_bits(grad_after)
    after_u, after_v, other = stage([(after_own, "u"), (after_own, "v"), (ahead, "c")])
    after_uv, after_vu = stage(corners(after_u, after_v), [other])
    total = ahead_rows(hidden[0], full_down, other)
    after_uv, after_vu, total = lax.optimization_barrier((after_uv, after_vu, total))
    after_all = weave(after_own, after_u, after_v, after_uv, after_vu)

    down_sum = wide_bits(down_kept) + wide_bits(down_got)
    down_kept, down_sent = both_halves(down_sum, w, 0)
    (after_other,) = stage([(after_all, "c")])
    from_v, from_u = stage(fold_sends(total), [after_uv])
    (down_got,) = stage([(low_bits(down_sent[0]), "w")], [after_other])
    after_all = (after_all, after_other)
    first = attend_back(after_all[0], full_output, turned[0], tables)
    kept, sends = fold(total, from_v, from_u)
    from_u, from_v = stage(sends, [first, after_other])
    second = attend_back(after_other, full_output, turned[1], tables, wide_total)
    grad_qkv = (first, second)
    ahead = back_rows([second], [full_qkv])
    qkv_outer = outer_rows(norm_in, grad_qkv)
    mixed = low_bits((after_attn + fold_end(kept, from_u, from_v)) * live)
    (other,) = stage([(ahead, "c")])
    other, qkv_outer = lax.optimization_barrier((other, qkv_outer))
    (mixed_got,) = stage([(mixed[tok_rows:], "w")], [other, down_got])
    output_outer = outer_rows(attended, after_all)
    total = back_rows([first], [full_qkv], [other])
    qkv_kept, qkv_sent = both_halves(qkv_outer, x, 1)
    output_kept, output_sent = both_halves(output_outer, x, 1)
    from_v, from_u, qkv_got = stage(fold_sends(total) + [(qkv_sent, "x")], [mixed])
    qkv_sum = wide_bits(qkv_kept) + wide_bits(qkv_got)
    qkv_kept, qkv_sent = both_halves(qkv_sum, w, 0)
    kept, sends = fold(total, from_v, from_u)
    from_u, from_v, qkv_got, output_got = stage(
        sends + [(low_bits(qkv_sent[0]), "w"), (output_sent, "x")], [mixed_got]
    )
    grad_norm_in = fold_end(kept, from_u, from_v)
    token_grad = grad_after + norm_in_back(grad_norm_in)[0]
    output_sum = wide_bits(output_kept) + wide_bits(output_got)
    output_kept, output_sent = both_halves(output_sum, w, 0)
    token_got, output_got = stage(
        [(low_bits(token_grad[tok_rows:]), "w"), (low_bits(output_sent[0]), "w")]
    )
    down_kept, down_got, wide_total, _ = lax.optimization_barrier(
        (down_kept, down_got, wide_total, from_u)
    )
    down_total = low_bits(down_kept[0] + wide_bits(down_got))
    qkv_total = qkv_kept[0] + wide_bits(qkv_got)
    output_total = low_bits(output_kept[0] + wide_bits(output_got))

    wide_parts = [wide_total[:, at : at + tile] for at in range(0, 2 * wide_columns, tile)]
    wide_total = jnp.concatenate(wide_parts[0::2] + wide_parts[1::2], axis=1)

    def columns_home(total, sizes):
        kept, sent = both_halves(total, c, 0)
        return join_columns(kept, swap(low_bits(sent), "c"), c, sizes)

    def rows_home(total):
        kept, sent = both_halves(total, u, 1)
        parts = join(kept[None], swap(sent, "u")[None], u, 0)
        kept, sent = both_halves(parts, c, 0)
        parts = join(kept, swap(sent, "c"), c, 0)
        kept, sent = both_halves(parts, v, 2)
        return wide_bits(join(kept[None], swap(sent, "v")[None], v, 0))

    gate_grad, up_grad = columns_home(wide_total, (wide_columns,) * 2)
    query_grad, key_grad, value_grad = columns_home(qkv_total, (HEAD_DIM,) * 3)
    return (
        join(mixed[None, :tok_rows], mixed_got[None], w, 0),
        join(token_grad[None, :tok_rows], wide_bits(token_got)[None], w, 0),
        query_grad,
        key_grad,
        value_grad,
        rows_home(output_total).reshape(output_weight.shape),
        gate_grad,
        up_grad,
        rows_home(down_total).reshape(down_weight.shape),
    )


def paired_solution(mesh):
    pairs = Mesh(mesh.devices.reshape((2,) * 5), PAIRS)
    rows, columns = ("x", "c"), ("w", "u", "v")
    slots = P(rows, columns, None)
    weight = P(rows, columns)
    return jax.shard_map(
        paired_body,
        mesh=pairs,
        in_specs=(slots, slots, P(rows)) + (weight,) * 7,
        out_specs=(slots, slots) + (weight,) * 7,
        check_vma=False,
    )


def solution(mesh):
    if mesh.shape["ctx"] == 8 and mesh.shape["dp"] == 4:
        return paired_solution(mesh)
    in_specs = (
        P("dp", "ctx", None),
        P("dp", "ctx", None),
        P("dp"),
        P("dp", "ctx"),
        P("dp", "ctx"),
        P("dp", "ctx"),
        P("dp", "ctx"),
        P("dp", "ctx"),
        P("dp", "ctx"),
        P("dp", "ctx"),
    )
    out_specs = (
        P("dp", "ctx", None),
        P("dp", "ctx", None),
        P("dp", "ctx"),
        P("dp", "ctx"),
        P("dp", "ctx"),
        P("dp", "ctx"),
        P("dp", "ctx"),
        P("dp", "ctx"),
        P("dp", "ctx"),
    )
    return jax.shard_map(body, mesh=mesh, in_specs=in_specs, out_specs=out_specs, check_vma=False)
```

```python
import functools

import jax
import jax.numpy as jnp
from jax import lax
from jax.experimental import pallas as pl
from jax.experimental.pallas import tpu as pltpu
from jax.sharding import Mesh
from jax.sharding import PartitionSpec as P

HEADS = 16
HEAD_DIM = 128
FF = 8192


epsilon = 1e-05
rope_base = 10000.0


def layer_norm(values):
    centred = values - jnp.mean(values, axis=-1, keepdims=True)
    variance = jnp.mean(centred * centred, axis=-1, keepdims=True)
    return centred * lax.rsqrt(variance + epsilon)


def paired_positions(row_index, tok_rows, blocks):
    half_block = tok_rows // 2
    device = row_index // tok_rows
    offset = row_index % tok_rows
    return jnp.where(
        offset < half_block,
        device * half_block + offset,
        (2 * blocks - 1 - device) * half_block + offset - half_block,
    )


def rope_tables(positions):
    half_dim = HEAD_DIM // 2
    frequency = rope_base ** (-jnp.arange(half_dim, dtype=jnp.float32) / half_dim)
    angles = positions.astype(jnp.float32)[:, None] * frequency[None, :]
    return (jnp.cos(angles)[:, None, :], jnp.sin(angles)[:, None, :])


def rotate(values, cosine_table, sine_table):
    half_dim = values.shape[-1] // 2
    first_half = values[..., :half_dim]
    second_half = values[..., half_dim:]
    return jnp.concatenate(
        [
            first_half * cosine_table - second_half * sine_table,
            second_half * cosine_table + first_half * sine_table,
        ],
        axis=-1,
    )


def outer_sum(left, right):
    return lax.dot_general(
        left, right, (((0,), (0,)), ((), ())), preferred_element_type=jnp.float32
    )


def back_product(grad_rows, weight):
    return lax.dot_general(
        grad_rows, weight, (((1,), (1,)), ((), ())), preferred_element_type=jnp.float32
    )


def block_start(block, tile_span, blocks):
    upper_side = (block >= blocks // tile_span).astype(jnp.int32)
    lead_tile = jnp.where(
        upper_side == 0, block * tile_span, 2 * blocks - (block + 1) * tile_span
    ).astype(jnp.int32)
    return (lead_tile, upper_side)


def tile_starts(tiles, lead_tile, upper_side):
    zero_index = jnp.zeros((), jnp.int32)
    return (lead_tile, upper_side) + (zero_index,) * (tiles.ndim - 2)


def take_block(tiles, lead_tile, upper_side, tile_span):
    piece = lax.dynamic_slice(
        tiles, tile_starts(tiles, lead_tile, upper_side), (tile_span, 1) + tiles.shape[2:]
    )
    return piece.reshape((tile_span * tiles.shape[2],) + tiles.shape[3:])


def add_block(tiles, part, lead_tile, upper_side, tile_span):
    starts = tile_starts(tiles, lead_tile, upper_side)
    piece_shape = (tile_span, 1) + tiles.shape[2:]
    before = lax.dynamic_slice(tiles, starts, piece_shape)
    return lax.dynamic_update_slice(tiles, before + part.reshape(piece_shape), starts)


def block_scores(query_half, query_pos, key_block, key_pos):
    scores = jnp.einsum(
        "qhd,khd->hqk", query_half, key_block, preferred_element_type=jnp.float32
    ) * HEAD_DIM ** (-0.5)
    allowed = query_pos[:, None] >= key_pos[None, :]
    return jnp.where(allowed[None, :, :], scores, -1e30)


def attend_half(query_half, query_pos, tables, needed, tile_span, blocks):
    key_tiles, value_tiles, pos_tiles = tables
    row_count = query_half.shape[0]

    def scores_at(block):
        lead_tile, upper_side = block_start(block, tile_span, blocks)
        key_block = take_block(key_tiles, lead_tile, upper_side, tile_span)
        key_pos = take_block(pos_tiles, lead_tile, upper_side, tile_span)
        return (block_scores(query_half, query_pos, key_block, key_pos), lead_tile, upper_side)

    def total_step(block, carried):
        highest, total_mass = carried
        scores = scores_at(block)[0]
        new_highest = jnp.maximum(highest, jnp.max(scores, axis=-1))
        total_mass = total_mass * jnp.exp(highest - new_highest) + jnp.sum(
            jnp.exp(scores - new_highest[..., None]), axis=-1
        )
        return (new_highest, total_mass)

    start_high = jnp.full((HEADS, row_count), -1e30, jnp.float32)
    highest, total_mass = lax.fori_loop(
        0, needed, total_step, (start_high, jnp.zeros((HEADS, row_count), jnp.float32))
    )
    log_total = highest + jnp.log(total_mass)

    def value_step(block, output_rows):
        scores, lead_tile, upper_side = scores_at(block)
        soft_low = jnp.exp(scores - log_total[..., None]).astype(jnp.bfloat16)
        value_block = take_block(value_tiles, lead_tile, upper_side, tile_span)
        return output_rows + jnp.einsum(
            "hqk,khd->qhd", soft_low, value_block, preferred_element_type=jnp.float32
        )

    output_rows = lax.fori_loop(
        0, needed, value_step, jnp.zeros((row_count, HEADS, HEAD_DIM), jnp.float32)
    )
    return (output_rows, log_total)


def attend_half_back(
    query_half,
    query_pos,
    grad_half,
    log_total,
    centre,
    tables,
    needed,
    tile_span,
    blocks,
    key_grad,
    value_grad,
):
    key_tiles, value_tiles, pos_tiles = tables
    score_scale = HEAD_DIM ** (-0.5)

    def back_step(block, state):
        query_grad, key_acc, value_acc = state
        lead_tile, upper_side = block_start(block, tile_span, blocks)
        key_block = take_block(key_tiles, lead_tile, upper_side, tile_span)
        value_block = take_block(value_tiles, lead_tile, upper_side, tile_span)
        key_pos = take_block(pos_tiles, lead_tile, upper_side, tile_span)
        soft = jnp.exp(
            block_scores(query_half, query_pos, key_block, key_pos) - log_total[..., None]
        )
        value_part = jnp.einsum(
            "hqk,qhd->khd", soft.astype(jnp.bfloat16), grad_half, preferred_element_type=jnp.float32
        )
        grad_soft = jnp.einsum(
            "qhd,khd->hqk", grad_half, value_block, preferred_element_type=jnp.float32
        )
        grad_scores = (soft * (grad_soft - centre[..., None]) * score_scale).astype(jnp.bfloat16)
        query_grad = query_grad + jnp.einsum(
            "hqk,khd->qhd", grad_scores, key_block, preferred_element_type=jnp.float32
        )
        key_part = jnp.einsum(
            "hqk,qhd->khd", grad_scores, query_half, preferred_element_type=jnp.float32
        )
        key_acc = add_block(key_acc, key_part, lead_tile, upper_side, tile_span)
        value_acc = add_block(value_acc, value_part, lead_tile, upper_side, tile_span)
        return (query_grad, key_acc, value_acc)

    initial = (jnp.zeros(query_half.shape, jnp.float32), key_grad, value_grad)
    return lax.fori_loop(0, needed, back_step, initial)


def gather_weights(
    query_weight, key_weight, value_weight, output_weight, gate_weight, up_weight, down_weight
):
    row_parts = (
        lax.all_gather(query_weight, "dp", axis=0, tiled=True),
        lax.all_gather(key_weight, "dp", axis=0, tiled=True),
        lax.all_gather(value_weight, "dp", axis=0, tiled=True),
        lax.all_gather(output_weight, "dp", axis=0, tiled=True),
        lax.all_gather(gate_weight, "dp", axis=0, tiled=True),
        lax.all_gather(up_weight, "dp", axis=0, tiled=True),
        lax.all_gather(down_weight, "dp", axis=0, tiled=True),
    )
    return (
        lax.all_gather(row_parts[0], "ctx", axis=1, tiled=True),
        lax.all_gather(row_parts[1], "ctx", axis=1, tiled=True),
        lax.all_gather(row_parts[2], "ctx", axis=1, tiled=True),
        lax.all_gather(row_parts[3], "ctx", axis=1, tiled=True),
        lax.all_gather(row_parts[4], "ctx", axis=1, tiled=True),
        lax.all_gather(row_parts[5], "ctx", axis=1, tiled=True),
        lax.all_gather(row_parts[6], "ctx", axis=1, tiled=True),
    )


def fold_columns(running, operands, grads):
    norm_in_low, attended_low, norm_mid_low, hidden_low = operands
    columns = (
        lax.all_to_all(grads[0], "ctx", split_axis=1, concat_axis=0, tiled=True),
        lax.all_to_all(grads[1], "ctx", split_axis=1, concat_axis=0, tiled=True),
        lax.all_to_all(grads[2], "ctx", split_axis=1, concat_axis=0, tiled=True),
        lax.all_to_all(grads[3], "ctx", split_axis=1, concat_axis=0, tiled=True),
        lax.all_to_all(grads[4], "ctx", split_axis=1, concat_axis=0, tiled=True),
        lax.all_to_all(grads[5], "ctx", split_axis=1, concat_axis=0, tiled=True),
        lax.all_to_all(grads[6], "ctx", split_axis=1, concat_axis=0, tiled=True),
    )
    totals = tuple(running)
    norm_in_piece = lax.all_gather(norm_in_low, "ctx", axis=0, tiled=True)
    attended_piece = lax.all_gather(attended_low, "ctx", axis=0, tiled=True)
    norm_mid_piece = lax.all_gather(norm_mid_low, "ctx", axis=0, tiled=True)
    hidden_piece = lax.all_gather(hidden_low, "ctx", axis=0, tiled=True)
    lefts = (
        norm_in_piece,
        norm_in_piece,
        norm_in_piece,
        attended_piece,
        norm_mid_piece,
        norm_mid_piece,
        hidden_piece,
    )
    return list(
        tuple(
            (total + outer_sum(left, column) for total, left, column in zip(totals, lefts, columns))
        )
    )


def body(
    tokens,
    cotangent,
    counts,
    query_weight,
    key_weight,
    value_weight,
    output_weight,
    gate_weight,
    up_weight,
    down_weight,
):
    slot_count, tok_rows, model_width = tokens.shape
    blocks = lax.axis_size("ctx")
    ctx_index = lax.axis_index("ctx")
    seq_rows = tok_rows * blocks
    half_rows = tok_rows // 2
    proj_width = HEADS * HEAD_DIM
    tile_span = min(512, seq_rows // 2) // half_rows
    first_needed = ctx_index // tile_span + 1
    second_needed = (2 * blocks - 1 - ctx_index) // tile_span + 1
    own_positions = paired_positions(
        ctx_index * tok_rows + jnp.arange(tok_rows, dtype=jnp.int32), tok_rows, blocks
    )
    pos_tiles = paired_positions(jnp.arange(seq_rows, dtype=jnp.int32), tok_rows, blocks).reshape(
        blocks, 2, half_rows
    )
    cosine_table, sine_table = rope_tables(own_positions)

    def rotate_heads(projected):
        return rotate(
            projected.reshape(tok_rows, HEADS, HEAD_DIM), cosine_table, sine_table
        ).reshape(tok_rows, proj_width)

    running = [
        jnp.zeros((model_width, proj_width // blocks), jnp.float32),
        jnp.zeros((model_width, proj_width // blocks), jnp.float32),
        jnp.zeros((model_width, proj_width // blocks), jnp.float32),
        jnp.zeros((proj_width, model_width // blocks), jnp.float32),
        jnp.zeros((model_width, FF // blocks), jnp.float32),
        jnp.zeros((model_width, FF // blocks), jnp.float32),
        jnp.zeros((FF, model_width // blocks), jnp.float32),
    ]
    outputs = []
    token_grads = []
    for slot_index in range(slot_count):
        gathered = gather_weights(
            query_weight,
            key_weight,
            value_weight,
            output_weight,
            gate_weight,
            up_weight,
            down_weight,
        )
        full_query, full_key, full_value, full_output, full_gate, full_up, full_down = gathered
        live_mask = (slot_index < counts[0]).astype(jnp.float32)
        inputs = tokens[slot_index].astype(jnp.float32)
        normed_in, norm_in_back = jax.vjp(layer_norm, inputs)
        norm_in_low = normed_in.astype(jnp.bfloat16)
        query_proj = jnp.dot(norm_in_low, full_query, preferred_element_type=jnp.float32)
        key_proj = jnp.dot(norm_in_low, full_key, preferred_element_type=jnp.float32)
        value_proj = jnp.dot(norm_in_low, full_value, preferred_element_type=jnp.float32)
        query_rot, query_turn_back = jax.vjp(rotate_heads, query_proj)
        key_rot, key_turn_back = jax.vjp(rotate_heads, key_proj)
        query_heads = query_rot.astype(jnp.bfloat16).reshape(tok_rows, HEADS, HEAD_DIM)
        key_rows, value_rows = (
            lax.all_gather(key_rot.astype(jnp.bfloat16), "ctx", axis=0, tiled=True),
            lax.all_gather(value_proj.astype(jnp.bfloat16), "ctx", axis=0, tiled=True),
        )
        tables = (
            key_rows.reshape(blocks, 2, half_rows, HEADS, HEAD_DIM),
            value_rows.reshape(blocks, 2, half_rows, HEADS, HEAD_DIM),
            pos_tiles,
        )
        first_out, first_total = attend_half(
            query_heads[:half_rows],
            own_positions[:half_rows],
            tables,
            first_needed,
            tile_span,
            blocks,
        )
        second_out, second_total = attend_half(
            query_heads[half_rows:],
            own_positions[half_rows:],
            tables,
            second_needed,
            tile_span,
            blocks,
        )
        attended_wide = jnp.concatenate([first_out, second_out], axis=0)
        attended_low = attended_wide.reshape(tok_rows, proj_width).astype(jnp.bfloat16)
        after_attn = inputs + jnp.dot(attended_low, full_output, preferred_element_type=jnp.float32)
        normed_mid, norm_mid_back = jax.vjp(layer_norm, after_attn)
        norm_mid_low = normed_mid.astype(jnp.bfloat16)
        gate_proj = jnp.dot(norm_mid_low, full_gate, preferred_element_type=jnp.float32)
        up_proj = jnp.dot(norm_mid_low, full_up, preferred_element_type=jnp.float32)
        hidden, hidden_back = jax.vjp(
            lambda gate_in, up_in: jax.nn.silu(gate_in) * up_in, gate_proj, up_proj
        )
        hidden_low = hidden.astype(jnp.bfloat16)
        layer_out = after_attn + jnp.dot(hidden_low, full_down, preferred_element_type=jnp.float32)
        outputs.append((layer_out * live_mask).astype(jnp.bfloat16))
        grad_out = cotangent[slot_index].astype(jnp.float32) * live_mask
        grad_out_low = grad_out.astype(jnp.bfloat16)
        grad_gate_in, grad_up_in = hidden_back(back_product(grad_out_low, full_down))
        grad_gate_low = grad_gate_in.astype(jnp.bfloat16)
        grad_up_low = grad_up_in.astype(jnp.bfloat16)
        grad_norm_mid = back_product(grad_gate_low, full_gate) + back_product(grad_up_low, full_up)
        grad_after = grad_out + norm_mid_back(grad_norm_mid)[0]
        grad_after_low = grad_after.astype(jnp.bfloat16)
        grad_attended_low = back_product(grad_after_low, full_output).astype(jnp.bfloat16)
        grad_heads = grad_attended_low.reshape(tok_rows, HEADS, HEAD_DIM)
        centre = jnp.einsum("qhd,qhd->hq", grad_heads.astype(jnp.float32), attended_wide)
        empty_tiles = jnp.zeros((blocks, 2, half_rows, HEADS, HEAD_DIM), jnp.float32)
        first_query, key_acc, value_acc = attend_half_back(
            query_heads[:half_rows],
            own_positions[:half_rows],
            grad_heads[:half_rows],
            first_total,
            centre[:, :half_rows],
            tables,
            first_needed,
            tile_span,
            blocks,
            empty_tiles,
            empty_tiles,
        )
        second_query, key_acc, value_acc = attend_half_back(
            query_heads[half_rows:],
            own_positions[half_rows:],
            grad_heads[half_rows:],
            second_total,
            centre[:, half_rows:],
            tables,
            second_needed,
            tile_span,
            blocks,
            key_acc,
            value_acc,
        )
        grad_query_rot = jnp.concatenate([first_query, second_query], axis=0).reshape(
            tok_rows, proj_width
        )
        key_share, value_share = (
            lax.psum_scatter(
                key_acc.reshape(seq_rows, proj_width).astype(jnp.bfloat16),
                "ctx",
                scatter_dimension=0,
                tiled=True,
            ).astype(jnp.float32),
            lax.psum_scatter(
                value_acc.reshape(seq_rows, proj_width).astype(jnp.bfloat16),
                "ctx",
                scatter_dimension=0,
                tiled=True,
            ).astype(jnp.float32),
        )
        grad_query_low = query_turn_back(grad_query_rot)[0].astype(jnp.bfloat16)
        grad_key_low = key_turn_back(key_share)[0].astype(jnp.bfloat16)
        grad_value_low = value_share.astype(jnp.bfloat16)
        grad_norm_in = (
            back_product(grad_query_low, full_query)
            + back_product(grad_key_low, full_key)
            + back_product(grad_value_low, full_value)
        )
        token_grads.append(grad_after + norm_in_back(grad_norm_in)[0])
        grads = (
            grad_query_low,
            grad_key_low,
            grad_value_low,
            grad_after_low,
            grad_gate_low,
            grad_up_low,
            grad_out_low,
        )
        running = fold_columns(
            running, (norm_in_low, attended_low, norm_mid_low, hidden_low), grads
        )
    row_sums = (
        lax.psum_scatter(
            running[0].astype(jnp.bfloat16), "dp", scatter_dimension=0, tiled=True
        ).astype(jnp.float32),
        lax.psum_scatter(
            running[1].astype(jnp.bfloat16), "dp", scatter_dimension=0, tiled=True
        ).astype(jnp.float32),
        lax.psum_scatter(
            running[2].astype(jnp.bfloat16), "dp", scatter_dimension=0, tiled=True
        ).astype(jnp.float32),
        lax.psum_scatter(
            running[3].astype(jnp.bfloat16), "dp", scatter_dimension=0, tiled=True
        ).astype(jnp.float32),
        lax.psum_scatter(
            running[4].astype(jnp.bfloat16), "dp", scatter_dimension=0, tiled=True
        ).astype(jnp.float32),
        lax.psum_scatter(
            running[5].astype(jnp.bfloat16), "dp", scatter_dimension=0, tiled=True
        ).astype(jnp.float32),
        lax.psum_scatter(
            running[6].astype(jnp.bfloat16), "dp", scatter_dimension=0, tiled=True
        ).astype(jnp.float32),
    )
    return (
        jnp.stack(outputs),
        jnp.stack(token_grads),
        row_sums[0],
        row_sums[1],
        row_sums[2],
        row_sums[3],
        row_sums[4],
        row_sums[5],
        row_sums[6],
    )


PAIRS = ("x", "c", "w", "u", "v")
SWAP = ((0, 1), (1, 0))


def swap(value, axis):
    return lax.ppermute(value, axis, SWAP)


def join(own, other, bit, axis):
    low = jnp.where(bit == 0, own, other)
    high = jnp.where(bit == 0, other, own)
    return jnp.concatenate([low, high], axis=axis)


def low_bits(value):
    return value.astype(jnp.bfloat16)


def wide_bits(value):
    return value.astype(jnp.float32)


def half(value, bit, axis):
    size = value.shape[axis] // 2
    return lax.dynamic_slice_in_dim(value, bit * size, size, axis)


def stage(sends, waits=()):
    values, _ = lax.optimization_barrier((tuple(value for value, _ in sends), tuple(waits)))
    return [swap(value, axis) for value, (_, axis) in zip(values, sends)]


def both_halves(value, bit, axis):
    return half(value, bit, axis), half(value, 1 - bit, axis)


def column_halves(weights, c):
    return tuple(
        jnp.concatenate([half(weight, bit, 1) for weight in weights], axis=1) for bit in (c, 1 - c)
    )


def join_columns(kept, other, c, counts):
    grads, at = [], 0
    for count in counts:
        grads.append(join(wide_bits(kept[:, at : at + count]), wide_bits(other[:, at : at + count]), c, 1))
        at += count
    return grads


def square(own, beside, across, both, spots):
    first = join(own, across, spots["x"], 0)
    second = join(beside, both, spots["x"], 0)
    return join(first[None], second[None], spots["w"], 0)


def corner_blocks(grad, w, x):
    _, rows, columns = grad.shape
    rows //= 2
    parts = grad.reshape(2, 2, rows, columns)
    return [
        lax.dynamic_slice(parts, (at_w, at_x, 0, 0), (1, 1, rows, columns))[0, 0]
        for at_w, at_x in ((1 - w, 1 - x), (1 - w, x), (w, 1 - x), (w, x))
    ]


def plus(left, right):
    return low_bits(wide_bits(left) + wide_bits(right))


def weave(own, from_u, from_v, first_uv, second_uv):
    size = own.shape[0] // 2
    return jnp.concatenate(
        [
            own[:size],
            from_u[:size],
            from_v[:size],
            first_uv,
            own[size:],
            from_v[size:],
            from_u[size:],
            second_uv,
        ],
        axis=0,
    )


def corners(from_u, from_v):
    size = from_u.shape[0] // 2
    return [(from_u[:size], "v"), (from_v[size:], "u")]


def fold_sends(total):
    size = total.shape[0] // 8
    return [(total[2 * size : 4 * size], "v"), (total[6 * size :], "u")]


def fold(total, from_v, from_u):
    size = total.shape[0] // 8
    first = wide_bits(total[: 2 * size]) + wide_bits(from_v)
    second = wide_bits(total[4 * size : 6 * size]) + wide_bits(from_u)
    kept = jnp.concatenate([first[:size], second[:size]], axis=0)
    return kept, [(low_bits(first[size:]), "u"), (low_bits(second[size:]), "v")]


def fold_end(kept, from_u, from_v):
    return kept + jnp.concatenate([wide_bits(from_u), wide_bits(from_v)], axis=0)


ACROSS = (((1,), (1,)), ((), ()))
DOWN = (((0,), (0,)), ((), ()))
CHUNK = 256
TALL = 1024


def dot(left, right, dims=(((1,), (0,)), ((), ()))):
    return lax.dot_general(left, right, dims, preferred_element_type=jnp.float32)


def whole(shape):
    return pl.BlockSpec(shape, lambda *_: (0,) * len(shape))


def kernel_call(kernel, grid, in_specs, out_specs, out_shape, flops, size, scratch=(), weight=1000):
    return pl.pallas_call(
        kernel,
        grid=grid,
        in_specs=in_specs,
        out_specs=out_specs,
        out_shape=out_shape,
        scratch_shapes=scratch,
        compiler_params=pltpu.CompilerParams(vmem_limit_bytes=48 * 2**20),
        cost_estimate=pl.CostEstimate(
            flops=flops // weight, bytes_accessed=size // weight, transcendentals=0
        ),
    )


def turn(values, cosine, sine):
    return values * cosine + pltpu.roll(values, HEAD_DIM // 2, 1) * sine


def attend_kernel(rows_ref, weight_ref, cos_ref, sin_ref, pos_col_ref, pos_row_ref, *refs):
    turned_ref, out_ref = refs[-2:]
    key_pos = pos_row_ref[...]
    rows = rows_ref.shape[0]

    @pl.loop(0, rows // CHUNK)
    def _(i):
        at = pl.ds(pl.multiple_of(i * CHUNK, CHUNK), CHUNK)
        proj = dot(rows_ref[at, :], weight_ref[0])
        cosine, sine = cos_ref[at, :], sin_ref[at, :]
        turned_ref[at, :HEAD_DIM] = low_bits(turn(proj[:, :HEAD_DIM], cosine, sine))
        turned_ref[at, HEAD_DIM : 2 * HEAD_DIM] = low_bits(
            turn(proj[:, HEAD_DIM : 2 * HEAD_DIM], cosine, sine)
        )
        turned_ref[at, 2 * HEAD_DIM :] = low_bits(proj[:, 2 * HEAD_DIM :])

    @pl.loop(0, rows // CHUNK)
    def _(i):
        at = pl.ds(pl.multiple_of(i * CHUNK, CHUNK), CHUNK)
        scores = dot(turned_ref[at, :HEAD_DIM], turned_ref[:, HEAD_DIM : 2 * HEAD_DIM], ACROSS)
        scores = scores * HEAD_DIM ** (-0.5)
        scores = jnp.where(pos_col_ref[at, :] >= key_pos, scores, -1e30)
        shifted = jnp.exp(scores - jnp.max(scores, axis=1, keepdims=True))
        soft = shifted / jnp.sum(shifted, axis=1, keepdims=True)
        out_ref[at, :] = low_bits(dot(low_bits(soft), turned_ref[:, 2 * HEAD_DIM :]))


def attend(rows, weight, tables, *held):
    count, width = rows.shape
    span = weight.shape[2]
    return kernel_call(
        attend_kernel,
        (2,),
        [
            whole(rows.shape),
            pl.BlockSpec((1, width, span), lambda h: (h, 0, 0)),
            *[whole(table.shape) for table in tables],
            *[pl.BlockSpec(memory_space=pl.ANY) for _ in held],
        ],
        (
            pl.BlockSpec((count, span), lambda h: (0, h)),
            pl.BlockSpec((count, HEAD_DIM), lambda h: (0, h)),
        ),
        (
            jax.ShapeDtypeStruct((count, 2 * span), jnp.bfloat16),
            jax.ShapeDtypeStruct((count, 2 * HEAD_DIM), jnp.bfloat16),
        ),
        2 * count * width * 2 * span + 8 * count * count * HEAD_DIM * 3,
        count * width * 2 + weight.size * 2,
        weight=1,
    )(rows, weight, *tables, *held)


def attend_back_kernel(
    grad_ref, weight_ref, turned_ref, cos_ref, sin_ref, pos_col_ref, pos_row_ref, *refs
):
    out_ref, key_acc, value_acc = refs[-3:]
    key_pos = pos_col_ref[...]
    rows, width = grad_ref.shape
    scale = HEAD_DIM ** (-0.5)
    keys = turned_ref[:, HEAD_DIM : 2 * HEAD_DIM]
    values = turned_ref[:, 2 * HEAD_DIM :]
    key_acc[...] = jnp.zeros_like(key_acc)
    value_acc[...] = jnp.zeros_like(value_acc)
    for start in range(0, rows, CHUNK):
        at = slice(start, start + CHUNK)
        queries = turned_ref[at, :HEAD_DIM]
        grads = low_bits(
            dot(grad_ref[at, : width // 2], weight_ref[0], ACROSS)
            + dot(grad_ref[at, width // 2 :], weight_ref[1], ACROSS)
        )
        scores = dot(keys, queries, ACROSS) * scale
        scores = jnp.where(pos_row_ref[:, at] >= key_pos, scores, -1e30)
        shifted = jnp.exp(scores - jnp.max(scores, axis=0, keepdims=True))
        soft = shifted / jnp.sum(shifted, axis=0, keepdims=True)
        grad_soft = dot(values, grads, ACROSS)
        centre = jnp.sum(soft * grad_soft, axis=0, keepdims=True)
        grad_scores = low_bits(soft * (grad_soft - centre) * scale)
        value_acc[...] += dot(low_bits(soft), grads)
        key_acc[...] += dot(grad_scores, queries)
        query_grad = dot(grad_scores, keys, DOWN)
        out_ref[at, :HEAD_DIM] = low_bits(turn(query_grad, cos_ref[at, :], -sin_ref[at, :]))
    out_ref[:, HEAD_DIM : 2 * HEAD_DIM] = low_bits(turn(key_acc[...], cos_ref[...], -sin_ref[...]))
    out_ref[:, 2 * HEAD_DIM :] = low_bits(value_acc[...])


def attend_back(grads, weight, turned, tables, *held):
    count, width = grads.shape
    span = turned.shape[1] // 2
    return kernel_call(
        attend_back_kernel,
        (2,),
        [
            whole(grads.shape),
            pl.BlockSpec((2, HEAD_DIM, width // 2), lambda h: (0, h, 0)),
            pl.BlockSpec((count, span), lambda h: (0, h)),
            *[whole(table.shape) for table in tables],
            *[pl.BlockSpec(memory_space=pl.ANY) for _ in held],
        ],
        pl.BlockSpec((count, span), lambda h: (0, h)),
        jax.ShapeDtypeStruct(turned.shape, jnp.bfloat16),
        2 * count * width * 2 * HEAD_DIM + 20 * count * count * HEAD_DIM * 2,
        count * width * 2 + turned.size * 4,
        [pltpu.VMEM((count, HEAD_DIM), jnp.float32)] * 2,
    )(grads, weight, turned, *tables, *held)


def hidden_kernel(rows_ref, grad_ref, wide_ref, down_ref, hidden_ref, out_ref):
    rows, width = rows_ref.shape
    span = hidden_ref.shape[1]

    @pl.loop(0, rows // CHUNK)
    def _(i):
        at = pl.ds(pl.multiple_of(i * CHUNK, CHUNK), CHUNK)
        both = dot(rows_ref[at, :], wide_ref[0])
        gate, up = both[:, :span], both[:, span:]
        grad_hidden = dot(grad_ref[at, : width // 2], down_ref[0], ACROSS) + dot(
            grad_ref[at, width // 2 :], down_ref[1], ACROSS
        )
        sigma = jax.nn.sigmoid(gate)
        silu = gate * sigma
        hidden_ref[at, :] = low_bits(silu * up)
        out_ref[at, :span] = low_bits(grad_hidden * up * (sigma * (1.0 + gate * (1.0 - sigma))))
        out_ref[at, span:] = low_bits(grad_hidden * silu)


def hidden_pass(rows, grads, wide, down):
    count, width = rows.shape
    tile = wide.shape[2] // 2
    return kernel_call(
        hidden_kernel,
        (2,),
        [
            whole(rows.shape),
            whole(grads.shape),
            pl.BlockSpec((1, width, 2 * tile), lambda w: (w, 0, 0)),
            pl.BlockSpec((2, tile, width // 2), lambda w: (0, w, 0)),
        ],
        (
            pl.BlockSpec((count, tile), lambda w: (0, w)),
            pl.BlockSpec((count, 2 * tile), lambda w: (0, w)),
        ),
        (
            jax.ShapeDtypeStruct((count, 2 * tile), jnp.bfloat16),
            jax.ShapeDtypeStruct((count, 4 * tile), jnp.bfloat16),
        ),
        2 * count * width * 6 * tile,
        count * width * 4 + wide.size * 3,
    )(rows, grads, wide, down)


def back_kernel(counts, *refs):
    out_ref = refs[-1]
    pairs, more = counts
    lefts, weights = refs[:pairs], refs[pairs : 2 * pairs]
    added = refs[2 * pairs : 2 * pairs + more]
    rows, depth = lefts[0].shape

    @pl.loop(0, rows // TALL)
    def _(i):
        at = pl.ds(pl.multiple_of(i * TALL, TALL), TALL)
        total = sum(
            dot(left_ref[at, : depth // 2], weight_ref[0], ACROSS)
            + dot(left_ref[at, depth // 2 :], weight_ref[1], ACROSS)
            for left_ref, weight_ref in zip(lefts, weights)
        )
        for added_ref in added:
            total += wide_bits(added_ref[at, :])
        out_ref[at, :] = low_bits(total)


def back_rows(lefts, weights, added=(), held=()):
    count, depth = lefts[0].shape
    width = weights[0].shape[1]
    tile = 256
    return kernel_call(
        functools.partial(back_kernel, (len(lefts), len(added))),
        (width // tile,),
        [
            *[whole(left.shape) for left in lefts],
            *[pl.BlockSpec((2, tile, depth // 2), lambda i: (0, i, 0)) for _ in weights],
            *[pl.BlockSpec((count, tile), lambda i: (0, i)) for _ in added],
            *[pl.BlockSpec(memory_space=pl.ANY) for _ in held],
        ],
        pl.BlockSpec((count, tile), lambda i: (0, i)),
        jax.ShapeDtypeStruct((count, width), jnp.bfloat16),
        2 * count * width * depth * len(lefts),
        len(lefts) * (count * (width + depth) * 2 + weights[0].size * 2),
    )(*lefts, *weights, *added, *held)


def ahead_kernel(counts, *refs):
    out_ref = refs[-1]
    pairs, more = counts
    lefts, weights = refs[:pairs], refs[pairs : 2 * pairs]
    added = refs[2 * pairs : 2 * pairs + more]
    rows = lefts[0].shape[0]

    @pl.loop(0, rows // TALL)
    def _(i):
        at = pl.ds(pl.multiple_of(i * TALL, TALL), TALL)
        total = sum(dot(left_ref[at, :], weight_ref[0]) for left_ref, weight_ref in zip(lefts, weights))
        for added_ref in added:
            total += wide_bits(added_ref[at, :])
        out_ref[at, :] = low_bits(total)


def ahead_rows(lefts, weights, added=()):
    count, depth = lefts[0].shape
    span = weights[0].shape[2]
    tile = 512
    tiles = span // tile
    return kernel_call(
        functools.partial(ahead_kernel, (len(lefts), len(added))),
        (2, tiles),
        [
            *[whole(left.shape) for left in lefts],
            *[pl.BlockSpec((1, depth, tile), lambda w, t: (w, 0, t)) for _ in weights],
            *[pl.BlockSpec((count, tile), lambda w, t: (0, w * tiles + t)) for _ in added],
        ],
        pl.BlockSpec((count, tile), lambda w, t: (0, w * tiles + t)),
        jax.ShapeDtypeStruct((count, 2 * span), jnp.bfloat16),
        2 * count * depth * 2 * span * len(lefts),
        len(lefts) * (count * (2 * span + depth) * 2 + weights[0].size * 2),
    )(*lefts, *weights, *added)


def outer_kernel(left_ref, left_other_ref, right_ref, right_other_ref, out_ref):
    out_ref[0] = low_bits(
        dot(left_ref[...], right_ref[...], DOWN) + dot(left_other_ref[...], right_other_ref[...], DOWN)
    )


def outer_rows(lefts, rights):
    count, depth = lefts[0].shape
    span = rights[0].shape[1] // 2
    tile = min(depth, 512)
    left_spec = pl.BlockSpec((count, tile), lambda w, i: (0, i))
    right_spec = pl.BlockSpec((count, span), lambda w, i: (0, w))
    return kernel_call(
        outer_kernel,
        (2, depth // tile),
        [left_spec, left_spec, right_spec, right_spec],
        pl.BlockSpec((1, tile, span), lambda w, i: (w, i, 0)),
        jax.ShapeDtypeStruct((2, depth, span), jnp.bfloat16),
        2 * 2 * count * depth * 2 * span,
        4 * count * (depth + 2 * span) + depth * span * 4,
    )(*lefts, *rights)


def row_tables(half_block, blocks, spots):
    block_at = jnp.arange(2 * half_block, dtype=jnp.int32)
    pieces = []
    for side, order in (("own", ((0, 0), (1, 0), (0, 1), (1, 1))), ("other", ((0, 0), (0, 1), (1, 0), (1, 1)))):
        far = spots["w"] if side == "own" else 1 - spots["w"]
        for flip_u, flip_v in order:
            block = far * 4 + (spots["u"] ^ flip_u) * 2 + (spots["v"] ^ flip_v)
            pieces.append(paired_positions(block * 2 * half_block + block_at, 2 * half_block, blocks))
    positions = jnp.concatenate(pieces)
    cosine, sine = rope_tables(positions)
    cosine, sine = cosine[:, 0], sine[:, 0]
    return (
        jnp.concatenate([cosine, cosine], axis=1),
        jnp.concatenate([-sine, sine], axis=1),
        positions[:, None],
        positions[None, :],
    )


def paired_body(
    tokens,
    cotangent,
    counts,
    query_weight,
    key_weight,
    value_weight,
    output_weight,
    gate_weight,
    up_weight,
    down_weight,
):
    tok_rows = tokens.shape[1]
    spots = {name: lax.axis_index(name) for name in PAIRS}
    c, w, x, u, v = (spots[name] for name in ("c", "w", "x", "u", "v"))
    tables = row_tables(tok_rows // 2, 8, spots)
    live = (w < counts[0]).astype(jnp.float32)
    tile = 256
    head_columns = 3 * HEAD_DIM
    wide_columns = gate_weight.shape[1] // 2
    output_span, down_span = output_weight.shape[0] // 4, down_weight.shape[0] // 4

    token_kept, token_sent = both_halves(tokens, w, 0)
    cotangent_kept, cotangent_sent = both_halves(cotangent, w, 0)
    columns_kept, columns_sent = column_halves(
        [query_weight, key_weight, value_weight, gate_weight, up_weight], c
    )
    parts = jnp.concatenate(
        [output_weight.reshape(2, 2, output_span, -1), down_weight.reshape(2, 2, down_span, -1)],
        axis=2,
    )
    parts_kept, parts_sent = both_halves(parts, v, 0)
    token_got, columns_got, parts_got = (
        swap(token_sent[0], "w"),
        swap(columns_sent, "c"),
        swap(parts_sent[0], "v"),
    )
    inputs = wide_bits(jnp.concatenate([token_kept[0], token_got], axis=0))
    normed_in, norm_in_back = jax.vjp(layer_norm, inputs)
    norm_own = low_bits(normed_in)
    columns = join(columns_kept, columns_got, c, 0)
    qkv_piece = columns[:, :head_columns]
    wide_pieces = [
        jnp.concatenate(
            [
                columns[:, at + start : at + start + tile]
                for at in (head_columns, head_columns + wide_columns)
            ],
            axis=1,
        )
        for start in range(0, wide_columns, tile)
    ]
    size = wide_pieces[0].shape[0] // 2
    parts = join(parts_kept[0], parts_got, v, 2)
    parts_kept, parts_sent = both_halves(parts, c, 0)
    norm_u, norm_v, qkv_w, qkv_x, parts_got = stage(
        [(norm_own, "u"), (norm_own, "v"), (qkv_piece, "w"), (qkv_piece, "x"), (parts_sent[0], "c")]
    )
    parts = join(parts_kept, parts_got[None], c, 0)
    parts_kept, parts_sent = both_halves(parts, u, 0)
    norm_uv, qkv_wx, parts_got, cotangent_got = stage(
        [(norm_u, "v"), (qkv_w, "x"), (parts_sent[0], "u"), (cotangent_sent[0], "w")], [norm_v, qkv_x]
    )
    norm_in = weave(norm_own, norm_u, norm_v, norm_uv[:tok_rows], norm_uv[tok_rows:])
    full_qkv = square(qkv_piece, qkv_w, qkv_x, qkv_wx, spots)
    parts = join(parts_kept[0], parts_got, u, 1)
    output_piece, down_piece = parts[:output_span], parts[output_span:]
    down_pieces = [down_piece[: down_span // 2], down_piece[down_span // 2 :]]
    grad_out = wide_bits(jnp.concatenate([cotangent_kept[0], cotangent_got], axis=0)) * live
    grad_own = low_bits(grad_out)

    wide_x0, output_x, output_w, wide_w0a, norm_other = stage(
        [
            (wide_pieces[0], "x"),
            (output_piece, "x"),
            (output_piece, "w"),
            (wide_pieces[0][:size], "w"),
            (norm_in, "c"),
        ],
        [qkv_wx, cotangent_got],
    )
    first = attend(norm_in, full_qkv, tables)
    output_w, norm_other, _ = lax.optimization_barrier((output_w, norm_other, first[0]))
    output_wx = swap(output_w, "x")
    second = attend(norm_other, full_qkv, tables)
    output_x, second, wide_w0a, wide_x0 = lax.optimization_barrier(
        (output_x, second, wide_w0a, wide_x0)
    )
    norm_in = (norm_in, norm_other)
    turned, attended = zip(first, second)
    full_output = square(output_piece, output_w, output_x, output_wx, spots)
    other = swap(ahead_rows([attended[1]], [full_output]), "c")
    wide_w0b, wide_x1, grad_u, grad_v = stage(
        [
            (wide_pieces[0][size:], "w"),
            (wide_pieces[1], "x"),
            (grad_own, "u"),
            (grad_own, "v"),
        ],
        [wide_w0a, wide_x0, first[0], second[0]],
    )
    total = ahead_rows([attended[0]], [full_output], [other])
    from_v, from_u, down_w0, down_x = stage(
        fold_sends(total) + [(down_pieces[0], "w"), (down_piece, "x")],
        [wide_w0b, wide_x1, grad_u, grad_v],
    )
    kept, sends = fold(total, from_v, from_u)
    from_u, from_v, grad_uv, grad_vu, wide_wx0 = stage(
        sends
        + corners(grad_u, grad_v)
        + [(jnp.concatenate([wide_w0a, wide_w0b], axis=0), "x")],
        [down_w0, down_x],
    )
    grad_all = weave(grad_own, grad_u, grad_v, grad_uv, grad_vu)
    after_attn = inputs + fold_end(kept, from_u, from_v)
    normed_mid, norm_mid_back = jax.vjp(layer_norm, after_attn)
    mid_own = low_bits(normed_mid)
    mid_u, mid_v, grad_other, down_wx0, wide_w1a = stage(
        [
            (mid_own, "u"),
            (mid_own, "v"),
            (grad_all, "c"),
            (down_w0, "x"),
            (wide_pieces[1][:size], "w"),
        ],
        [wide_wx0, grad_uv],
    )
    grad_all = (grad_all, grad_other)
    mid_uv, mid_vu, down_w1, wide_wx1a = stage(
        corners(mid_u, mid_v) + [(down_pieces[1], "w"), (wide_w1a, "x")], [grad_other, down_wx0]
    )
    norm_mid = weave(mid_own, mid_u, mid_v, mid_uv, mid_vu)
    full_wide = [
        square(wide_pieces[0], jnp.concatenate([wide_w0a, wide_w0b], axis=0), wide_x0, wide_wx0, spots)
    ]
    half_rows = down_span // 2
    full_down = [square(down_pieces[0], down_w0, down_x[:half_rows], down_wx0, spots)]
    norm_other, wide_w1b, down_wx1 = stage(
        [(norm_mid, "c"), (wide_pieces[1][size:], "w"), (down_w1, "x")], [mid_uv, wide_wx1a]
    )
    norm_mid = (norm_mid, norm_other)

    first = hidden_pass(norm_mid[0], grad_all[0], full_wide[0], full_down[0])
    second = hidden_pass(norm_other, grad_all[1], full_wide[0], full_down[0])
    second, wide_w1b = lax.optimization_barrier((second, wide_w1b))
    passes = [(first, second)]
    wide_outers = [outer_rows(norm_mid, [first[1], second[1]])]
    far0, far_kept0, near0, near_kept0 = corner_blocks(wide_outers[0], w, x)
    wide_wx1b = swap(wide_w1b, "x")
    far_got0 = swap(far0, "x")
    full_wide.append(
        square(
            wide_pieces[1],
            jnp.concatenate([wide_w1a, wide_w1b], axis=0),
            wide_x1,
            jnp.concatenate([wide_wx1a, wide_wx1b], axis=0),
            spots,
        )
    )
    full_down.append(square(down_pieces[1], down_w1, down_x[half_rows:], down_wx1, spots))
    first = hidden_pass(norm_mid[0], grad_all[0], full_wide[1], full_down[1])
    second = hidden_pass(norm_mid[1], grad_all[1], full_wide[1], full_down[1])
    passes.append((first, second))
    grad_wide = [[made[side][1] for made in passes] for side in (0, 1)]
    hidden = [[made[side][0] for made in passes] for side in (0, 1)]
    far_got0, grad_wide[1] = lax.optimization_barrier((far_got0, grad_wide[1]))
    far_sum0 = plus(far_kept0, far_got0)
    wide_g0a, near_got0 = stage([(far_sum0[:size], "w"), (near0, "x")])
    other = swap(back_rows(grad_wide[1], full_wide), "c")
    wide_outers.append(outer_rows(norm_mid, [first[1], second[1]]))
    other, wide_outers[1], wide_g0a, near_got0 = lax.optimization_barrier(
        (other, wide_outers[1], wide_g0a, near_got0)
    )
    far1, far_kept1, near1, near_kept1 = corner_blocks(wide_outers[1], w, x)
    wide_g0b, far_got1 = stage([(far_sum0[size:], "w"), (far1, "x")], [wide_g0a, near_got0])
    total = back_rows(grad_wide[0], full_wide, [other])
    from_v, from_u = stage(fold_sends(total))
    down_outers = [outer_rows([made[0][0], made[1][0]], grad_all) for made in passes]
    down_blocks = [corner_blocks(outer, w, x) for outer in down_outers]
    down_far, down_far_kept, down_near, down_near_kept = (
        jnp.concatenate(blocks, axis=0) for blocks in zip(*down_blocks)
    )
    far_sum1 = plus(far_kept1, far_got1)
    kept, sends = fold(total, from_v, from_u)
    from_u, from_v, wide_g1a, near_got1 = stage(
        sends + [(far_sum1[:size], "w"), (near1, "x")], [wide_g0b, down_far]
    )
    ahead = ahead_rows(hidden[1], full_down)
    grad_norm_mid = fold_end(kept, from_u, from_v)
    grad_after = grad_out + norm_mid_back(grad_norm_mid)[0]
    after_own = low_bits(grad_after)
    after_u, after_v, other, down_far_got = stage(
        [(after_own, "u"), (after_own, "v"), (ahead, "c"), (down_far, "x")], [wide_g1a, near_got1]
    )
    down_sum = plus(down_far_kept, down_far_got)
    after_uv, after_vu, wide_g1b, down_near_got = stage(
        corners(after_u, after_v) + [(far_sum1[size:], "w"), (down_near, "x")], [other, down_far_got]
    )
    total = ahead_rows(hidden[0], full_down, [other])
    after_all = weave(after_own, after_u, after_v, after_uv, after_vu)

    from_v, from_u, down_g0, after_other = stage(
        fold_sends(total) + [(down_sum[:half_rows], "w"), (after_all, "c")], [wide_g1b, down_near_got]
    )
    after_all = (after_all, after_other)
    first = attend_back(after_all[0], full_output, turned[0], tables)
    output_outer = outer_rows(attended, after_all)
    output_far, output_far_kept, output_near, output_near_kept = corner_blocks(output_outer, w, x)
    kept, sends = fold(total, from_v, from_u)
    from_u, from_v, down_g1, output_got = stage(
        sends + [(down_sum[half_rows:], "w"), (output_far, "x")],
        [first, after_other, down_g0, output_outer],
    )
    second = attend_back(after_other, full_output, turned[1], tables)
    grad_qkv = (first, second)
    ahead = back_rows([second], [full_qkv])
    mixed = low_bits((after_attn + fold_end(kept, from_u, from_v)) * live)
    other, mixed_got, output_got, output_near_got = stage(
        [
            (ahead, "c"),
            (mixed[tok_rows:], "w"),
            (plus(output_far_kept, output_got), "w"),
            (output_near, "x"),
        ],
        [down_g1],
    )
    qkv_outer = outer_rows(norm_in, grad_qkv)
    other, qkv_outer = lax.optimization_barrier((other, qkv_outer))
    qkv_far, qkv_far_kept, qkv_near, qkv_near_kept = corner_blocks(qkv_outer, w, x)
    qkv_got = swap(qkv_far, "x")
    total = back_rows([first], [full_qkv], [other])
    qkv_got, total = lax.optimization_barrier((qkv_got, total))
    from_v, from_u, qkv_got = stage(
        fold_sends(total) + [(plus(qkv_far_kept, qkv_got), "w")], [mixed_got, output_got]
    )
    kept, sends = fold(total, from_v, from_u)
    from_u, from_v, qkv_near_got = stage(sends + [(qkv_near, "x")])
    grad_norm_in = fold_end(kept, from_u, from_v)
    token_grad = grad_after + norm_in_back(grad_norm_in)[0]
    token_got = swap(low_bits(token_grad[tok_rows:]), "w")

    def add_up(*values):
        return sum(wide_bits(value) for value in values)

    held = (
        (near_kept0, near_got0, wide_g0a, wide_g0b),
        (near_kept1, near_got1, wide_g1a, wide_g1b),
        (down_near_kept, down_near_got, down_g0, down_g1),
    )
    held, _ = lax.optimization_barrier((held, from_u))
    wide_totals = [
        add_up(kept, got, jnp.concatenate([top, bottom], axis=0)) for kept, got, top, bottom in held
    ]
    down_total = low_bits(wide_totals.pop())
    qkv_total = add_up(qkv_near_kept, qkv_near_got, qkv_got)
    output_total = low_bits(add_up(output_near_kept, output_near_got, output_got))

    wide_total = jnp.concatenate(
        [part[:, at : at + tile] for at in (0, tile) for part in wide_totals], axis=1
    )

    def columns_home(total, sizes):
        kept, sent = both_halves(total, c, 0)
        return join_columns(kept, swap(low_bits(sent), "c"), c, sizes)

    def rows_home(total):
        kept, sent = both_halves(total, u, 1)
        parts = join(kept[None], swap(sent, "u")[None], u, 0)
        kept, sent = both_halves(parts, c, 0)
        parts = join(kept, swap(sent, "c"), c, 0)
        kept, sent = both_halves(parts, v, 2)
        return wide_bits(join(kept[None], swap(sent, "v")[None], v, 0))

    gate_grad, up_grad = columns_home(wide_total, (wide_columns,) * 2)
    query_grad, key_grad, value_grad = columns_home(qkv_total, (HEAD_DIM,) * 3)
    return (
        join(mixed[None, :tok_rows], mixed_got[None], w, 0),
        join(token_grad[None, :tok_rows], wide_bits(token_got)[None], w, 0),
        query_grad,
        key_grad,
        value_grad,
        rows_home(output_total).reshape(output_weight.shape),
        gate_grad,
        up_grad,
        rows_home(down_total).reshape(down_weight.shape),
    )


def paired_solution(mesh):
    pairs = Mesh(mesh.devices.reshape((2,) * 5), PAIRS)
    rows, columns = ("x", "c"), ("w", "u", "v")
    slots = P(rows, columns, None)
    weight = P(rows, columns)
    return jax.shard_map(
        paired_body,
        mesh=pairs,
        in_specs=(slots, slots, P(rows)) + (weight,) * 7,
        out_specs=(slots, slots) + (weight,) * 7,
        check_vma=False,
    )


def solution(mesh):
    if mesh.shape["ctx"] == 8 and mesh.shape["dp"] == 4:
        return paired_solution(mesh)
    in_specs = (
        P("dp", "ctx", None),
        P("dp", "ctx", None),
        P("dp"),
        P("dp", "ctx"),
        P("dp", "ctx"),
        P("dp", "ctx"),
        P("dp", "ctx"),
        P("dp", "ctx"),
        P("dp", "ctx"),
        P("dp", "ctx"),
    )
    out_specs = (
        P("dp", "ctx", None),
        P("dp", "ctx", None),
        P("dp", "ctx"),
        P("dp", "ctx"),
        P("dp", "ctx"),
        P("dp", "ctx"),
        P("dp", "ctx"),
        P("dp", "ctx"),
        P("dp", "ctx"),
    )
    return jax.shard_map(body, mesh=mesh, in_specs=in_specs, out_specs=out_specs, check_vma=False)
```

```python
import functools

import jax
import jax.numpy as jnp
from jax import lax
from jax.experimental import pallas as pl
from jax.experimental.pallas import tpu as pltpu
from jax.sharding import Mesh
from jax.sharding import PartitionSpec as P

HEADS = 16
HEAD_DIM = 128
FF = 8192


epsilon = 1e-05
rope_base = 10000.0


def layer_norm(values):
    centred = values - jnp.mean(values, axis=-1, keepdims=True)
    variance = jnp.mean(centred * centred, axis=-1, keepdims=True)
    return centred * lax.rsqrt(variance + epsilon)


def paired_positions(row_index, tok_rows, blocks):
    half_block = tok_rows // 2
    device = row_index // tok_rows
    offset = row_index % tok_rows
    return jnp.where(
        offset < half_block,
        device * half_block + offset,
        (2 * blocks - 1 - device) * half_block + offset - half_block,
    )


def rope_tables(positions):
    half_dim = HEAD_DIM // 2
    frequency = rope_base ** (-jnp.arange(half_dim, dtype=jnp.float32) / half_dim)
    angles = positions.astype(jnp.float32)[:, None] * frequency[None, :]
    return (jnp.cos(angles)[:, None, :], jnp.sin(angles)[:, None, :])


def rotate(values, cosine_table, sine_table):
    half_dim = values.shape[-1] // 2
    first_half = values[..., :half_dim]
    second_half = values[..., half_dim:]
    return jnp.concatenate(
        [
            first_half * cosine_table - second_half * sine_table,
            second_half * cosine_table + first_half * sine_table,
        ],
        axis=-1,
    )


def outer_sum(left, right):
    return lax.dot_general(
        left, right, (((0,), (0,)), ((), ())), preferred_element_type=jnp.float32
    )


def back_product(grad_rows, weight):
    return lax.dot_general(
        grad_rows, weight, (((1,), (1,)), ((), ())), preferred_element_type=jnp.float32
    )


def block_start(block, tile_span, blocks):
    upper_side = (block >= blocks // tile_span).astype(jnp.int32)
    lead_tile = jnp.where(
        upper_side == 0, block * tile_span, 2 * blocks - (block + 1) * tile_span
    ).astype(jnp.int32)
    return (lead_tile, upper_side)


def tile_starts(tiles, lead_tile, upper_side):
    zero_index = jnp.zeros((), jnp.int32)
    return (lead_tile, upper_side) + (zero_index,) * (tiles.ndim - 2)


def take_block(tiles, lead_tile, upper_side, tile_span):
    piece = lax.dynamic_slice(
        tiles, tile_starts(tiles, lead_tile, upper_side), (tile_span, 1) + tiles.shape[2:]
    )
    return piece.reshape((tile_span * tiles.shape[2],) + tiles.shape[3:])


def add_block(tiles, part, lead_tile, upper_side, tile_span):
    starts = tile_starts(tiles, lead_tile, upper_side)
    piece_shape = (tile_span, 1) + tiles.shape[2:]
    before = lax.dynamic_slice(tiles, starts, piece_shape)
    return lax.dynamic_update_slice(tiles, before + part.reshape(piece_shape), starts)


def block_scores(query_half, query_pos, key_block, key_pos):
    scores = jnp.einsum(
        "qhd,khd->hqk", query_half, key_block, preferred_element_type=jnp.float32
    ) * HEAD_DIM ** (-0.5)
    allowed = query_pos[:, None] >= key_pos[None, :]
    return jnp.where(allowed[None, :, :], scores, -1e30)


def attend_half(query_half, query_pos, tables, needed, tile_span, blocks):
    key_tiles, value_tiles, pos_tiles = tables
    row_count = query_half.shape[0]

    def scores_at(block):
        lead_tile, upper_side = block_start(block, tile_span, blocks)
        key_block = take_block(key_tiles, lead_tile, upper_side, tile_span)
        key_pos = take_block(pos_tiles, lead_tile, upper_side, tile_span)
        return (block_scores(query_half, query_pos, key_block, key_pos), lead_tile, upper_side)

    def total_step(block, carried):
        highest, total_mass = carried
        scores = scores_at(block)[0]
        new_highest = jnp.maximum(highest, jnp.max(scores, axis=-1))
        total_mass = total_mass * jnp.exp(highest - new_highest) + jnp.sum(
            jnp.exp(scores - new_highest[..., None]), axis=-1
        )
        return (new_highest, total_mass)

    start_high = jnp.full((HEADS, row_count), -1e30, jnp.float32)
    highest, total_mass = lax.fori_loop(
        0, needed, total_step, (start_high, jnp.zeros((HEADS, row_count), jnp.float32))
    )
    log_total = highest + jnp.log(total_mass)

    def value_step(block, output_rows):
        scores, lead_tile, upper_side = scores_at(block)
        soft_low = jnp.exp(scores - log_total[..., None]).astype(jnp.bfloat16)
        value_block = take_block(value_tiles, lead_tile, upper_side, tile_span)
        return output_rows + jnp.einsum(
            "hqk,khd->qhd", soft_low, value_block, preferred_element_type=jnp.float32
        )

    output_rows = lax.fori_loop(
        0, needed, value_step, jnp.zeros((row_count, HEADS, HEAD_DIM), jnp.float32)
    )
    return (output_rows, log_total)


def attend_half_back(
    query_half,
    query_pos,
    grad_half,
    log_total,
    centre,
    tables,
    needed,
    tile_span,
    blocks,
    key_grad,
    value_grad,
):
    key_tiles, value_tiles, pos_tiles = tables
    score_scale = HEAD_DIM ** (-0.5)

    def back_step(block, state):
        query_grad, key_acc, value_acc = state
        lead_tile, upper_side = block_start(block, tile_span, blocks)
        key_block = take_block(key_tiles, lead_tile, upper_side, tile_span)
        value_block = take_block(value_tiles, lead_tile, upper_side, tile_span)
        key_pos = take_block(pos_tiles, lead_tile, upper_side, tile_span)
        soft = jnp.exp(
            block_scores(query_half, query_pos, key_block, key_pos) - log_total[..., None]
        )
        value_part = jnp.einsum(
            "hqk,qhd->khd", soft.astype(jnp.bfloat16), grad_half, preferred_element_type=jnp.float32
        )
        grad_soft = jnp.einsum(
            "qhd,khd->hqk", grad_half, value_block, preferred_element_type=jnp.float32
        )
        grad_scores = (soft * (grad_soft - centre[..., None]) * score_scale).astype(jnp.bfloat16)
        query_grad = query_grad + jnp.einsum(
            "hqk,khd->qhd", grad_scores, key_block, preferred_element_type=jnp.float32
        )
        key_part = jnp.einsum(
            "hqk,qhd->khd", grad_scores, query_half, preferred_element_type=jnp.float32
        )
        key_acc = add_block(key_acc, key_part, lead_tile, upper_side, tile_span)
        value_acc = add_block(value_acc, value_part, lead_tile, upper_side, tile_span)
        return (query_grad, key_acc, value_acc)

    initial = (jnp.zeros(query_half.shape, jnp.float32), key_grad, value_grad)
    return lax.fori_loop(0, needed, back_step, initial)


def gather_weights(
    query_weight, key_weight, value_weight, output_weight, gate_weight, up_weight, down_weight
):
    row_parts = (
        lax.all_gather(query_weight, "dp", axis=0, tiled=True),
        lax.all_gather(key_weight, "dp", axis=0, tiled=True),
        lax.all_gather(value_weight, "dp", axis=0, tiled=True),
        lax.all_gather(output_weight, "dp", axis=0, tiled=True),
        lax.all_gather(gate_weight, "dp", axis=0, tiled=True),
        lax.all_gather(up_weight, "dp", axis=0, tiled=True),
        lax.all_gather(down_weight, "dp", axis=0, tiled=True),
    )
    return (
        lax.all_gather(row_parts[0], "ctx", axis=1, tiled=True),
        lax.all_gather(row_parts[1], "ctx", axis=1, tiled=True),
        lax.all_gather(row_parts[2], "ctx", axis=1, tiled=True),
        lax.all_gather(row_parts[3], "ctx", axis=1, tiled=True),
        lax.all_gather(row_parts[4], "ctx", axis=1, tiled=True),
        lax.all_gather(row_parts[5], "ctx", axis=1, tiled=True),
        lax.all_gather(row_parts[6], "ctx", axis=1, tiled=True),
    )


def fold_columns(running, operands, grads):
    norm_in_low, attended_low, norm_mid_low, hidden_low = operands
    columns = (
        lax.all_to_all(grads[0], "ctx", split_axis=1, concat_axis=0, tiled=True),
        lax.all_to_all(grads[1], "ctx", split_axis=1, concat_axis=0, tiled=True),
        lax.all_to_all(grads[2], "ctx", split_axis=1, concat_axis=0, tiled=True),
        lax.all_to_all(grads[3], "ctx", split_axis=1, concat_axis=0, tiled=True),
        lax.all_to_all(grads[4], "ctx", split_axis=1, concat_axis=0, tiled=True),
        lax.all_to_all(grads[5], "ctx", split_axis=1, concat_axis=0, tiled=True),
        lax.all_to_all(grads[6], "ctx", split_axis=1, concat_axis=0, tiled=True),
    )
    totals = tuple(running)
    norm_in_piece = lax.all_gather(norm_in_low, "ctx", axis=0, tiled=True)
    attended_piece = lax.all_gather(attended_low, "ctx", axis=0, tiled=True)
    norm_mid_piece = lax.all_gather(norm_mid_low, "ctx", axis=0, tiled=True)
    hidden_piece = lax.all_gather(hidden_low, "ctx", axis=0, tiled=True)
    lefts = (
        norm_in_piece,
        norm_in_piece,
        norm_in_piece,
        attended_piece,
        norm_mid_piece,
        norm_mid_piece,
        hidden_piece,
    )
    return list(
        tuple(
            (total + outer_sum(left, column) for total, left, column in zip(totals, lefts, columns))
        )
    )


def body(
    tokens,
    cotangent,
    counts,
    query_weight,
    key_weight,
    value_weight,
    output_weight,
    gate_weight,
    up_weight,
    down_weight,
):
    slot_count, tok_rows, model_width = tokens.shape
    blocks = lax.axis_size("ctx")
    ctx_index = lax.axis_index("ctx")
    seq_rows = tok_rows * blocks
    half_rows = tok_rows // 2
    proj_width = HEADS * HEAD_DIM
    tile_span = min(512, seq_rows // 2) // half_rows
    first_needed = ctx_index // tile_span + 1
    second_needed = (2 * blocks - 1 - ctx_index) // tile_span + 1
    own_positions = paired_positions(
        ctx_index * tok_rows + jnp.arange(tok_rows, dtype=jnp.int32), tok_rows, blocks
    )
    pos_tiles = paired_positions(jnp.arange(seq_rows, dtype=jnp.int32), tok_rows, blocks).reshape(
        blocks, 2, half_rows
    )
    cosine_table, sine_table = rope_tables(own_positions)

    def rotate_heads(projected):
        return rotate(
            projected.reshape(tok_rows, HEADS, HEAD_DIM), cosine_table, sine_table
        ).reshape(tok_rows, proj_width)

    running = [
        jnp.zeros((model_width, proj_width // blocks), jnp.float32),
        jnp.zeros((model_width, proj_width // blocks), jnp.float32),
        jnp.zeros((model_width, proj_width // blocks), jnp.float32),
        jnp.zeros((proj_width, model_width // blocks), jnp.float32),
        jnp.zeros((model_width, FF // blocks), jnp.float32),
        jnp.zeros((model_width, FF // blocks), jnp.float32),
        jnp.zeros((FF, model_width // blocks), jnp.float32),
    ]
    outputs = []
    token_grads = []
    for slot_index in range(slot_count):
        gathered = gather_weights(
            query_weight,
            key_weight,
            value_weight,
            output_weight,
            gate_weight,
            up_weight,
            down_weight,
        )
        full_query, full_key, full_value, full_output, full_gate, full_up, full_down = gathered
        live_mask = (slot_index < counts[0]).astype(jnp.float32)
        inputs = tokens[slot_index].astype(jnp.float32)
        normed_in, norm_in_back = jax.vjp(layer_norm, inputs)
        norm_in_low = normed_in.astype(jnp.bfloat16)
        query_proj = jnp.dot(norm_in_low, full_query, preferred_element_type=jnp.float32)
        key_proj = jnp.dot(norm_in_low, full_key, preferred_element_type=jnp.float32)
        value_proj = jnp.dot(norm_in_low, full_value, preferred_element_type=jnp.float32)
        query_rot, query_turn_back = jax.vjp(rotate_heads, query_proj)
        key_rot, key_turn_back = jax.vjp(rotate_heads, key_proj)
        query_heads = query_rot.astype(jnp.bfloat16).reshape(tok_rows, HEADS, HEAD_DIM)
        key_rows, value_rows = (
            lax.all_gather(key_rot.astype(jnp.bfloat16), "ctx", axis=0, tiled=True),
            lax.all_gather(value_proj.astype(jnp.bfloat16), "ctx", axis=0, tiled=True),
        )
        tables = (
            key_rows.reshape(blocks, 2, half_rows, HEADS, HEAD_DIM),
            value_rows.reshape(blocks, 2, half_rows, HEADS, HEAD_DIM),
            pos_tiles,
        )
        first_out, first_total = attend_half(
            query_heads[:half_rows],
            own_positions[:half_rows],
            tables,
            first_needed,
            tile_span,
            blocks,
        )
        second_out, second_total = attend_half(
            query_heads[half_rows:],
            own_positions[half_rows:],
            tables,
            second_needed,
            tile_span,
            blocks,
        )
        attended_wide = jnp.concatenate([first_out, second_out], axis=0)
        attended_low = attended_wide.reshape(tok_rows, proj_width).astype(jnp.bfloat16)
        after_attn = inputs + jnp.dot(attended_low, full_output, preferred_element_type=jnp.float32)
        normed_mid, norm_mid_back = jax.vjp(layer_norm, after_attn)
        norm_mid_low = normed_mid.astype(jnp.bfloat16)
        gate_proj = jnp.dot(norm_mid_low, full_gate, preferred_element_type=jnp.float32)
        up_proj = jnp.dot(norm_mid_low, full_up, preferred_element_type=jnp.float32)
        hidden, hidden_back = jax.vjp(
            lambda gate_in, up_in: jax.nn.silu(gate_in) * up_in, gate_proj, up_proj
        )
        hidden_low = hidden.astype(jnp.bfloat16)
        layer_out = after_attn + jnp.dot(hidden_low, full_down, preferred_element_type=jnp.float32)
        outputs.append((layer_out * live_mask).astype(jnp.bfloat16))
        grad_out = cotangent[slot_index].astype(jnp.float32) * live_mask
        grad_out_low = grad_out.astype(jnp.bfloat16)
        grad_gate_in, grad_up_in = hidden_back(back_product(grad_out_low, full_down))
        grad_gate_low = grad_gate_in.astype(jnp.bfloat16)
        grad_up_low = grad_up_in.astype(jnp.bfloat16)
        grad_norm_mid = back_product(grad_gate_low, full_gate) + back_product(grad_up_low, full_up)
        grad_after = grad_out + norm_mid_back(grad_norm_mid)[0]
        grad_after_low = grad_after.astype(jnp.bfloat16)
        grad_attended_low = back_product(grad_after_low, full_output).astype(jnp.bfloat16)
        grad_heads = grad_attended_low.reshape(tok_rows, HEADS, HEAD_DIM)
        centre = jnp.einsum("qhd,qhd->hq", grad_heads.astype(jnp.float32), attended_wide)
        empty_tiles = jnp.zeros((blocks, 2, half_rows, HEADS, HEAD_DIM), jnp.float32)
        first_query, key_acc, value_acc = attend_half_back(
            query_heads[:half_rows],
            own_positions[:half_rows],
            grad_heads[:half_rows],
            first_total,
            centre[:, :half_rows],
            tables,
            first_needed,
            tile_span,
            blocks,
            empty_tiles,
            empty_tiles,
        )
        second_query, key_acc, value_acc = attend_half_back(
            query_heads[half_rows:],
            own_positions[half_rows:],
            grad_heads[half_rows:],
            second_total,
            centre[:, half_rows:],
            tables,
            second_needed,
            tile_span,
            blocks,
            key_acc,
            value_acc,
        )
        grad_query_rot = jnp.concatenate([first_query, second_query], axis=0).reshape(
            tok_rows, proj_width
        )
        key_share, value_share = (
            lax.psum_scatter(
                key_acc.reshape(seq_rows, proj_width).astype(jnp.bfloat16),
                "ctx",
                scatter_dimension=0,
                tiled=True,
            ).astype(jnp.float32),
            lax.psum_scatter(
                value_acc.reshape(seq_rows, proj_width).astype(jnp.bfloat16),
                "ctx",
                scatter_dimension=0,
                tiled=True,
            ).astype(jnp.float32),
        )
        grad_query_low = query_turn_back(grad_query_rot)[0].astype(jnp.bfloat16)
        grad_key_low = key_turn_back(key_share)[0].astype(jnp.bfloat16)
        grad_value_low = value_share.astype(jnp.bfloat16)
        grad_norm_in = (
            back_product(grad_query_low, full_query)
            + back_product(grad_key_low, full_key)
            + back_product(grad_value_low, full_value)
        )
        token_grads.append(grad_after + norm_in_back(grad_norm_in)[0])
        grads = (
            grad_query_low,
            grad_key_low,
            grad_value_low,
            grad_after_low,
            grad_gate_low,
            grad_up_low,
            grad_out_low,
        )
        running = fold_columns(
            running, (norm_in_low, attended_low, norm_mid_low, hidden_low), grads
        )
    row_sums = (
        lax.psum_scatter(
            running[0].astype(jnp.bfloat16), "dp", scatter_dimension=0, tiled=True
        ).astype(jnp.float32),
        lax.psum_scatter(
            running[1].astype(jnp.bfloat16), "dp", scatter_dimension=0, tiled=True
        ).astype(jnp.float32),
        lax.psum_scatter(
            running[2].astype(jnp.bfloat16), "dp", scatter_dimension=0, tiled=True
        ).astype(jnp.float32),
        lax.psum_scatter(
            running[3].astype(jnp.bfloat16), "dp", scatter_dimension=0, tiled=True
        ).astype(jnp.float32),
        lax.psum_scatter(
            running[4].astype(jnp.bfloat16), "dp", scatter_dimension=0, tiled=True
        ).astype(jnp.float32),
        lax.psum_scatter(
            running[5].astype(jnp.bfloat16), "dp", scatter_dimension=0, tiled=True
        ).astype(jnp.float32),
        lax.psum_scatter(
            running[6].astype(jnp.bfloat16), "dp", scatter_dimension=0, tiled=True
        ).astype(jnp.float32),
    )
    return (
        jnp.stack(outputs),
        jnp.stack(token_grads),
        row_sums[0],
        row_sums[1],
        row_sums[2],
        row_sums[3],
        row_sums[4],
        row_sums[5],
        row_sums[6],
    )


PAIRS = ("x", "c", "w", "u", "v")
SWAP = ((0, 1), (1, 0))


def swap(value, axis):
    return lax.ppermute(value, axis, SWAP)


def join(own, other, bit, axis):
    low = jnp.where(bit == 0, own, other)
    high = jnp.where(bit == 0, other, own)
    return jnp.concatenate([low, high], axis=axis)


def low_bits(value):
    return value.astype(jnp.bfloat16)


def wide_bits(value):
    return value.astype(jnp.float32)


def half(value, bit, axis):
    size = value.shape[axis] // 2
    return lax.dynamic_slice_in_dim(value, bit * size, size, axis)


def stage(sends, waits=()):
    values, _ = lax.optimization_barrier((tuple(value for value, _ in sends), tuple(waits)))
    return [swap(value, axis) for value, (_, axis) in zip(values, sends)]


def both_halves(value, bit, axis):
    return half(value, bit, axis), half(value, 1 - bit, axis)


def column_halves(weights, c):
    return tuple(
        jnp.concatenate([half(weight, bit, 1) for weight in weights], axis=1) for bit in (c, 1 - c)
    )


def join_columns(kept, other, c, counts):
    grads, at = [], 0
    for count in counts:
        grads.append(join(wide_bits(kept[:, at : at + count]), wide_bits(other[:, at : at + count]), c, 1))
        at += count
    return grads


def square(own, beside, across, both, spots):
    first = join(own, across, spots["x"], 0)
    second = join(beside, both, spots["x"], 0)
    return join(first[None], second[None], spots["w"], 0)


def corner_blocks(grad, w, x):
    _, rows, columns = grad.shape
    rows //= 2
    parts = grad.reshape(2, 2, rows, columns)
    return [
        lax.dynamic_slice(parts, (at_w, at_x, 0, 0), (1, 1, rows, columns))[0, 0]
        for at_w, at_x in ((1 - w, 1 - x), (1 - w, x), (w, 1 - x), (w, x))
    ]


def plus(left, right):
    return low_bits(wide_bits(left) + wide_bits(right))


def weave(own, from_u, from_v, first_uv, second_uv):
    size = own.shape[0] // 2
    return jnp.concatenate(
        [
            own[:size],
            from_u[:size],
            from_v[:size],
            first_uv,
            own[size:],
            from_v[size:],
            from_u[size:],
            second_uv,
        ],
        axis=0,
    )


def corners(from_u, from_v):
    size = from_u.shape[0] // 2
    return [(from_u[:size], "v"), (from_v[size:], "u")]


def fold_sends(total):
    size = total.shape[0] // 8
    return [(total[2 * size : 4 * size], "v"), (total[6 * size :], "u")]


def fold(total, from_v, from_u):
    size = total.shape[0] // 8
    first = wide_bits(total[: 2 * size]) + wide_bits(from_v)
    second = wide_bits(total[4 * size : 6 * size]) + wide_bits(from_u)
    kept = jnp.concatenate([first[:size], second[:size]], axis=0)
    return kept, [(low_bits(first[size:]), "u"), (low_bits(second[size:]), "v")]


def fold_end(kept, from_u, from_v):
    return kept + jnp.concatenate([wide_bits(from_u), wide_bits(from_v)], axis=0)


ACROSS = (((1,), (1,)), ((), ()))
DOWN = (((0,), (0,)), ((), ()))
CHUNK = 256
TALL = 1024


def dot(left, right, dims=(((1,), (0,)), ((), ()))):
    return lax.dot_general(left, right, dims, preferred_element_type=jnp.float32)


def whole(shape):
    return pl.BlockSpec(shape, lambda *_: (0,) * len(shape))


def kernel_call(kernel, grid, in_specs, out_specs, out_shape, flops, size, scratch=(), weight=1000):
    return pl.pallas_call(
        kernel,
        grid=grid,
        in_specs=in_specs,
        out_specs=out_specs,
        out_shape=out_shape,
        scratch_shapes=scratch,
        compiler_params=pltpu.CompilerParams(vmem_limit_bytes=48 * 2**20),
        cost_estimate=pl.CostEstimate(
            flops=flops // weight, bytes_accessed=size // weight, transcendentals=0
        ),
    )


def turn(values, cosine, sine):
    return values * cosine + pltpu.roll(values, HEAD_DIM // 2, 1) * sine


def attend_kernel(rows_ref, weight_ref, cos_ref, sin_ref, pos_col_ref, pos_row_ref, *refs):
    turned_ref, out_ref = refs[-2:]
    key_pos = pos_row_ref[...]
    rows = rows_ref.shape[0]

    @pl.loop(0, rows // CHUNK)
    def _(i):
        at = pl.ds(pl.multiple_of(i * CHUNK, CHUNK), CHUNK)
        proj = dot(rows_ref[at, :], weight_ref[0])
        cosine, sine = cos_ref[at, :], sin_ref[at, :]
        turned_ref[at, :HEAD_DIM] = low_bits(turn(proj[:, :HEAD_DIM], cosine, sine))
        turned_ref[at, HEAD_DIM : 2 * HEAD_DIM] = low_bits(
            turn(proj[:, HEAD_DIM : 2 * HEAD_DIM], cosine, sine)
        )
        turned_ref[at, 2 * HEAD_DIM :] = low_bits(proj[:, 2 * HEAD_DIM :])

    @pl.loop(0, rows // CHUNK)
    def _(i):
        at = pl.ds(pl.multiple_of(i * CHUNK, CHUNK), CHUNK)
        scores = dot(turned_ref[at, :HEAD_DIM], turned_ref[:, HEAD_DIM : 2 * HEAD_DIM], ACROSS)
        scores = scores * HEAD_DIM ** (-0.5)
        scores = jnp.where(pos_col_ref[at, :] >= key_pos, scores, -1e30)
        shifted = jnp.exp(scores - jnp.max(scores, axis=1, keepdims=True))
        soft = shifted / jnp.sum(shifted, axis=1, keepdims=True)
        out_ref[at, :] = low_bits(dot(low_bits(soft), turned_ref[:, 2 * HEAD_DIM :]))


def attend(rows, weight, tables, *held):
    count, width = rows.shape
    span = weight.shape[2]
    return kernel_call(
        attend_kernel,
        (2,),
        [
            whole(rows.shape),
            pl.BlockSpec((1, width, span), lambda h: (h, 0, 0)),
            *[whole(table.shape) for table in tables],
            *[pl.BlockSpec(memory_space=pl.ANY) for _ in held],
        ],
        (
            pl.BlockSpec((count, span), lambda h: (0, h)),
            pl.BlockSpec((count, HEAD_DIM), lambda h: (0, h)),
        ),
        (
            jax.ShapeDtypeStruct((count, 2 * span), jnp.bfloat16),
            jax.ShapeDtypeStruct((count, 2 * HEAD_DIM), jnp.bfloat16),
        ),
        2 * count * width * 2 * span + 8 * count * count * HEAD_DIM * 3,
        count * width * 2 + weight.size * 2,
        weight=1,
    )(rows, weight, *tables, *held)


def attend_back_kernel(
    grad_ref, weight_ref, turned_ref, cos_ref, sin_ref, pos_col_ref, pos_row_ref, *refs
):
    out_ref, key_acc, value_acc = refs[-3:]
    key_pos = pos_col_ref[...]
    rows, width = grad_ref.shape
    scale = HEAD_DIM ** (-0.5)
    keys = turned_ref[:, HEAD_DIM : 2 * HEAD_DIM]
    values = turned_ref[:, 2 * HEAD_DIM :]
    key_acc[...] = jnp.zeros_like(key_acc)
    value_acc[...] = jnp.zeros_like(value_acc)
    for start in range(0, rows, CHUNK):
        at = slice(start, start + CHUNK)
        queries = turned_ref[at, :HEAD_DIM]
        grads = low_bits(
            dot(grad_ref[at, : width // 2], weight_ref[0], ACROSS)
            + dot(grad_ref[at, width // 2 :], weight_ref[1], ACROSS)
        )
        scores = dot(keys, queries, ACROSS) * scale
        scores = jnp.where(pos_row_ref[:, at] >= key_pos, scores, -1e30)
        shifted = jnp.exp(scores - jnp.max(scores, axis=0, keepdims=True))
        soft = shifted / jnp.sum(shifted, axis=0, keepdims=True)
        grad_soft = dot(values, grads, ACROSS)
        centre = jnp.sum(soft * grad_soft, axis=0, keepdims=True)
        grad_scores = low_bits(soft * (grad_soft - centre) * scale)
        value_acc[...] += dot(low_bits(soft), grads)
        key_acc[...] += dot(grad_scores, queries)
        query_grad = dot(grad_scores, keys, DOWN)
        out_ref[at, :HEAD_DIM] = low_bits(turn(query_grad, cos_ref[at, :], -sin_ref[at, :]))
    out_ref[:, HEAD_DIM : 2 * HEAD_DIM] = low_bits(turn(key_acc[...], cos_ref[...], -sin_ref[...]))
    out_ref[:, 2 * HEAD_DIM :] = low_bits(value_acc[...])


def attend_back(grads, weight, turned, tables, *held):
    count, width = grads.shape
    span = turned.shape[1] // 2
    return kernel_call(
        attend_back_kernel,
        (2,),
        [
            whole(grads.shape),
            pl.BlockSpec((2, HEAD_DIM, width // 2), lambda h: (0, h, 0)),
            pl.BlockSpec((count, span), lambda h: (0, h)),
            *[whole(table.shape) for table in tables],
            *[pl.BlockSpec(memory_space=pl.ANY) for _ in held],
        ],
        pl.BlockSpec((count, span), lambda h: (0, h)),
        jax.ShapeDtypeStruct(turned.shape, jnp.bfloat16),
        2 * count * width * 2 * HEAD_DIM + 20 * count * count * HEAD_DIM * 2,
        count * width * 2 + turned.size * 4,
        [pltpu.VMEM((count, HEAD_DIM), jnp.float32)] * 2,
    )(grads, weight, turned, *tables, *held)


def hidden_kernel(rows_ref, grad_ref, wide_ref, down_ref, hidden_ref, out_ref):
    rows, width = rows_ref.shape
    span = hidden_ref.shape[1]

    @pl.loop(0, rows // CHUNK)
    def _(i):
        at = pl.ds(pl.multiple_of(i * CHUNK, CHUNK), CHUNK)
        both = dot(rows_ref[at, :], wide_ref[0])
        gate, up = both[:, :span], both[:, span:]
        grad_hidden = dot(grad_ref[at, : width // 2], down_ref[0], ACROSS) + dot(
            grad_ref[at, width // 2 :], down_ref[1], ACROSS
        )
        sigma = jax.nn.sigmoid(gate)
        silu = gate * sigma
        hidden_ref[at, :] = low_bits(silu * up)
        out_ref[at, :span] = low_bits(grad_hidden * up * (sigma * (1.0 + gate * (1.0 - sigma))))
        out_ref[at, span:] = low_bits(grad_hidden * silu)


def hidden_pass(rows, grads, wide, down):
    count, width = rows.shape
    tile = wide.shape[2] // 2
    return kernel_call(
        hidden_kernel,
        (2,),
        [
            whole(rows.shape),
            whole(grads.shape),
            pl.BlockSpec((1, width, 2 * tile), lambda w: (w, 0, 0)),
            pl.BlockSpec((2, tile, width // 2), lambda w: (0, w, 0)),
        ],
        (
            pl.BlockSpec((count, tile), lambda w: (0, w)),
            pl.BlockSpec((count, 2 * tile), lambda w: (0, w)),
        ),
        (
            jax.ShapeDtypeStruct((count, 2 * tile), jnp.bfloat16),
            jax.ShapeDtypeStruct((count, 4 * tile), jnp.bfloat16),
        ),
        2 * count * width * 6 * tile,
        count * width * 4 + wide.size * 3,
    )(rows, grads, wide, down)


def back_kernel(counts, *refs):
    out_ref = refs[-1]
    pairs, more = counts
    lefts, weights = refs[:pairs], refs[pairs : 2 * pairs]
    added = refs[2 * pairs : 2 * pairs + more]
    rows, depth = lefts[0].shape

    @pl.loop(0, rows // TALL)
    def _(i):
        at = pl.ds(pl.multiple_of(i * TALL, TALL), TALL)
        total = sum(
            dot(left_ref[at, : depth // 2], weight_ref[0], ACROSS)
            + dot(left_ref[at, depth // 2 :], weight_ref[1], ACROSS)
            for left_ref, weight_ref in zip(lefts, weights)
        )
        for added_ref in added:
            total += wide_bits(added_ref[at, :])
        out_ref[at, :] = low_bits(total)


def back_rows(lefts, weights, added=(), held=()):
    count, depth = lefts[0].shape
    width = weights[0].shape[1]
    tile = 256
    return kernel_call(
        functools.partial(back_kernel, (len(lefts), len(added))),
        (width // tile,),
        [
            *[whole(left.shape) for left in lefts],
            *[pl.BlockSpec((2, tile, depth // 2), lambda i: (0, i, 0)) for _ in weights],
            *[pl.BlockSpec((count, tile), lambda i: (0, i)) for _ in added],
            *[pl.BlockSpec(memory_space=pl.ANY) for _ in held],
        ],
        pl.BlockSpec((count, tile), lambda i: (0, i)),
        jax.ShapeDtypeStruct((count, width), jnp.bfloat16),
        2 * count * width * depth * len(lefts),
        len(lefts) * (count * (width + depth) * 2 + weights[0].size * 2),
    )(*lefts, *weights, *added, *held)


def ahead_kernel(counts, *refs):
    out_ref = refs[-1]
    pairs, more = counts
    lefts, weights = refs[:pairs], refs[pairs : 2 * pairs]
    added = refs[2 * pairs : 2 * pairs + more]
    rows = lefts[0].shape[0]

    @pl.loop(0, rows // TALL)
    def _(i):
        at = pl.ds(pl.multiple_of(i * TALL, TALL), TALL)
        total = sum(dot(left_ref[at, :], weight_ref[0]) for left_ref, weight_ref in zip(lefts, weights))
        for added_ref in added:
            total += wide_bits(added_ref[at, :])
        out_ref[at, :] = low_bits(total)


def ahead_rows(lefts, weights, added=()):
    count, depth = lefts[0].shape
    span = weights[0].shape[2]
    tile = 512
    tiles = span // tile
    return kernel_call(
        functools.partial(ahead_kernel, (len(lefts), len(added))),
        (2, tiles),
        [
            *[whole(left.shape) for left in lefts],
            *[pl.BlockSpec((1, depth, tile), lambda w, t: (w, 0, t)) for _ in weights],
            *[pl.BlockSpec((count, tile), lambda w, t: (0, w * tiles + t)) for _ in added],
        ],
        pl.BlockSpec((count, tile), lambda w, t: (0, w * tiles + t)),
        jax.ShapeDtypeStruct((count, 2 * span), jnp.bfloat16),
        2 * count * depth * 2 * span * len(lefts),
        len(lefts) * (count * (2 * span + depth) * 2 + weights[0].size * 2),
    )(*lefts, *weights, *added)


def outer_kernel(left_ref, left_other_ref, right_ref, right_other_ref, out_ref):
    out_ref[0] = low_bits(
        dot(left_ref[...], right_ref[...], DOWN) + dot(left_other_ref[...], right_other_ref[...], DOWN)
    )


def outer_rows(lefts, rights):
    count, depth = lefts[0].shape
    span = rights[0].shape[1] // 2
    tile = min(depth, 512)
    left_spec = pl.BlockSpec((count, tile), lambda w, i: (0, i))
    right_spec = pl.BlockSpec((count, span), lambda w, i: (0, w))
    return kernel_call(
        outer_kernel,
        (2, depth // tile),
        [left_spec, left_spec, right_spec, right_spec],
        pl.BlockSpec((1, tile, span), lambda w, i: (w, i, 0)),
        jax.ShapeDtypeStruct((2, depth, span), jnp.bfloat16),
        2 * 2 * count * depth * 2 * span,
        4 * count * (depth + 2 * span) + depth * span * 4,
    )(*lefts, *rights)


def row_tables(half_block, blocks, spots):
    block_at = jnp.arange(2 * half_block, dtype=jnp.int32)
    pieces = []
    for side, order in (("own", ((0, 0), (1, 0), (0, 1), (1, 1))), ("other", ((0, 0), (0, 1), (1, 0), (1, 1)))):
        far = spots["w"] if side == "own" else 1 - spots["w"]
        for flip_u, flip_v in order:
            block = far * 4 + (spots["u"] ^ flip_u) * 2 + (spots["v"] ^ flip_v)
            pieces.append(paired_positions(block * 2 * half_block + block_at, 2 * half_block, blocks))
    positions = jnp.concatenate(pieces)
    cosine, sine = rope_tables(positions)
    cosine, sine = cosine[:, 0], sine[:, 0]
    return (
        jnp.concatenate([cosine, cosine], axis=1),
        jnp.concatenate([-sine, sine], axis=1),
        positions[:, None],
        positions[None, :],
    )


def paired_body(
    tokens,
    cotangent,
    counts,
    query_weight,
    key_weight,
    value_weight,
    output_weight,
    gate_weight,
    up_weight,
    down_weight,
):
    tok_rows = tokens.shape[1]
    spots = {name: lax.axis_index(name) for name in PAIRS}
    c, w, x, u, v = (spots[name] for name in ("c", "w", "x", "u", "v"))
    tables = row_tables(tok_rows // 2, 8, spots)
    live = (w < counts[0]).astype(jnp.float32)
    tile = 256
    head_columns = 3 * HEAD_DIM
    wide_columns = gate_weight.shape[1] // 2
    output_span, down_span = output_weight.shape[0] // 4, down_weight.shape[0] // 4

    token_kept, token_sent = both_halves(tokens, w, 0)
    cotangent_kept, cotangent_sent = both_halves(cotangent, w, 0)
    columns_kept, columns_sent = column_halves(
        [query_weight, key_weight, value_weight, gate_weight, up_weight], c
    )
    parts = jnp.concatenate(
        [output_weight.reshape(2, 2, output_span, -1), down_weight.reshape(2, 2, down_span, -1)],
        axis=2,
    )
    parts_kept, parts_sent = both_halves(parts, v, 0)
    token_got, columns_got, parts_got = (
        swap(token_sent[0], "w"),
        swap(columns_sent, "c"),
        swap(parts_sent[0], "v"),
    )
    inputs = wide_bits(jnp.concatenate([token_kept[0], token_got], axis=0))
    normed_in, norm_in_back = jax.vjp(layer_norm, inputs)
    norm_own = low_bits(normed_in)
    columns = join(columns_kept, columns_got, c, 0)
    qkv_piece = columns[:, :head_columns]
    wide_pieces = [
        jnp.concatenate(
            [
                columns[:, at + start : at + start + tile]
                for at in (head_columns, head_columns + wide_columns)
            ],
            axis=1,
        )
        for start in range(0, wide_columns, tile)
    ]
    size = wide_pieces[0].shape[0] // 2
    parts = join(parts_kept[0], parts_got, v, 2)
    parts_kept, parts_sent = both_halves(parts, c, 0)
    norm_u, norm_v, qkv_w, qkv_x, parts_got = stage(
        [(norm_own, "u"), (norm_own, "v"), (qkv_piece, "w"), (qkv_piece, "x"), (parts_sent[0], "c")]
    )
    parts = join(parts_kept, parts_got[None], c, 0)
    parts_kept, parts_sent = both_halves(parts, u, 0)
    norm_uv, qkv_wx, parts_got, cotangent_got = stage(
        [(norm_u, "v"), (qkv_w, "x"), (parts_sent[0], "u"), (cotangent_sent[0], "w")], [norm_v, qkv_x]
    )
    norm_in = weave(norm_own, norm_u, norm_v, norm_uv[:tok_rows], norm_uv[tok_rows:])
    full_qkv = square(qkv_piece, qkv_w, qkv_x, qkv_wx, spots)
    parts = join(parts_kept[0], parts_got, u, 1)
    output_piece, down_piece = parts[:output_span], parts[output_span:]
    down_pieces = [down_piece[: down_span // 2], down_piece[down_span // 2 :]]
    grad_out = wide_bits(jnp.concatenate([cotangent_kept[0], cotangent_got], axis=0)) * live
    grad_own = low_bits(grad_out)

    output_x, output_w, grad_u, grad_v, norm_other = stage(
        [
            (output_piece, "x"),
            (output_piece, "w"),
            (grad_own, "u"),
            (grad_own, "v"),
            (norm_in, "c"),
        ],
        [qkv_wx, cotangent_got],
    )
    first = attend(norm_in, full_qkv, tables)
    output_w, norm_other, _ = lax.optimization_barrier((output_w, norm_other, first[0]))
    output_wx, wide_w0a = stage([(output_w, "x"), (wide_pieces[0][:size], "w")])
    second = attend(norm_other, full_qkv, tables)
    output_x, second, grad_u, grad_v, wide_w0a = lax.optimization_barrier(
        (output_x, second, grad_u, grad_v, wide_w0a)
    )
    norm_in = (norm_in, norm_other)
    turned, attended = zip(first, second)
    full_output = square(output_piece, output_w, output_x, output_wx, spots)
    other, grad_uv, grad_vu = stage(
        [(ahead_rows([attended[1]], [full_output]), "c")] + corners(grad_u, grad_v)
    )
    total = ahead_rows([attended[0]], [full_output], [other])
    grad_uv, grad_vu, total = lax.optimization_barrier((grad_uv, grad_vu, total))
    grad_all = weave(grad_own, grad_u, grad_v, grad_uv, grad_vu)
    from_v, from_u, wide_w0b, wide_x0, grad_other = stage(
        fold_sends(total)
        + [(wide_pieces[0][size:], "w"), (wide_pieces[0], "x"), (grad_all, "c")],
        [wide_w0a],
    )
    grad_all = (grad_all, grad_other)
    kept, sends = fold(total, from_v, from_u)
    from_u, from_v, down_w0, wide_wx0 = stage(
        sends
        + [(down_pieces[0], "w"), (jnp.concatenate([wide_w0a, wide_w0b], axis=0), "x")],
        [wide_x0, grad_other],
    )
    after_attn = inputs + fold_end(kept, from_u, from_v)
    normed_mid, norm_mid_back = jax.vjp(layer_norm, after_attn)
    mid_own = low_bits(normed_mid)
    mid_u, mid_v, wide_w1a, down_x = stage(
        [(mid_own, "u"), (mid_own, "v"), (wide_pieces[1][:size], "w"), (down_piece, "x")],
        [wide_wx0, down_w0],
    )
    mid_uv, mid_vu, down_w1, down_wx0, wide_wx1a = stage(
        corners(mid_u, mid_v) + [(down_pieces[1], "w"), (down_w0, "x"), (wide_w1a, "x")],
        [down_x],
    )
    norm_mid = weave(mid_own, mid_u, mid_v, mid_uv, mid_vu)
    full_wide = [
        square(wide_pieces[0], jnp.concatenate([wide_w0a, wide_w0b], axis=0), wide_x0, wide_wx0, spots)
    ]
    half_rows = down_span // 2
    full_down = [square(down_pieces[0], down_w0, down_x[:half_rows], down_wx0, spots)]
    norm_other, wide_w1b, wide_x1, down_wx1 = stage(
        [
            (norm_mid, "c"),
            (wide_pieces[1][size:], "w"),
            (wide_pieces[1], "x"),
            (down_w1, "x"),
        ],
        [mid_uv, wide_wx1a, down_wx0],
    )
    norm_mid = (norm_mid, norm_other)

    first = hidden_pass(norm_mid[0], grad_all[0], full_wide[0], full_down[0])
    second = hidden_pass(norm_other, grad_all[1], full_wide[0], full_down[0])
    second, wide_w1b = lax.optimization_barrier((second, wide_w1b))
    passes = [(first, second)]
    wide_outers = [outer_rows(norm_mid, [first[1], second[1]])]
    far0, far_kept0, near0, near_kept0 = corner_blocks(wide_outers[0], w, x)
    wide_wx1b = swap(wide_w1b, "x")
    far_got0 = swap(far0, "x")
    full_wide.append(
        square(
            wide_pieces[1],
            jnp.concatenate([wide_w1a, wide_w1b], axis=0),
            wide_x1,
            jnp.concatenate([wide_wx1a, wide_wx1b], axis=0),
            spots,
        )
    )
    full_down.append(square(down_pieces[1], down_w1, down_x[half_rows:], down_wx1, spots))
    first = hidden_pass(norm_mid[0], grad_all[0], full_wide[1], full_down[1])
    second = hidden_pass(norm_mid[1], grad_all[1], full_wide[1], full_down[1])
    passes.append((first, second))
    grad_wide = [[made[side][1] for made in passes] for side in (0, 1)]
    hidden = [[made[side][0] for made in passes] for side in (0, 1)]
    far_got0, grad_wide[1] = lax.optimization_barrier((far_got0, grad_wide[1]))
    far_sum0 = plus(far_kept0, far_got0)
    wide_g0a, near_got0 = stage([(far_sum0[:size], "w"), (near0, "x")])
    other = swap(back_rows(grad_wide[1], full_wide), "c")
    wide_outers.append(outer_rows(norm_mid, [first[1], second[1]]))
    other, wide_outers[1], wide_g0a, near_got0 = lax.optimization_barrier(
        (other, wide_outers[1], wide_g0a, near_got0)
    )
    far1, far_kept1, near1, near_kept1 = corner_blocks(wide_outers[1], w, x)
    total = back_rows(grad_wide[0], full_wide, [other])
    from_v, from_u, far_got1 = stage(fold_sends(total) + [(far1, "x")])
    ahead = ahead_rows(hidden[1], full_down)
    down_outers = [outer_rows([made[0][0], made[1][0]], grad_all) for made in passes]
    down_blocks = [corner_blocks(outer, w, x) for outer in down_outers]
    down_far, down_far_kept, down_near, down_near_kept = (
        jnp.concatenate(blocks, axis=0) for blocks in zip(*down_blocks)
    )
    far_sum1 = plus(far_kept1, far_got1)
    kept, sends = fold(total, from_v, from_u)
    from_u, from_v, wide_g0b, near_got1 = stage(
        sends + [(far_sum0[size:], "w"), (near1, "x")], [down_far, ahead, far_got1]
    )
    grad_norm_mid = fold_end(kept, from_u, from_v)
    grad_after = grad_out + norm_mid_back(grad_norm_mid)[0]
    after_own = low_bits(grad_after)
    after_u, after_v, other, wide_g1a, down_far_got = stage(
        [
            (after_own, "u"),
            (after_own, "v"),
            (ahead, "c"),
            (far_sum1[:size], "w"),
            (down_far, "x"),
        ],
        [wide_g0b, near_got1],
    )
    down_sum = plus(down_far_kept, down_far_got)
    after_uv, after_vu, wide_g1b, down_near_got = stage(
        corners(after_u, after_v) + [(far_sum1[size:], "w"), (down_near, "x")], [other, down_far_got, wide_g1a]
    )
    total = ahead_rows(hidden[0], full_down, [other])
    after_all = weave(after_own, after_u, after_v, after_uv, after_vu)

    from_v, from_u, down_g0, after_other = stage(
        fold_sends(total) + [(down_sum[:half_rows], "w"), (after_all, "c")], [wide_g1b, down_near_got]
    )
    after_all = (after_all, after_other)
    first = attend_back(after_all[0], full_output, turned[0], tables)
    output_outer = outer_rows(attended, after_all)
    output_far, output_far_kept, output_near, output_near_kept = corner_blocks(output_outer, w, x)
    kept, sends = fold(total, from_v, from_u)
    from_u, from_v, down_g1, output_got = stage(
        sends + [(down_sum[half_rows:], "w"), (output_far, "x")],
        [first, after_other, down_g0, output_outer],
    )
    second = attend_back(after_other, full_output, turned[1], tables)
    grad_qkv = (first, second)
    ahead = back_rows([second], [full_qkv])
    mixed = low_bits((after_attn + fold_end(kept, from_u, from_v)) * live)
    other, mixed_got, output_got, output_near_got = stage(
        [
            (ahead, "c"),
            (mixed[tok_rows:], "w"),
            (plus(output_far_kept, output_got), "w"),
            (output_near, "x"),
        ],
        [down_g1],
    )
    qkv_outer = outer_rows(norm_in, grad_qkv)
    other, qkv_outer = lax.optimization_barrier((other, qkv_outer))
    qkv_far, qkv_far_kept, qkv_near, qkv_near_kept = corner_blocks(qkv_outer, w, x)
    qkv_got = swap(qkv_far, "x")
    total = back_rows([first], [full_qkv], [other])
    qkv_got, total = lax.optimization_barrier((qkv_got, total))
    from_v, from_u, qkv_got = stage(
        fold_sends(total) + [(plus(qkv_far_kept, qkv_got), "w")]
    )
    kept, sends = fold(total, from_v, from_u)
    from_u, from_v, qkv_near_got = stage(sends + [(qkv_near, "x")])
    grad_norm_in = fold_end(kept, from_u, from_v)
    token_grad = grad_after + norm_in_back(grad_norm_in)[0]
    token_got = swap(low_bits(token_grad[tok_rows:]), "w")

    def add_up(*values):
        return sum(wide_bits(value) for value in values)

    held = (
        (near_kept0, near_got0, wide_g0a, wide_g0b),
        (near_kept1, near_got1, wide_g1a, wide_g1b),
        (down_near_kept, down_near_got, down_g0, down_g1),
    )
    held, _ = lax.optimization_barrier((held, from_u))
    wide_totals = [
        add_up(kept, got, jnp.concatenate([top, bottom], axis=0)) for kept, got, top, bottom in held
    ]
    down_total = low_bits(wide_totals.pop())
    qkv_total = add_up(qkv_near_kept, qkv_near_got, qkv_got)
    output_total = low_bits(add_up(output_near_kept, output_near_got, output_got))

    wide_total = jnp.concatenate(
        [part[:, at : at + tile] for at in (0, tile) for part in wide_totals], axis=1
    )

    def columns_home(total, sizes):
        kept, sent = both_halves(total, c, 0)
        return join_columns(kept, swap(low_bits(sent), "c"), c, sizes)

    def rows_home(total):
        kept, sent = both_halves(total, u, 1)
        parts = join(kept[None], swap(sent, "u")[None], u, 0)
        kept, sent = both_halves(parts, c, 0)
        parts = join(kept, swap(sent, "c"), c, 0)
        kept, sent = both_halves(parts, v, 2)
        return wide_bits(join(kept[None], swap(sent, "v")[None], v, 0))

    gate_grad, up_grad = columns_home(wide_total, (wide_columns,) * 2)
    query_grad, key_grad, value_grad = columns_home(qkv_total, (HEAD_DIM,) * 3)
    return (
        join(mixed[None, :tok_rows], mixed_got[None], w, 0),
        join(token_grad[None, :tok_rows], wide_bits(token_got)[None], w, 0),
        query_grad,
        key_grad,
        value_grad,
        rows_home(output_total).reshape(output_weight.shape),
        gate_grad,
        up_grad,
        rows_home(down_total).reshape(down_weight.shape),
    )


def paired_solution(mesh):
    pairs = Mesh(mesh.devices.reshape((2,) * 5), PAIRS)
    rows, columns = ("x", "c"), ("w", "u", "v")
    slots = P(rows, columns, None)
    weight = P(rows, columns)
    return jax.shard_map(
        paired_body,
        mesh=pairs,
        in_specs=(slots, slots, P(rows)) + (weight,) * 7,
        out_specs=(slots, slots) + (weight,) * 7,
        check_vma=False,
    )


def solution(mesh):
    if mesh.shape["ctx"] == 8 and mesh.shape["dp"] == 4:
        return paired_solution(mesh)
    in_specs = (
        P("dp", "ctx", None),
        P("dp", "ctx", None),
        P("dp"),
        P("dp", "ctx"),
        P("dp", "ctx"),
        P("dp", "ctx"),
        P("dp", "ctx"),
        P("dp", "ctx"),
        P("dp", "ctx"),
        P("dp", "ctx"),
    )
    out_specs = (
        P("dp", "ctx", None),
        P("dp", "ctx", None),
        P("dp", "ctx"),
        P("dp", "ctx"),
        P("dp", "ctx"),
        P("dp", "ctx"),
        P("dp", "ctx"),
        P("dp", "ctx"),
        P("dp", "ctx"),
    )
    return jax.shard_map(body, mesh=mesh, in_specs=in_specs, out_specs=out_specs, check_vma=False)
```

```python
import functools

import jax
import jax.numpy as jnp
from jax import lax
from jax.experimental import pallas as pl
from jax.experimental.pallas import tpu as pltpu
from jax.sharding import Mesh
from jax.sharding import PartitionSpec as P

HEADS = 16
HEAD_DIM = 128
FF = 8192


epsilon = 1e-05
rope_base = 10000.0


def layer_norm(values):
    centred = values - jnp.mean(values, axis=-1, keepdims=True)
    variance = jnp.mean(centred * centred, axis=-1, keepdims=True)
    return centred * lax.rsqrt(variance + epsilon)


def paired_positions(row_index, tok_rows, blocks):
    half_block = tok_rows // 2
    device = row_index // tok_rows
    offset = row_index % tok_rows
    return jnp.where(
        offset < half_block,
        device * half_block + offset,
        (2 * blocks - 1 - device) * half_block + offset - half_block,
    )


def rope_tables(positions):
    half_dim = HEAD_DIM // 2
    frequency = rope_base ** (-jnp.arange(half_dim, dtype=jnp.float32) / half_dim)
    angles = positions.astype(jnp.float32)[:, None] * frequency[None, :]
    return (jnp.cos(angles)[:, None, :], jnp.sin(angles)[:, None, :])


def rotate(values, cosine_table, sine_table):
    half_dim = values.shape[-1] // 2
    first_half = values[..., :half_dim]
    second_half = values[..., half_dim:]
    return jnp.concatenate(
        [
            first_half * cosine_table - second_half * sine_table,
            second_half * cosine_table + first_half * sine_table,
        ],
        axis=-1,
    )


def outer_sum(left, right):
    return lax.dot_general(
        left, right, (((0,), (0,)), ((), ())), preferred_element_type=jnp.float32
    )


def back_product(grad_rows, weight):
    return lax.dot_general(
        grad_rows, weight, (((1,), (1,)), ((), ())), preferred_element_type=jnp.float32
    )


def block_start(block, tile_span, blocks):
    upper_side = (block >= blocks // tile_span).astype(jnp.int32)
    lead_tile = jnp.where(
        upper_side == 0, block * tile_span, 2 * blocks - (block + 1) * tile_span
    ).astype(jnp.int32)
    return (lead_tile, upper_side)


def tile_starts(tiles, lead_tile, upper_side):
    zero_index = jnp.zeros((), jnp.int32)
    return (lead_tile, upper_side) + (zero_index,) * (tiles.ndim - 2)


def take_block(tiles, lead_tile, upper_side, tile_span):
    piece = lax.dynamic_slice(
        tiles, tile_starts(tiles, lead_tile, upper_side), (tile_span, 1) + tiles.shape[2:]
    )
    return piece.reshape((tile_span * tiles.shape[2],) + tiles.shape[3:])


def add_block(tiles, part, lead_tile, upper_side, tile_span):
    starts = tile_starts(tiles, lead_tile, upper_side)
    piece_shape = (tile_span, 1) + tiles.shape[2:]
    before = lax.dynamic_slice(tiles, starts, piece_shape)
    return lax.dynamic_update_slice(tiles, before + part.reshape(piece_shape), starts)


def block_scores(query_half, query_pos, key_block, key_pos):
    scores = jnp.einsum(
        "qhd,khd->hqk", query_half, key_block, preferred_element_type=jnp.float32
    ) * HEAD_DIM ** (-0.5)
    allowed = query_pos[:, None] >= key_pos[None, :]
    return jnp.where(allowed[None, :, :], scores, -1e30)


def attend_half(query_half, query_pos, tables, needed, tile_span, blocks):
    key_tiles, value_tiles, pos_tiles = tables
    row_count = query_half.shape[0]

    def scores_at(block):
        lead_tile, upper_side = block_start(block, tile_span, blocks)
        key_block = take_block(key_tiles, lead_tile, upper_side, tile_span)
        key_pos = take_block(pos_tiles, lead_tile, upper_side, tile_span)
        return (block_scores(query_half, query_pos, key_block, key_pos), lead_tile, upper_side)

    def total_step(block, carried):
        highest, total_mass = carried
        scores = scores_at(block)[0]
        new_highest = jnp.maximum(highest, jnp.max(scores, axis=-1))
        total_mass = total_mass * jnp.exp(highest - new_highest) + jnp.sum(
            jnp.exp(scores - new_highest[..., None]), axis=-1
        )
        return (new_highest, total_mass)

    start_high = jnp.full((HEADS, row_count), -1e30, jnp.float32)
    highest, total_mass = lax.fori_loop(
        0, needed, total_step, (start_high, jnp.zeros((HEADS, row_count), jnp.float32))
    )
    log_total = highest + jnp.log(total_mass)

    def value_step(block, output_rows):
        scores, lead_tile, upper_side = scores_at(block)
        soft_low = jnp.exp(scores - log_total[..., None]).astype(jnp.bfloat16)
        value_block = take_block(value_tiles, lead_tile, upper_side, tile_span)
        return output_rows + jnp.einsum(
            "hqk,khd->qhd", soft_low, value_block, preferred_element_type=jnp.float32
        )

    output_rows = lax.fori_loop(
        0, needed, value_step, jnp.zeros((row_count, HEADS, HEAD_DIM), jnp.float32)
    )
    return (output_rows, log_total)


def attend_half_back(
    query_half,
    query_pos,
    grad_half,
    log_total,
    centre,
    tables,
    needed,
    tile_span,
    blocks,
    key_grad,
    value_grad,
):
    key_tiles, value_tiles, pos_tiles = tables
    score_scale = HEAD_DIM ** (-0.5)

    def back_step(block, state):
        query_grad, key_acc, value_acc = state
        lead_tile, upper_side = block_start(block, tile_span, blocks)
        key_block = take_block(key_tiles, lead_tile, upper_side, tile_span)
        value_block = take_block(value_tiles, lead_tile, upper_side, tile_span)
        key_pos = take_block(pos_tiles, lead_tile, upper_side, tile_span)
        soft = jnp.exp(
            block_scores(query_half, query_pos, key_block, key_pos) - log_total[..., None]
        )
        value_part = jnp.einsum(
            "hqk,qhd->khd", soft.astype(jnp.bfloat16), grad_half, preferred_element_type=jnp.float32
        )
        grad_soft = jnp.einsum(
            "qhd,khd->hqk", grad_half, value_block, preferred_element_type=jnp.float32
        )
        grad_scores = (soft * (grad_soft - centre[..., None]) * score_scale).astype(jnp.bfloat16)
        query_grad = query_grad + jnp.einsum(
            "hqk,khd->qhd", grad_scores, key_block, preferred_element_type=jnp.float32
        )
        key_part = jnp.einsum(
            "hqk,qhd->khd", grad_scores, query_half, preferred_element_type=jnp.float32
        )
        key_acc = add_block(key_acc, key_part, lead_tile, upper_side, tile_span)
        value_acc = add_block(value_acc, value_part, lead_tile, upper_side, tile_span)
        return (query_grad, key_acc, value_acc)

    initial = (jnp.zeros(query_half.shape, jnp.float32), key_grad, value_grad)
    return lax.fori_loop(0, needed, back_step, initial)


def gather_weights(
    query_weight, key_weight, value_weight, output_weight, gate_weight, up_weight, down_weight
):
    row_parts = (
        lax.all_gather(query_weight, "dp", axis=0, tiled=True),
        lax.all_gather(key_weight, "dp", axis=0, tiled=True),
        lax.all_gather(value_weight, "dp", axis=0, tiled=True),
        lax.all_gather(output_weight, "dp", axis=0, tiled=True),
        lax.all_gather(gate_weight, "dp", axis=0, tiled=True),
        lax.all_gather(up_weight, "dp", axis=0, tiled=True),
        lax.all_gather(down_weight, "dp", axis=0, tiled=True),
    )
    return (
        lax.all_gather(row_parts[0], "ctx", axis=1, tiled=True),
        lax.all_gather(row_parts[1], "ctx", axis=1, tiled=True),
        lax.all_gather(row_parts[2], "ctx", axis=1, tiled=True),
        lax.all_gather(row_parts[3], "ctx", axis=1, tiled=True),
        lax.all_gather(row_parts[4], "ctx", axis=1, tiled=True),
        lax.all_gather(row_parts[5], "ctx", axis=1, tiled=True),
        lax.all_gather(row_parts[6], "ctx", axis=1, tiled=True),
    )


def fold_columns(running, operands, grads):
    norm_in_low, attended_low, norm_mid_low, hidden_low = operands
    columns = (
        lax.all_to_all(grads[0], "ctx", split_axis=1, concat_axis=0, tiled=True),
        lax.all_to_all(grads[1], "ctx", split_axis=1, concat_axis=0, tiled=True),
        lax.all_to_all(grads[2], "ctx", split_axis=1, concat_axis=0, tiled=True),
        lax.all_to_all(grads[3], "ctx", split_axis=1, concat_axis=0, tiled=True),
        lax.all_to_all(grads[4], "ctx", split_axis=1, concat_axis=0, tiled=True),
        lax.all_to_all(grads[5], "ctx", split_axis=1, concat_axis=0, tiled=True),
        lax.all_to_all(grads[6], "ctx", split_axis=1, concat_axis=0, tiled=True),
    )
    totals = tuple(running)
    norm_in_piece = lax.all_gather(norm_in_low, "ctx", axis=0, tiled=True)
    attended_piece = lax.all_gather(attended_low, "ctx", axis=0, tiled=True)
    norm_mid_piece = lax.all_gather(norm_mid_low, "ctx", axis=0, tiled=True)
    hidden_piece = lax.all_gather(hidden_low, "ctx", axis=0, tiled=True)
    lefts = (
        norm_in_piece,
        norm_in_piece,
        norm_in_piece,
        attended_piece,
        norm_mid_piece,
        norm_mid_piece,
        hidden_piece,
    )
    return list(
        tuple(
            (total + outer_sum(left, column) for total, left, column in zip(totals, lefts, columns))
        )
    )


def body(
    tokens,
    cotangent,
    counts,
    query_weight,
    key_weight,
    value_weight,
    output_weight,
    gate_weight,
    up_weight,
    down_weight,
):
    slot_count, tok_rows, model_width = tokens.shape
    blocks = lax.axis_size("ctx")
    ctx_index = lax.axis_index("ctx")
    seq_rows = tok_rows * blocks
    half_rows = tok_rows // 2
    proj_width = HEADS * HEAD_DIM
    tile_span = min(512, seq_rows // 2) // half_rows
    first_needed = ctx_index // tile_span + 1
    second_needed = (2 * blocks - 1 - ctx_index) // tile_span + 1
    own_positions = paired_positions(
        ctx_index * tok_rows + jnp.arange(tok_rows, dtype=jnp.int32), tok_rows, blocks
    )
    pos_tiles = paired_positions(jnp.arange(seq_rows, dtype=jnp.int32), tok_rows, blocks).reshape(
        blocks, 2, half_rows
    )
    cosine_table, sine_table = rope_tables(own_positions)

    def rotate_heads(projected):
        return rotate(
            projected.reshape(tok_rows, HEADS, HEAD_DIM), cosine_table, sine_table
        ).reshape(tok_rows, proj_width)

    running = [
        jnp.zeros((model_width, proj_width // blocks), jnp.float32),
        jnp.zeros((model_width, proj_width // blocks), jnp.float32),
        jnp.zeros((model_width, proj_width // blocks), jnp.float32),
        jnp.zeros((proj_width, model_width // blocks), jnp.float32),
        jnp.zeros((model_width, FF // blocks), jnp.float32),
        jnp.zeros((model_width, FF // blocks), jnp.float32),
        jnp.zeros((FF, model_width // blocks), jnp.float32),
    ]
    outputs = []
    token_grads = []
    for slot_index in range(slot_count):
        gathered = gather_weights(
            query_weight,
            key_weight,
            value_weight,
            output_weight,
            gate_weight,
            up_weight,
            down_weight,
        )
        full_query, full_key, full_value, full_output, full_gate, full_up, full_down = gathered
        live_mask = (slot_index < counts[0]).astype(jnp.float32)
        inputs = tokens[slot_index].astype(jnp.float32)
        normed_in, norm_in_back = jax.vjp(layer_norm, inputs)
        norm_in_low = normed_in.astype(jnp.bfloat16)
        query_proj = jnp.dot(norm_in_low, full_query, preferred_element_type=jnp.float32)
        key_proj = jnp.dot(norm_in_low, full_key, preferred_element_type=jnp.float32)
        value_proj = jnp.dot(norm_in_low, full_value, preferred_element_type=jnp.float32)
        query_rot, query_turn_back = jax.vjp(rotate_heads, query_proj)
        key_rot, key_turn_back = jax.vjp(rotate_heads, key_proj)
        query_heads = query_rot.astype(jnp.bfloat16).reshape(tok_rows, HEADS, HEAD_DIM)
        key_rows, value_rows = (
            lax.all_gather(key_rot.astype(jnp.bfloat16), "ctx", axis=0, tiled=True),
            lax.all_gather(value_proj.astype(jnp.bfloat16), "ctx", axis=0, tiled=True),
        )
        tables = (
            key_rows.reshape(blocks, 2, half_rows, HEADS, HEAD_DIM),
            value_rows.reshape(blocks, 2, half_rows, HEADS, HEAD_DIM),
            pos_tiles,
        )
        first_out, first_total = attend_half(
            query_heads[:half_rows],
            own_positions[:half_rows],
            tables,
            first_needed,
            tile_span,
            blocks,
        )
        second_out, second_total = attend_half(
            query_heads[half_rows:],
            own_positions[half_rows:],
            tables,
            second_needed,
            tile_span,
            blocks,
        )
        attended_wide = jnp.concatenate([first_out, second_out], axis=0)
        attended_low = attended_wide.reshape(tok_rows, proj_width).astype(jnp.bfloat16)
        after_attn = inputs + jnp.dot(attended_low, full_output, preferred_element_type=jnp.float32)
        normed_mid, norm_mid_back = jax.vjp(layer_norm, after_attn)
        norm_mid_low = normed_mid.astype(jnp.bfloat16)
        gate_proj = jnp.dot(norm_mid_low, full_gate, preferred_element_type=jnp.float32)
        up_proj = jnp.dot(norm_mid_low, full_up, preferred_element_type=jnp.float32)
        hidden, hidden_back = jax.vjp(
            lambda gate_in, up_in: jax.nn.silu(gate_in) * up_in, gate_proj, up_proj
        )
        hidden_low = hidden.astype(jnp.bfloat16)
        layer_out = after_attn + jnp.dot(hidden_low, full_down, preferred_element_type=jnp.float32)
        outputs.append((layer_out * live_mask).astype(jnp.bfloat16))
        grad_out = cotangent[slot_index].astype(jnp.float32) * live_mask
        grad_out_low = grad_out.astype(jnp.bfloat16)
        grad_gate_in, grad_up_in = hidden_back(back_product(grad_out_low, full_down))
        grad_gate_low = grad_gate_in.astype(jnp.bfloat16)
        grad_up_low = grad_up_in.astype(jnp.bfloat16)
        grad_norm_mid = back_product(grad_gate_low, full_gate) + back_product(grad_up_low, full_up)
        grad_after = grad_out + norm_mid_back(grad_norm_mid)[0]
        grad_after_low = grad_after.astype(jnp.bfloat16)
        grad_attended_low = back_product(grad_after_low, full_output).astype(jnp.bfloat16)
        grad_heads = grad_attended_low.reshape(tok_rows, HEADS, HEAD_DIM)
        centre = jnp.einsum("qhd,qhd->hq", grad_heads.astype(jnp.float32), attended_wide)
        empty_tiles = jnp.zeros((blocks, 2, half_rows, HEADS, HEAD_DIM), jnp.float32)
        first_query, key_acc, value_acc = attend_half_back(
            query_heads[:half_rows],
            own_positions[:half_rows],
            grad_heads[:half_rows],
            first_total,
            centre[:, :half_rows],
            tables,
            first_needed,
            tile_span,
            blocks,
            empty_tiles,
            empty_tiles,
        )
        second_query, key_acc, value_acc = attend_half_back(
            query_heads[half_rows:],
            own_positions[half_rows:],
            grad_heads[half_rows:],
            second_total,
            centre[:, half_rows:],
            tables,
            second_needed,
            tile_span,
            blocks,
            key_acc,
            value_acc,
        )
        grad_query_rot = jnp.concatenate([first_query, second_query], axis=0).reshape(
            tok_rows, proj_width
        )
        key_share, value_share = (
            lax.psum_scatter(
                key_acc.reshape(seq_rows, proj_width).astype(jnp.bfloat16),
                "ctx",
                scatter_dimension=0,
                tiled=True,
            ).astype(jnp.float32),
            lax.psum_scatter(
                value_acc.reshape(seq_rows, proj_width).astype(jnp.bfloat16),
                "ctx",
                scatter_dimension=0,
                tiled=True,
            ).astype(jnp.float32),
        )
        grad_query_low = query_turn_back(grad_query_rot)[0].astype(jnp.bfloat16)
        grad_key_low = key_turn_back(key_share)[0].astype(jnp.bfloat16)
        grad_value_low = value_share.astype(jnp.bfloat16)
        grad_norm_in = (
            back_product(grad_query_low, full_query)
            + back_product(grad_key_low, full_key)
            + back_product(grad_value_low, full_value)
        )
        token_grads.append(grad_after + norm_in_back(grad_norm_in)[0])
        grads = (
            grad_query_low,
            grad_key_low,
            grad_value_low,
            grad_after_low,
            grad_gate_low,
            grad_up_low,
            grad_out_low,
        )
        running = fold_columns(
            running, (norm_in_low, attended_low, norm_mid_low, hidden_low), grads
        )
    row_sums = (
        lax.psum_scatter(
            running[0].astype(jnp.bfloat16), "dp", scatter_dimension=0, tiled=True
        ).astype(jnp.float32),
        lax.psum_scatter(
            running[1].astype(jnp.bfloat16), "dp", scatter_dimension=0, tiled=True
        ).astype(jnp.float32),
        lax.psum_scatter(
            running[2].astype(jnp.bfloat16), "dp", scatter_dimension=0, tiled=True
        ).astype(jnp.float32),
        lax.psum_scatter(
            running[3].astype(jnp.bfloat16), "dp", scatter_dimension=0, tiled=True
        ).astype(jnp.float32),
        lax.psum_scatter(
            running[4].astype(jnp.bfloat16), "dp", scatter_dimension=0, tiled=True
        ).astype(jnp.float32),
        lax.psum_scatter(
            running[5].astype(jnp.bfloat16), "dp", scatter_dimension=0, tiled=True
        ).astype(jnp.float32),
        lax.psum_scatter(
            running[6].astype(jnp.bfloat16), "dp", scatter_dimension=0, tiled=True
        ).astype(jnp.float32),
    )
    return (
        jnp.stack(outputs),
        jnp.stack(token_grads),
        row_sums[0],
        row_sums[1],
        row_sums[2],
        row_sums[3],
        row_sums[4],
        row_sums[5],
        row_sums[6],
    )


PAIRS = ("x", "c", "w", "u", "v")
SWAP = ((0, 1), (1, 0))


def swap(value, axis):
    return lax.ppermute(value, axis, SWAP)


def join(own, other, bit, axis):
    low = jnp.where(bit == 0, own, other)
    high = jnp.where(bit == 0, other, own)
    return jnp.concatenate([low, high], axis=axis)


def low_bits(value):
    return value.astype(jnp.bfloat16)


def wide_bits(value):
    return value.astype(jnp.float32)


def half(value, bit, axis):
    size = value.shape[axis] // 2
    return lax.dynamic_slice_in_dim(value, bit * size, size, axis)


def stage(sends, waits=()):
    values, _ = lax.optimization_barrier((tuple(value for value, _ in sends), tuple(waits)))
    return [swap(value, axis) for value, (_, axis) in zip(values, sends)]


def both_halves(value, bit, axis):
    return half(value, bit, axis), half(value, 1 - bit, axis)


def column_halves(weights, c):
    return tuple(
        jnp.concatenate([half(weight, bit, 1) for weight in weights], axis=1) for bit in (c, 1 - c)
    )


def join_columns(kept, other, c, counts):
    grads, at = [], 0
    for count in counts:
        grads.append(join(wide_bits(kept[:, at : at + count]), wide_bits(other[:, at : at + count]), c, 1))
        at += count
    return grads


def square(own, beside, across, both, spots):
    first = join(own, across, spots["x"], 0)
    second = join(beside, both, spots["x"], 0)
    return join(first[None], second[None], spots["w"], 0)


def corner_blocks(grad, w, x):
    _, rows, columns = grad.shape
    rows //= 2
    parts = grad.reshape(2, 2, rows, columns)
    return [
        lax.dynamic_slice(parts, (at_w, at_x, 0, 0), (1, 1, rows, columns))[0, 0]
        for at_w, at_x in ((1 - w, 1 - x), (1 - w, x), (w, 1 - x), (w, x))
    ]


def plus(left, right):
    return low_bits(wide_bits(left) + wide_bits(right))


def weave(own, from_u, from_v, first_uv, second_uv):
    size = own.shape[0] // 2
    return jnp.concatenate(
        [
            own[:size],
            from_u[:size],
            from_v[:size],
            first_uv,
            own[size:],
            from_v[size:],
            from_u[size:],
            second_uv,
        ],
        axis=0,
    )


def corners(from_u, from_v):
    size = from_u.shape[0] // 2
    return [(from_u[:size], "v"), (from_v[size:], "u")]


def fold_sends(total):
    size = total.shape[0] // 8
    return [(total[2 * size : 4 * size], "v"), (total[6 * size :], "u")]


def fold(total, from_v, from_u):
    size = total.shape[0] // 8
    first = wide_bits(total[: 2 * size]) + wide_bits(from_v)
    second = wide_bits(total[4 * size : 6 * size]) + wide_bits(from_u)
    kept = jnp.concatenate([first[:size], second[:size]], axis=0)
    return kept, [(low_bits(first[size:]), "u"), (low_bits(second[size:]), "v")]


def fold_end(kept, from_u, from_v):
    return kept + jnp.concatenate([wide_bits(from_u), wide_bits(from_v)], axis=0)


ACROSS = (((1,), (1,)), ((), ()))
DOWN = (((0,), (0,)), ((), ()))
CHUNK = 256
TALL = 1024


def dot(left, right, dims=(((1,), (0,)), ((), ()))):
    return lax.dot_general(left, right, dims, preferred_element_type=jnp.float32)


def whole(shape):
    return pl.BlockSpec(shape, lambda *_: (0,) * len(shape))


def kernel_call(kernel, grid, in_specs, out_specs, out_shape, flops, size, scratch=(), weight=1000):
    return pl.pallas_call(
        kernel,
        grid=grid,
        in_specs=in_specs,
        out_specs=out_specs,
        out_shape=out_shape,
        scratch_shapes=scratch,
        compiler_params=pltpu.CompilerParams(vmem_limit_bytes=48 * 2**20),
        cost_estimate=pl.CostEstimate(
            flops=flops // weight, bytes_accessed=size // weight, transcendentals=0
        ),
    )


def turn(values, cosine, sine):
    return values * cosine + pltpu.roll(values, HEAD_DIM // 2, 1) * sine


def attend_kernel(rows_ref, weight_ref, cos_ref, sin_ref, pos_col_ref, pos_row_ref, *refs):
    turned_ref, out_ref = refs[-2:]
    key_pos = pos_row_ref[...]
    rows = rows_ref.shape[0]

    @pl.loop(0, rows // CHUNK)
    def _(i):
        at = pl.ds(pl.multiple_of(i * CHUNK, CHUNK), CHUNK)
        proj = dot(rows_ref[at, :], weight_ref[0])
        cosine, sine = cos_ref[at, :], sin_ref[at, :]
        turned_ref[at, :HEAD_DIM] = low_bits(turn(proj[:, :HEAD_DIM], cosine, sine))
        turned_ref[at, HEAD_DIM : 2 * HEAD_DIM] = low_bits(
            turn(proj[:, HEAD_DIM : 2 * HEAD_DIM], cosine, sine)
        )
        turned_ref[at, 2 * HEAD_DIM :] = low_bits(proj[:, 2 * HEAD_DIM :])

    @pl.loop(0, rows // CHUNK)
    def _(i):
        at = pl.ds(pl.multiple_of(i * CHUNK, CHUNK), CHUNK)
        scores = dot(turned_ref[at, :HEAD_DIM], turned_ref[:, HEAD_DIM : 2 * HEAD_DIM], ACROSS)
        scores = scores * HEAD_DIM ** (-0.5)
        scores = jnp.where(pos_col_ref[at, :] >= key_pos, scores, -1e30)
        shifted = jnp.exp(scores - jnp.max(scores, axis=1, keepdims=True))
        soft = shifted / jnp.sum(shifted, axis=1, keepdims=True)
        out_ref[at, :] = low_bits(dot(low_bits(soft), turned_ref[:, 2 * HEAD_DIM :]))


def attend(rows, weight, tables, *held):
    count, width = rows.shape
    span = weight.shape[2]
    return kernel_call(
        attend_kernel,
        (2,),
        [
            whole(rows.shape),
            pl.BlockSpec((1, width, span), lambda h: (h, 0, 0)),
            *[whole(table.shape) for table in tables],
            *[pl.BlockSpec(memory_space=pl.ANY) for _ in held],
        ],
        (
            pl.BlockSpec((count, span), lambda h: (0, h)),
            pl.BlockSpec((count, HEAD_DIM), lambda h: (0, h)),
        ),
        (
            jax.ShapeDtypeStruct((count, 2 * span), jnp.bfloat16),
            jax.ShapeDtypeStruct((count, 2 * HEAD_DIM), jnp.bfloat16),
        ),
        2 * count * width * 2 * span + 8 * count * count * HEAD_DIM * 3,
        count * width * 2 + weight.size * 2,
        weight=1,
    )(rows, weight, *tables, *held)


def attend_back_kernel(
    grad_ref, weight_ref, turned_ref, cos_ref, sin_ref, pos_col_ref, pos_row_ref, *refs
):
    out_ref, key_acc, value_acc = refs[-3:]
    key_pos = pos_col_ref[...]
    rows, width = grad_ref.shape
    scale = HEAD_DIM ** (-0.5)
    keys = turned_ref[:, HEAD_DIM : 2 * HEAD_DIM]
    values = turned_ref[:, 2 * HEAD_DIM :]
    key_acc[...] = jnp.zeros_like(key_acc)
    value_acc[...] = jnp.zeros_like(value_acc)
    for start in range(0, rows, CHUNK):
        at = slice(start, start + CHUNK)
        queries = turned_ref[at, :HEAD_DIM]
        grads = low_bits(
            dot(grad_ref[at, : width // 2], weight_ref[0], ACROSS)
            + dot(grad_ref[at, width // 2 :], weight_ref[1], ACROSS)
        )
        scores = dot(keys, queries, ACROSS) * scale
        scores = jnp.where(pos_row_ref[:, at] >= key_pos, scores, -1e30)
        shifted = jnp.exp(scores - jnp.max(scores, axis=0, keepdims=True))
        soft = shifted / jnp.sum(shifted, axis=0, keepdims=True)
        grad_soft = dot(values, grads, ACROSS)
        centre = jnp.sum(soft * grad_soft, axis=0, keepdims=True)
        grad_scores = low_bits(soft * (grad_soft - centre) * scale)
        value_acc[...] += dot(low_bits(soft), grads)
        key_acc[...] += dot(grad_scores, queries)
        query_grad = dot(grad_scores, keys, DOWN)
        out_ref[at, :HEAD_DIM] = low_bits(turn(query_grad, cos_ref[at, :], -sin_ref[at, :]))
    out_ref[:, HEAD_DIM : 2 * HEAD_DIM] = low_bits(turn(key_acc[...], cos_ref[...], -sin_ref[...]))
    out_ref[:, 2 * HEAD_DIM :] = low_bits(value_acc[...])


def attend_back(grads, weight, turned, tables, *held):
    count, width = grads.shape
    span = turned.shape[1] // 2
    return kernel_call(
        attend_back_kernel,
        (2,),
        [
            whole(grads.shape),
            pl.BlockSpec((2, HEAD_DIM, width // 2), lambda h: (0, h, 0)),
            pl.BlockSpec((count, span), lambda h: (0, h)),
            *[whole(table.shape) for table in tables],
            *[pl.BlockSpec(memory_space=pl.ANY) for _ in held],
        ],
        pl.BlockSpec((count, span), lambda h: (0, h)),
        jax.ShapeDtypeStruct(turned.shape, jnp.bfloat16),
        2 * count * width * 2 * HEAD_DIM + 20 * count * count * HEAD_DIM * 2,
        count * width * 2 + turned.size * 4,
        [pltpu.VMEM((count, HEAD_DIM), jnp.float32)] * 2,
    )(grads, weight, turned, *tables, *held)


def hidden_kernel(rows_ref, grad_ref, wide_ref, down_ref, hidden_ref, out_ref):
    rows, width = rows_ref.shape
    span = hidden_ref.shape[1]

    @pl.loop(0, rows // CHUNK)
    def _(i):
        at = pl.ds(pl.multiple_of(i * CHUNK, CHUNK), CHUNK)
        both = dot(rows_ref[at, :], wide_ref[0])
        gate, up = both[:, :span], both[:, span:]
        grad_hidden = dot(grad_ref[at, : width // 2], down_ref[0], ACROSS) + dot(
            grad_ref[at, width // 2 :], down_ref[1], ACROSS
        )
        sigma = jax.nn.sigmoid(gate)
        silu = gate * sigma
        hidden_ref[at, :] = low_bits(silu * up)
        out_ref[at, :span] = low_bits(grad_hidden * up * (sigma * (1.0 + gate * (1.0 - sigma))))
        out_ref[at, span:] = low_bits(grad_hidden * silu)


def hidden_pass(rows, grads, wide, down):
    count, width = rows.shape
    tile = wide.shape[2] // 2
    return kernel_call(
        hidden_kernel,
        (2,),
        [
            whole(rows.shape),
            whole(grads.shape),
            pl.BlockSpec((1, width, 2 * tile), lambda w: (w, 0, 0)),
            pl.BlockSpec((2, tile, width // 2), lambda w: (0, w, 0)),
        ],
        (
            pl.BlockSpec((count, tile), lambda w: (0, w)),
            pl.BlockSpec((count, 2 * tile), lambda w: (0, w)),
        ),
        (
            jax.ShapeDtypeStruct((count, 2 * tile), jnp.bfloat16),
            jax.ShapeDtypeStruct((count, 4 * tile), jnp.bfloat16),
        ),
        2 * count * width * 6 * tile,
        count * width * 4 + wide.size * 3,
    )(rows, grads, wide, down)


def back_kernel(counts, *refs):
    out_ref = refs[-1]
    pairs, more = counts
    lefts, weights = refs[:pairs], refs[pairs : 2 * pairs]
    added = refs[2 * pairs : 2 * pairs + more]
    rows, depth = lefts[0].shape

    @pl.loop(0, rows // TALL)
    def _(i):
        at = pl.ds(pl.multiple_of(i * TALL, TALL), TALL)
        total = sum(
            dot(left_ref[at, : depth // 2], weight_ref[0], ACROSS)
            + dot(left_ref[at, depth // 2 :], weight_ref[1], ACROSS)
            for left_ref, weight_ref in zip(lefts, weights)
        )
        for added_ref in added:
            total += wide_bits(added_ref[at, :])
        out_ref[at, :] = low_bits(total)


def back_rows(lefts, weights, added=(), held=()):
    count, depth = lefts[0].shape
    width = weights[0].shape[1]
    tile = 256
    return kernel_call(
        functools.partial(back_kernel, (len(lefts), len(added))),
        (width // tile,),
        [
            *[whole(left.shape) for left in lefts],
            *[pl.BlockSpec((2, tile, depth // 2), lambda i: (0, i, 0)) for _ in weights],
            *[pl.BlockSpec((count, tile), lambda i: (0, i)) for _ in added],
            *[pl.BlockSpec(memory_space=pl.ANY) for _ in held],
        ],
        pl.BlockSpec((count, tile), lambda i: (0, i)),
        jax.ShapeDtypeStruct((count, width), jnp.bfloat16),
        2 * count * width * depth * len(lefts),
        len(lefts) * (count * (width + depth) * 2 + weights[0].size * 2),
    )(*lefts, *weights, *added, *held)


def ahead_kernel(counts, *refs):
    out_ref = refs[-1]
    pairs, more = counts
    lefts, weights = refs[:pairs], refs[pairs : 2 * pairs]
    added = refs[2 * pairs : 2 * pairs + more]
    rows = lefts[0].shape[0]

    @pl.loop(0, rows // TALL)
    def _(i):
        at = pl.ds(pl.multiple_of(i * TALL, TALL), TALL)
        total = sum(dot(left_ref[at, :], weight_ref[0]) for left_ref, weight_ref in zip(lefts, weights))
        for added_ref in added:
            total += wide_bits(added_ref[at, :])
        out_ref[at, :] = low_bits(total)


def ahead_rows(lefts, weights, added=()):
    count, depth = lefts[0].shape
    span = weights[0].shape[2]
    tile = 512
    tiles = span // tile
    return kernel_call(
        functools.partial(ahead_kernel, (len(lefts), len(added))),
        (2, tiles),
        [
            *[whole(left.shape) for left in lefts],
            *[pl.BlockSpec((1, depth, tile), lambda w, t: (w, 0, t)) for _ in weights],
            *[pl.BlockSpec((count, tile), lambda w, t: (0, w * tiles + t)) for _ in added],
        ],
        pl.BlockSpec((count, tile), lambda w, t: (0, w * tiles + t)),
        jax.ShapeDtypeStruct((count, 2 * span), jnp.bfloat16),
        2 * count * depth * 2 * span * len(lefts),
        len(lefts) * (count * (2 * span + depth) * 2 + weights[0].size * 2),
    )(*lefts, *weights, *added)


def outer_kernel(left_ref, left_other_ref, right_ref, right_other_ref, out_ref):
    out_ref[0] = low_bits(
        dot(left_ref[...], right_ref[...], DOWN) + dot(left_other_ref[...], right_other_ref[...], DOWN)
    )


def outer_rows(lefts, rights):
    count, depth = lefts[0].shape
    span = rights[0].shape[1] // 2
    tile = min(depth, 512)
    left_spec = pl.BlockSpec((count, tile), lambda w, i: (0, i))
    right_spec = pl.BlockSpec((count, span), lambda w, i: (0, w))
    return kernel_call(
        outer_kernel,
        (2, depth // tile),
        [left_spec, left_spec, right_spec, right_spec],
        pl.BlockSpec((1, tile, span), lambda w, i: (w, i, 0)),
        jax.ShapeDtypeStruct((2, depth, span), jnp.bfloat16),
        2 * 2 * count * depth * 2 * span,
        4 * count * (depth + 2 * span) + depth * span * 4,
    )(*lefts, *rights)


def row_tables(half_block, blocks, spots):
    block_at = jnp.arange(2 * half_block, dtype=jnp.int32)
    pieces = []
    for side, order in (("own", ((0, 0), (1, 0), (0, 1), (1, 1))), ("other", ((0, 0), (0, 1), (1, 0), (1, 1)))):
        far = spots["w"] if side == "own" else 1 - spots["w"]
        for flip_u, flip_v in order:
            block = far * 4 + (spots["u"] ^ flip_u) * 2 + (spots["v"] ^ flip_v)
            pieces.append(paired_positions(block * 2 * half_block + block_at, 2 * half_block, blocks))
    positions = jnp.concatenate(pieces)
    cosine, sine = rope_tables(positions)
    cosine, sine = cosine[:, 0], sine[:, 0]
    return (
        jnp.concatenate([cosine, cosine], axis=1),
        jnp.concatenate([-sine, sine], axis=1),
        positions[:, None],
        positions[None, :],
    )


def paired_body(
    tokens,
    cotangent,
    counts,
    query_weight,
    key_weight,
    value_weight,
    output_weight,
    gate_weight,
    up_weight,
    down_weight,
):
    tok_rows = tokens.shape[1]
    spots = {name: lax.axis_index(name) for name in PAIRS}
    c, w, x, u, v = (spots[name] for name in ("c", "w", "x", "u", "v"))
    tables = row_tables(tok_rows // 2, 8, spots)
    live = (w < counts[0]).astype(jnp.float32)
    tile = 256
    head_columns = 3 * HEAD_DIM
    wide_columns = gate_weight.shape[1] // 2
    output_span, down_span = output_weight.shape[0] // 4, down_weight.shape[0] // 4

    token_kept, token_sent = both_halves(tokens, w, 0)
    cotangent_kept, cotangent_sent = both_halves(cotangent, w, 0)
    columns_kept, columns_sent = column_halves(
        [query_weight, key_weight, value_weight, gate_weight, up_weight], c
    )
    parts = jnp.concatenate(
        [output_weight.reshape(2, 2, output_span, -1), down_weight.reshape(2, 2, down_span, -1)],
        axis=2,
    )
    parts_kept, parts_sent = both_halves(parts, v, 0)
    token_got, columns_got, parts_got = (
        swap(token_sent[0], "w"),
        swap(columns_sent, "c"),
        swap(parts_sent[0], "v"),
    )
    inputs = wide_bits(jnp.concatenate([token_kept[0], token_got], axis=0))
    normed_in, norm_in_back = jax.vjp(layer_norm, inputs)
    norm_own = low_bits(normed_in)
    columns = join(columns_kept, columns_got, c, 0)
    qkv_piece = columns[:, :head_columns]
    wide_pieces = [
        jnp.concatenate(
            [
                columns[:, at + start : at + start + tile]
                for at in (head_columns, head_columns + wide_columns)
            ],
            axis=1,
        )
        for start in range(0, wide_columns, tile)
    ]
    size = wide_pieces[0].shape[0] // 2
    parts = join(parts_kept[0], parts_got, v, 2)
    parts_kept, parts_sent = both_halves(parts, c, 0)
    norm_u, norm_v, qkv_w, qkv_x, parts_got = stage(
        [(norm_own, "u"), (norm_own, "v"), (qkv_piece, "w"), (qkv_piece, "x"), (parts_sent[0], "c")]
    )
    parts = join(parts_kept, parts_got[None], c, 0)
    parts_kept, parts_sent = both_halves(parts, u, 0)
    norm_uv, qkv_wx, parts_got, cotangent_got = stage(
        [(norm_u, "v"), (qkv_w, "x"), (parts_sent[0], "u"), (cotangent_sent[0], "w")], [norm_v, qkv_x]
    )
    norm_in = weave(norm_own, norm_u, norm_v, norm_uv[:tok_rows], norm_uv[tok_rows:])
    full_qkv = square(qkv_piece, qkv_w, qkv_x, qkv_wx, spots)
    parts = join(parts_kept[0], parts_got, u, 1)
    output_piece, down_piece = parts[:output_span], parts[output_span:]
    down_pieces = [down_piece[: down_span // 2], down_piece[down_span // 2 :]]
    grad_out = wide_bits(jnp.concatenate([cotangent_kept[0], cotangent_got], axis=0)) * live
    grad_own = low_bits(grad_out)

    output_x, output_w, grad_u, grad_v, norm_other = stage(
        [
            (output_piece, "x"),
            (output_piece, "w"),
            (grad_own, "u"),
            (grad_own, "v"),
            (norm_in, "c"),
        ],
        [qkv_wx, cotangent_got],
    )
    first = attend(norm_in, full_qkv, tables)
    output_w, norm_other, _ = lax.optimization_barrier((output_w, norm_other, first[0]))
    output_wx, wide_w0a = stage([(output_w, "x"), (wide_pieces[0][:size], "w")])
    second = attend(norm_other, full_qkv, tables)
    output_x, second, grad_u, grad_v, wide_w0a = lax.optimization_barrier(
        (output_x, second, grad_u, grad_v, wide_w0a)
    )
    norm_in = (norm_in, norm_other)
    turned, attended = zip(first, second)
    full_output = square(output_piece, output_w, output_x, output_wx, spots)
    other, grad_uv, grad_vu = stage(
        [(ahead_rows([attended[1]], [full_output]), "c")] + corners(grad_u, grad_v)
    )
    total = ahead_rows([attended[0]], [full_output], [other])
    grad_uv, grad_vu, total = lax.optimization_barrier((grad_uv, grad_vu, total))
    grad_all = weave(grad_own, grad_u, grad_v, grad_uv, grad_vu)
    from_v, from_u, wide_w0b, wide_x0, grad_other = stage(
        fold_sends(total)
        + [(wide_pieces[0][size:], "w"), (wide_pieces[0], "x"), (grad_all, "c")],
        [wide_w0a],
    )
    grad_all = (grad_all, grad_other)
    kept, sends = fold(total, from_v, from_u)
    from_u, from_v, down_w0, wide_wx0 = stage(
        sends
        + [(down_pieces[0], "w"), (jnp.concatenate([wide_w0a, wide_w0b], axis=0), "x")],
        [wide_x0, grad_other],
    )
    after_attn = inputs + fold_end(kept, from_u, from_v)
    normed_mid, norm_mid_back = jax.vjp(layer_norm, after_attn)
    mid_own = low_bits(normed_mid)
    mid_u, mid_v, wide_w1a, down_x = stage(
        [(mid_own, "u"), (mid_own, "v"), (wide_pieces[1][:size], "w"), (down_piece, "x")],
        [wide_wx0, down_w0],
    )
    mid_uv, mid_vu, down_w1, down_wx0, wide_wx1a = stage(
        corners(mid_u, mid_v) + [(down_pieces[1], "w"), (down_w0, "x"), (wide_w1a, "x")],
        [down_x],
    )
    norm_mid = weave(mid_own, mid_u, mid_v, mid_uv, mid_vu)
    full_wide = [
        square(wide_pieces[0], jnp.concatenate([wide_w0a, wide_w0b], axis=0), wide_x0, wide_wx0, spots)
    ]
    half_rows = down_span // 2
    full_down = [square(down_pieces[0], down_w0, down_x[:half_rows], down_wx0, spots)]
    norm_other, wide_w1b, wide_x1, down_wx1 = stage(
        [
            (norm_mid, "c"),
            (wide_pieces[1][size:], "w"),
            (wide_pieces[1], "x"),
            (down_w1, "x"),
        ],
        [mid_uv, wide_wx1a, down_wx0],
    )
    norm_mid = (norm_mid, norm_other)

    first = hidden_pass(norm_mid[0], grad_all[0], full_wide[0], full_down[0])
    second = hidden_pass(norm_other, grad_all[1], full_wide[0], full_down[0])
    second, wide_w1b = lax.optimization_barrier((second, wide_w1b))
    passes = [(first, second)]
    wide_outers = [outer_rows(norm_mid, [first[1], second[1]])]
    far0, far_kept0, near0, near_kept0 = corner_blocks(wide_outers[0], w, x)
    wide_wx1b = swap(wide_w1b, "x")
    far_got0 = swap(far0, "x")
    full_wide.append(
        square(
            wide_pieces[1],
            jnp.concatenate([wide_w1a, wide_w1b], axis=0),
            wide_x1,
            jnp.concatenate([wide_wx1a, wide_wx1b], axis=0),
            spots,
        )
    )
    full_down.append(square(down_pieces[1], down_w1, down_x[half_rows:], down_wx1, spots))
    first = hidden_pass(norm_mid[0], grad_all[0], full_wide[1], full_down[1])
    second = hidden_pass(norm_mid[1], grad_all[1], full_wide[1], full_down[1])
    passes.append((first, second))
    grad_wide = [[made[side][1] for made in passes] for side in (0, 1)]
    hidden = [[made[side][0] for made in passes] for side in (0, 1)]
    far_got0, grad_wide[1] = lax.optimization_barrier((far_got0, grad_wide[1]))
    far_sum0 = plus(far_kept0, far_got0)
    wide_g0a, near_got0 = stage([(far_sum0[:size], "w"), (near0, "x")])
    other = swap(back_rows(grad_wide[1], full_wide), "c")
    wide_outers.append(outer_rows(norm_mid, [first[1], second[1]]))
    other, wide_outers[1], wide_g0a, near_got0 = lax.optimization_barrier(
        (other, wide_outers[1], wide_g0a, near_got0)
    )
    far1, far_kept1, near1, near_kept1 = corner_blocks(wide_outers[1], w, x)
    total = back_rows(grad_wide[0], full_wide, [other])
    from_v, from_u, far_got1 = stage(fold_sends(total) + [(far1, "x")])
    ahead = ahead_rows(hidden[1], full_down)
    down_outers = [outer_rows([made[0][0], made[1][0]], grad_all) for made in passes]
    down_blocks = [corner_blocks(outer, w, x) for outer in down_outers]
    down_far, down_far_kept, down_near, down_near_kept = (
        jnp.concatenate(blocks, axis=0) for blocks in zip(*down_blocks)
    )
    far_sum1 = plus(far_kept1, far_got1)
    kept, sends = fold(total, from_v, from_u)
    from_u, from_v, wide_g0b, near_got1 = stage(
        sends + [(far_sum0[size:], "w"), (near1, "x")], [down_far, ahead, far_got1]
    )
    grad_norm_mid = fold_end(kept, from_u, from_v)
    grad_after = grad_out + norm_mid_back(grad_norm_mid)[0]
    after_own = low_bits(grad_after)
    after_u, after_v, other, wide_g1a, down_far_got = stage(
        [
            (after_own, "u"),
            (after_own, "v"),
            (ahead, "c"),
            (far_sum1[:size], "w"),
            (down_far, "x"),
        ],
        [wide_g0b, near_got1],
    )
    down_sum = plus(down_far_kept, down_far_got)
    after_uv, after_vu, wide_g1b, down_near_got = stage(
        corners(after_u, after_v) + [(far_sum1[size:], "w"), (down_near, "x")], [other, down_far_got, wide_g1a]
    )
    total = ahead_rows(hidden[0], full_down, [other])
    after_all = weave(after_own, after_u, after_v, after_uv, after_vu)

    from_v, from_u, down_g0, after_other = stage(
        fold_sends(total) + [(down_sum[:half_rows], "w"), (after_all, "c")], [wide_g1b, down_near_got]
    )
    after_all = (after_all, after_other)
    first = attend_back(after_all[0], full_output, turned[0], tables)
    output_outer = outer_rows(attended, after_all)
    output_far, output_far_kept, output_near, output_near_kept = corner_blocks(output_outer, w, x)
    kept, sends = fold(total, from_v, from_u)
    from_u, from_v, down_g1, output_got = stage(
        sends + [(down_sum[half_rows:], "w"), (output_far, "x")],
        [first, after_other, down_g0, output_outer],
    )
    second = attend_back(after_other, full_output, turned[1], tables)
    grad_qkv = (first, second)
    ahead = back_rows([second], [full_qkv])
    mixed = low_bits((after_attn + fold_end(kept, from_u, from_v)) * live)
    other, mixed_got, output_got, output_near_got = stage(
        [
            (ahead, "c"),
            (mixed[tok_rows:], "w"),
            (plus(output_far_kept, output_got), "w"),
            (output_near, "x"),
        ],
        [down_g1],
    )
    qkv_outer = outer_rows(norm_in, grad_qkv)
    other, qkv_outer = lax.optimization_barrier((other, qkv_outer))
    qkv_far, qkv_far_kept, qkv_near, qkv_near_kept = corner_blocks(qkv_outer, w, x)
    qkv_got = swap(qkv_far, "x")
    total = back_rows([first], [full_qkv], [other])
    qkv_got, total = lax.optimization_barrier((qkv_got, total))
    from_v, from_u, qkv_got = stage(
        fold_sends(total) + [(plus(qkv_far_kept, qkv_got), "w")]
    )
    kept, sends = fold(total, from_v, from_u)
    from_u, from_v, qkv_near_got = stage(sends + [(qkv_near, "x")])
    grad_norm_in = fold_end(kept, from_u, from_v)
    token_grad = grad_after + norm_in_back(grad_norm_in)[0]
    token_got = swap(low_bits(token_grad[tok_rows:]), "w")

    def add_up(*values):
        return sum(wide_bits(value) for value in values)

    held = (
        (near_kept0, near_got0, wide_g0a, wide_g0b),
        (near_kept1, near_got1, wide_g1a, wide_g1b),
        (down_near_kept, down_near_got, down_g0, down_g1),
    )
    held, _ = lax.optimization_barrier((held, from_u))
    wide_totals = [
        add_up(kept, got, jnp.concatenate([top, bottom], axis=0)) for kept, got, top, bottom in held
    ]
    down_total = low_bits(wide_totals.pop())
    qkv_total = add_up(qkv_near_kept, qkv_near_got, qkv_got)
    output_total = low_bits(add_up(output_near_kept, output_near_got, output_got))

    wide_total = jnp.concatenate(
        [part[:, at : at + tile] for at in (0, tile) for part in wide_totals], axis=1
    )

    def columns_home(total, sizes):
        kept, sent = both_halves(total, c, 0)
        return join_columns(kept, swap(low_bits(sent), "c"), c, sizes)

    def rows_home(total):
        count = total.shape[1] // 4
        even = jnp.concatenate([total[:, :count], total[:, 2 * count : 3 * count]], axis=1)
        odd = jnp.concatenate([total[:, count : 2 * count], total[:, 3 * count :]], axis=1)
        sent = jnp.where(v == 0, odd, even)
        parts = join(jnp.where(v == 0, even, odd)[None], swap(sent, "v")[None], v, 0)
        kept, sent = both_halves(parts, u, 2)
        parts = join(kept[None], swap(sent, "u")[None], u, 0)
        kept, sent = both_halves(parts, c, 0)
        return wide_bits(join(kept[0][:, None], swap(sent, "c")[0][:, None], c, 1))

    gate_grad, up_grad = columns_home(wide_total, (wide_columns,) * 2)
    query_grad, key_grad, value_grad = columns_home(qkv_total, (HEAD_DIM,) * 3)
    output_grad, down_grad = rows_home(output_total), rows_home(down_total)
    token_got, gate_grad, up_grad, down_grad, output_grad = lax.optimization_barrier(
        (token_got, gate_grad, up_grad, down_grad, output_grad)
    )
    return (
        join(mixed[None, :tok_rows], mixed_got[None], w, 0),
        join(token_grad[None, :tok_rows], wide_bits(token_got)[None], w, 0),
        query_grad,
        key_grad,
        value_grad,
        output_grad.reshape(output_weight.shape),
        gate_grad,
        up_grad,
        down_grad.reshape(down_weight.shape),
    )


def paired_solution(mesh):
    pairs = Mesh(mesh.devices.reshape((2,) * 5), PAIRS)
    rows, columns = ("x", "c"), ("w", "u", "v")
    slots = P(rows, columns, None)
    weight = P(rows, columns)
    return jax.shard_map(
        paired_body,
        mesh=pairs,
        in_specs=(slots, slots, P(rows)) + (weight,) * 7,
        out_specs=(slots, slots) + (weight,) * 7,
        check_vma=False,
    )


def solution(mesh):
    if mesh.shape["ctx"] == 8 and mesh.shape["dp"] == 4:
        return paired_solution(mesh)
    in_specs = (
        P("dp", "ctx", None),
        P("dp", "ctx", None),
        P("dp"),
        P("dp", "ctx"),
        P("dp", "ctx"),
        P("dp", "ctx"),
        P("dp", "ctx"),
        P("dp", "ctx"),
        P("dp", "ctx"),
        P("dp", "ctx"),
    )
    out_specs = (
        P("dp", "ctx", None),
        P("dp", "ctx", None),
        P("dp", "ctx"),
        P("dp", "ctx"),
        P("dp", "ctx"),
        P("dp", "ctx"),
        P("dp", "ctx"),
        P("dp", "ctx"),
        P("dp", "ctx"),
    )
    return jax.shard_map(body, mesh=mesh, in_specs=in_specs, out_specs=out_specs, check_vma=False)
```

```python
import functools

import jax
import jax.numpy as jnp
from jax import lax
from jax.experimental import pallas as pl
from jax.experimental.pallas import tpu as pltpu
from jax.sharding import Mesh
from jax.sharding import PartitionSpec as P

HEADS = 16
HEAD_DIM = 128
FF = 8192


epsilon = 1e-05
rope_base = 10000.0


def layer_norm(values):
    centred = values - jnp.mean(values, axis=-1, keepdims=True)
    variance = jnp.mean(centred * centred, axis=-1, keepdims=True)
    return centred * lax.rsqrt(variance + epsilon)


def paired_positions(row_index, tok_rows, blocks):
    half_block = tok_rows // 2
    device = row_index // tok_rows
    offset = row_index % tok_rows
    return jnp.where(
        offset < half_block,
        device * half_block + offset,
        (2 * blocks - 1 - device) * half_block + offset - half_block,
    )


def rope_tables(positions):
    half_dim = HEAD_DIM // 2
    frequency = rope_base ** (-jnp.arange(half_dim, dtype=jnp.float32) / half_dim)
    angles = positions.astype(jnp.float32)[:, None] * frequency[None, :]
    return (jnp.cos(angles)[:, None, :], jnp.sin(angles)[:, None, :])


def rotate(values, cosine_table, sine_table):
    half_dim = values.shape[-1] // 2
    first_half = values[..., :half_dim]
    second_half = values[..., half_dim:]
    return jnp.concatenate(
        [
            first_half * cosine_table - second_half * sine_table,
            second_half * cosine_table + first_half * sine_table,
        ],
        axis=-1,
    )


def outer_sum(left, right):
    return lax.dot_general(
        left, right, (((0,), (0,)), ((), ())), preferred_element_type=jnp.float32
    )


def back_product(grad_rows, weight):
    return lax.dot_general(
        grad_rows, weight, (((1,), (1,)), ((), ())), preferred_element_type=jnp.float32
    )


def block_start(block, tile_span, blocks):
    upper_side = (block >= blocks // tile_span).astype(jnp.int32)
    lead_tile = jnp.where(
        upper_side == 0, block * tile_span, 2 * blocks - (block + 1) * tile_span
    ).astype(jnp.int32)
    return (lead_tile, upper_side)


def tile_starts(tiles, lead_tile, upper_side):
    zero_index = jnp.zeros((), jnp.int32)
    return (lead_tile, upper_side) + (zero_index,) * (tiles.ndim - 2)


def take_block(tiles, lead_tile, upper_side, tile_span):
    piece = lax.dynamic_slice(
        tiles, tile_starts(tiles, lead_tile, upper_side), (tile_span, 1) + tiles.shape[2:]
    )
    return piece.reshape((tile_span * tiles.shape[2],) + tiles.shape[3:])


def add_block(tiles, part, lead_tile, upper_side, tile_span):
    starts = tile_starts(tiles, lead_tile, upper_side)
    piece_shape = (tile_span, 1) + tiles.shape[2:]
    before = lax.dynamic_slice(tiles, starts, piece_shape)
    return lax.dynamic_update_slice(tiles, before + part.reshape(piece_shape), starts)


def block_scores(query_half, query_pos, key_block, key_pos):
    scores = jnp.einsum(
        "qhd,khd->hqk", query_half, key_block, preferred_element_type=jnp.float32
    ) * HEAD_DIM ** (-0.5)
    allowed = query_pos[:, None] >= key_pos[None, :]
    return jnp.where(allowed[None, :, :], scores, -1e30)


def attend_half(query_half, query_pos, tables, needed, tile_span, blocks):
    key_tiles, value_tiles, pos_tiles = tables
    row_count = query_half.shape[0]

    def scores_at(block):
        lead_tile, upper_side = block_start(block, tile_span, blocks)
        key_block = take_block(key_tiles, lead_tile, upper_side, tile_span)
        key_pos = take_block(pos_tiles, lead_tile, upper_side, tile_span)
        return (block_scores(query_half, query_pos, key_block, key_pos), lead_tile, upper_side)

    def total_step(block, carried):
        highest, total_mass = carried
        scores = scores_at(block)[0]
        new_highest = jnp.maximum(highest, jnp.max(scores, axis=-1))
        total_mass = total_mass * jnp.exp(highest - new_highest) + jnp.sum(
            jnp.exp(scores - new_highest[..., None]), axis=-1
        )
        return (new_highest, total_mass)

    start_high = jnp.full((HEADS, row_count), -1e30, jnp.float32)
    highest, total_mass = lax.fori_loop(
        0, needed, total_step, (start_high, jnp.zeros((HEADS, row_count), jnp.float32))
    )
    log_total = highest + jnp.log(total_mass)

    def value_step(block, output_rows):
        scores, lead_tile, upper_side = scores_at(block)
        soft_low = jnp.exp(scores - log_total[..., None]).astype(jnp.bfloat16)
        value_block = take_block(value_tiles, lead_tile, upper_side, tile_span)
        return output_rows + jnp.einsum(
            "hqk,khd->qhd", soft_low, value_block, preferred_element_type=jnp.float32
        )

    output_rows = lax.fori_loop(
        0, needed, value_step, jnp.zeros((row_count, HEADS, HEAD_DIM), jnp.float32)
    )
    return (output_rows, log_total)


def attend_half_back(
    query_half,
    query_pos,
    grad_half,
    log_total,
    centre,
    tables,
    needed,
    tile_span,
    blocks,
    key_grad,
    value_grad,
):
    key_tiles, value_tiles, pos_tiles = tables
    score_scale = HEAD_DIM ** (-0.5)

    def back_step(block, state):
        query_grad, key_acc, value_acc = state
        lead_tile, upper_side = block_start(block, tile_span, blocks)
        key_block = take_block(key_tiles, lead_tile, upper_side, tile_span)
        value_block = take_block(value_tiles, lead_tile, upper_side, tile_span)
        key_pos = take_block(pos_tiles, lead_tile, upper_side, tile_span)
        soft = jnp.exp(
            block_scores(query_half, query_pos, key_block, key_pos) - log_total[..., None]
        )
        value_part = jnp.einsum(
            "hqk,qhd->khd", soft.astype(jnp.bfloat16), grad_half, preferred_element_type=jnp.float32
        )
        grad_soft = jnp.einsum(
            "qhd,khd->hqk", grad_half, value_block, preferred_element_type=jnp.float32
        )
        grad_scores = (soft * (grad_soft - centre[..., None]) * score_scale).astype(jnp.bfloat16)
        query_grad = query_grad + jnp.einsum(
            "hqk,khd->qhd", grad_scores, key_block, preferred_element_type=jnp.float32
        )
        key_part = jnp.einsum(
            "hqk,qhd->khd", grad_scores, query_half, preferred_element_type=jnp.float32
        )
        key_acc = add_block(key_acc, key_part, lead_tile, upper_side, tile_span)
        value_acc = add_block(value_acc, value_part, lead_tile, upper_side, tile_span)
        return (query_grad, key_acc, value_acc)

    initial = (jnp.zeros(query_half.shape, jnp.float32), key_grad, value_grad)
    return lax.fori_loop(0, needed, back_step, initial)


def gather_weights(
    query_weight, key_weight, value_weight, output_weight, gate_weight, up_weight, down_weight
):
    row_parts = (
        lax.all_gather(query_weight, "dp", axis=0, tiled=True),
        lax.all_gather(key_weight, "dp", axis=0, tiled=True),
        lax.all_gather(value_weight, "dp", axis=0, tiled=True),
        lax.all_gather(output_weight, "dp", axis=0, tiled=True),
        lax.all_gather(gate_weight, "dp", axis=0, tiled=True),
        lax.all_gather(up_weight, "dp", axis=0, tiled=True),
        lax.all_gather(down_weight, "dp", axis=0, tiled=True),
    )
    return (
        lax.all_gather(row_parts[0], "ctx", axis=1, tiled=True),
        lax.all_gather(row_parts[1], "ctx", axis=1, tiled=True),
        lax.all_gather(row_parts[2], "ctx", axis=1, tiled=True),
        lax.all_gather(row_parts[3], "ctx", axis=1, tiled=True),
        lax.all_gather(row_parts[4], "ctx", axis=1, tiled=True),
        lax.all_gather(row_parts[5], "ctx", axis=1, tiled=True),
        lax.all_gather(row_parts[6], "ctx", axis=1, tiled=True),
    )


def fold_columns(running, operands, grads):
    norm_in_low, attended_low, norm_mid_low, hidden_low = operands
    columns = (
        lax.all_to_all(grads[0], "ctx", split_axis=1, concat_axis=0, tiled=True),
        lax.all_to_all(grads[1], "ctx", split_axis=1, concat_axis=0, tiled=True),
        lax.all_to_all(grads[2], "ctx", split_axis=1, concat_axis=0, tiled=True),
        lax.all_to_all(grads[3], "ctx", split_axis=1, concat_axis=0, tiled=True),
        lax.all_to_all(grads[4], "ctx", split_axis=1, concat_axis=0, tiled=True),
        lax.all_to_all(grads[5], "ctx", split_axis=1, concat_axis=0, tiled=True),
        lax.all_to_all(grads[6], "ctx", split_axis=1, concat_axis=0, tiled=True),
    )
    totals = tuple(running)
    norm_in_piece = lax.all_gather(norm_in_low, "ctx", axis=0, tiled=True)
    attended_piece = lax.all_gather(attended_low, "ctx", axis=0, tiled=True)
    norm_mid_piece = lax.all_gather(norm_mid_low, "ctx", axis=0, tiled=True)
    hidden_piece = lax.all_gather(hidden_low, "ctx", axis=0, tiled=True)
    lefts = (
        norm_in_piece,
        norm_in_piece,
        norm_in_piece,
        attended_piece,
        norm_mid_piece,
        norm_mid_piece,
        hidden_piece,
    )
    return list(
        tuple(
            (total + outer_sum(left, column) for total, left, column in zip(totals, lefts, columns))
        )
    )


def body(
    tokens,
    cotangent,
    counts,
    query_weight,
    key_weight,
    value_weight,
    output_weight,
    gate_weight,
    up_weight,
    down_weight,
):
    slot_count, tok_rows, model_width = tokens.shape
    blocks = lax.axis_size("ctx")
    ctx_index = lax.axis_index("ctx")
    seq_rows = tok_rows * blocks
    half_rows = tok_rows // 2
    proj_width = HEADS * HEAD_DIM
    tile_span = min(512, seq_rows // 2) // half_rows
    first_needed = ctx_index // tile_span + 1
    second_needed = (2 * blocks - 1 - ctx_index) // tile_span + 1
    own_positions = paired_positions(
        ctx_index * tok_rows + jnp.arange(tok_rows, dtype=jnp.int32), tok_rows, blocks
    )
    pos_tiles = paired_positions(jnp.arange(seq_rows, dtype=jnp.int32), tok_rows, blocks).reshape(
        blocks, 2, half_rows
    )
    cosine_table, sine_table = rope_tables(own_positions)

    def rotate_heads(projected):
        return rotate(
            projected.reshape(tok_rows, HEADS, HEAD_DIM), cosine_table, sine_table
        ).reshape(tok_rows, proj_width)

    running = [
        jnp.zeros((model_width, proj_width // blocks), jnp.float32),
        jnp.zeros((model_width, proj_width // blocks), jnp.float32),
        jnp.zeros((model_width, proj_width // blocks), jnp.float32),
        jnp.zeros((proj_width, model_width // blocks), jnp.float32),
        jnp.zeros((model_width, FF // blocks), jnp.float32),
        jnp.zeros((model_width, FF // blocks), jnp.float32),
        jnp.zeros((FF, model_width // blocks), jnp.float32),
    ]
    outputs = []
    token_grads = []
    for slot_index in range(slot_count):
        gathered = gather_weights(
            query_weight,
            key_weight,
            value_weight,
            output_weight,
            gate_weight,
            up_weight,
            down_weight,
        )
        full_query, full_key, full_value, full_output, full_gate, full_up, full_down = gathered
        live_mask = (slot_index < counts[0]).astype(jnp.float32)
        inputs = tokens[slot_index].astype(jnp.float32)
        normed_in, norm_in_back = jax.vjp(layer_norm, inputs)
        norm_in_low = normed_in.astype(jnp.bfloat16)
        query_proj = jnp.dot(norm_in_low, full_query, preferred_element_type=jnp.float32)
        key_proj = jnp.dot(norm_in_low, full_key, preferred_element_type=jnp.float32)
        value_proj = jnp.dot(norm_in_low, full_value, preferred_element_type=jnp.float32)
        query_rot, query_turn_back = jax.vjp(rotate_heads, query_proj)
        key_rot, key_turn_back = jax.vjp(rotate_heads, key_proj)
        query_heads = query_rot.astype(jnp.bfloat16).reshape(tok_rows, HEADS, HEAD_DIM)
        key_rows, value_rows = (
            lax.all_gather(key_rot.astype(jnp.bfloat16), "ctx", axis=0, tiled=True),
            lax.all_gather(value_proj.astype(jnp.bfloat16), "ctx", axis=0, tiled=True),
        )
        tables = (
            key_rows.reshape(blocks, 2, half_rows, HEADS, HEAD_DIM),
            value_rows.reshape(blocks, 2, half_rows, HEADS, HEAD_DIM),
            pos_tiles,
        )
        first_out, first_total = attend_half(
            query_heads[:half_rows],
            own_positions[:half_rows],
            tables,
            first_needed,
            tile_span,
            blocks,
        )
        second_out, second_total = attend_half(
            query_heads[half_rows:],
            own_positions[half_rows:],
            tables,
            second_needed,
            tile_span,
            blocks,
        )
        attended_wide = jnp.concatenate([first_out, second_out], axis=0)
        attended_low = attended_wide.reshape(tok_rows, proj_width).astype(jnp.bfloat16)
        after_attn = inputs + jnp.dot(attended_low, full_output, preferred_element_type=jnp.float32)
        normed_mid, norm_mid_back = jax.vjp(layer_norm, after_attn)
        norm_mid_low = normed_mid.astype(jnp.bfloat16)
        gate_proj = jnp.dot(norm_mid_low, full_gate, preferred_element_type=jnp.float32)
        up_proj = jnp.dot(norm_mid_low, full_up, preferred_element_type=jnp.float32)
        hidden, hidden_back = jax.vjp(
            lambda gate_in, up_in: jax.nn.silu(gate_in) * up_in, gate_proj, up_proj
        )
        hidden_low = hidden.astype(jnp.bfloat16)
        layer_out = after_attn + jnp.dot(hidden_low, full_down, preferred_element_type=jnp.float32)
        outputs.append((layer_out * live_mask).astype(jnp.bfloat16))
        grad_out = cotangent[slot_index].astype(jnp.float32) * live_mask
        grad_out_low = grad_out.astype(jnp.bfloat16)
        grad_gate_in, grad_up_in = hidden_back(back_product(grad_out_low, full_down))
        grad_gate_low = grad_gate_in.astype(jnp.bfloat16)
        grad_up_low = grad_up_in.astype(jnp.bfloat16)
        grad_norm_mid = back_product(grad_gate_low, full_gate) + back_product(grad_up_low, full_up)
        grad_after = grad_out + norm_mid_back(grad_norm_mid)[0]
        grad_after_low = grad_after.astype(jnp.bfloat16)
        grad_attended_low = back_product(grad_after_low, full_output).astype(jnp.bfloat16)
        grad_heads = grad_attended_low.reshape(tok_rows, HEADS, HEAD_DIM)
        centre = jnp.einsum("qhd,qhd->hq", grad_heads.astype(jnp.float32), attended_wide)
        empty_tiles = jnp.zeros((blocks, 2, half_rows, HEADS, HEAD_DIM), jnp.float32)
        first_query, key_acc, value_acc = attend_half_back(
            query_heads[:half_rows],
            own_positions[:half_rows],
            grad_heads[:half_rows],
            first_total,
            centre[:, :half_rows],
            tables,
            first_needed,
            tile_span,
            blocks,
            empty_tiles,
            empty_tiles,
        )
        second_query, key_acc, value_acc = attend_half_back(
            query_heads[half_rows:],
            own_positions[half_rows:],
            grad_heads[half_rows:],
            second_total,
            centre[:, half_rows:],
            tables,
            second_needed,
            tile_span,
            blocks,
            key_acc,
            value_acc,
        )
        grad_query_rot = jnp.concatenate([first_query, second_query], axis=0).reshape(
            tok_rows, proj_width
        )
        key_share, value_share = (
            lax.psum_scatter(
                key_acc.reshape(seq_rows, proj_width).astype(jnp.bfloat16),
                "ctx",
                scatter_dimension=0,
                tiled=True,
            ).astype(jnp.float32),
            lax.psum_scatter(
                value_acc.reshape(seq_rows, proj_width).astype(jnp.bfloat16),
                "ctx",
                scatter_dimension=0,
                tiled=True,
            ).astype(jnp.float32),
        )
        grad_query_low = query_turn_back(grad_query_rot)[0].astype(jnp.bfloat16)
        grad_key_low = key_turn_back(key_share)[0].astype(jnp.bfloat16)
        grad_value_low = value_share.astype(jnp.bfloat16)
        grad_norm_in = (
            back_product(grad_query_low, full_query)
            + back_product(grad_key_low, full_key)
            + back_product(grad_value_low, full_value)
        )
        token_grads.append(grad_after + norm_in_back(grad_norm_in)[0])
        grads = (
            grad_query_low,
            grad_key_low,
            grad_value_low,
            grad_after_low,
            grad_gate_low,
            grad_up_low,
            grad_out_low,
        )
        running = fold_columns(
            running, (norm_in_low, attended_low, norm_mid_low, hidden_low), grads
        )
    row_sums = (
        lax.psum_scatter(
            running[0].astype(jnp.bfloat16), "dp", scatter_dimension=0, tiled=True
        ).astype(jnp.float32),
        lax.psum_scatter(
            running[1].astype(jnp.bfloat16), "dp", scatter_dimension=0, tiled=True
        ).astype(jnp.float32),
        lax.psum_scatter(
            running[2].astype(jnp.bfloat16), "dp", scatter_dimension=0, tiled=True
        ).astype(jnp.float32),
        lax.psum_scatter(
            running[3].astype(jnp.bfloat16), "dp", scatter_dimension=0, tiled=True
        ).astype(jnp.float32),
        lax.psum_scatter(
            running[4].astype(jnp.bfloat16), "dp", scatter_dimension=0, tiled=True
        ).astype(jnp.float32),
        lax.psum_scatter(
            running[5].astype(jnp.bfloat16), "dp", scatter_dimension=0, tiled=True
        ).astype(jnp.float32),
        lax.psum_scatter(
            running[6].astype(jnp.bfloat16), "dp", scatter_dimension=0, tiled=True
        ).astype(jnp.float32),
    )
    return (
        jnp.stack(outputs),
        jnp.stack(token_grads),
        row_sums[0],
        row_sums[1],
        row_sums[2],
        row_sums[3],
        row_sums[4],
        row_sums[5],
        row_sums[6],
    )


PAIRS = ("x", "c", "w", "u", "v")
SWAP = ((0, 1), (1, 0))


def swap(value, axis):
    return lax.ppermute(value, axis, SWAP)


def join(own, other, bit, axis):
    low = jnp.where(bit == 0, own, other)
    high = jnp.where(bit == 0, other, own)
    return jnp.concatenate([low, high], axis=axis)


def low_bits(value):
    return value.astype(jnp.bfloat16)


def wide_bits(value):
    return value.astype(jnp.float32)


def half(value, bit, axis):
    size = value.shape[axis] // 2
    return lax.dynamic_slice_in_dim(value, bit * size, size, axis)


def stage(sends, waits=()):
    values, _ = lax.optimization_barrier((tuple(value for value, _ in sends), tuple(waits)))
    return [swap(value, axis) for value, (_, axis) in zip(values, sends)]


def both_halves(value, bit, axis):
    return half(value, bit, axis), half(value, 1 - bit, axis)


def column_halves(weights, c):
    return tuple(
        jnp.concatenate([half(weight, bit, 1) for weight in weights], axis=1) for bit in (c, 1 - c)
    )


def join_columns(kept, other, c, counts):
    grads, at = [], 0
    for count in counts:
        grads.append(join(wide_bits(kept[:, at : at + count]), wide_bits(other[:, at : at + count]), c, 1))
        at += count
    return grads


def square(own, beside, across, both, spots):
    first = join(own, across, spots["x"], 0)
    second = join(beside, both, spots["x"], 0)
    return join(first[None], second[None], spots["w"], 0)


def corner_blocks(grad, w, x):
    _, rows, columns = grad.shape
    rows //= 2
    parts = grad.reshape(2, 2, rows, columns)
    return [
        lax.dynamic_slice(parts, (at_w, at_x, 0, 0), (1, 1, rows, columns))[0, 0]
        for at_w, at_x in ((1 - w, 1 - x), (1 - w, x), (w, 1 - x), (w, x))
    ]


def plus(left, right):
    return low_bits(wide_bits(left) + wide_bits(right))


def weave(own, from_u, from_v, first_uv, second_uv):
    size = own.shape[0] // 2
    return jnp.concatenate(
        [
            own[:size],
            from_u[:size],
            from_v[:size],
            first_uv,
            own[size:],
            from_v[size:],
            from_u[size:],
            second_uv,
        ],
        axis=0,
    )


def corners(from_u, from_v):
    size = from_u.shape[0] // 2
    return [(from_u[:size], "v"), (from_v[size:], "u")]


def fold_sends(total):
    size = total.shape[0] // 8
    return [(total[2 * size : 4 * size], "v"), (total[6 * size :], "u")]


def fold(total, from_v, from_u):
    size = total.shape[0] // 8
    first = wide_bits(total[: 2 * size]) + wide_bits(from_v)
    second = wide_bits(total[4 * size : 6 * size]) + wide_bits(from_u)
    kept = jnp.concatenate([first[:size], second[:size]], axis=0)
    return kept, [(low_bits(first[size:]), "u"), (low_bits(second[size:]), "v")]


def fold_end(kept, from_u, from_v):
    return kept + jnp.concatenate([wide_bits(from_u), wide_bits(from_v)], axis=0)


ACROSS = (((1,), (1,)), ((), ()))
DOWN = (((0,), (0,)), ((), ()))
CHUNK = 256
TALL = 1024


def dot(left, right, dims=(((1,), (0,)), ((), ()))):
    return lax.dot_general(left, right, dims, preferred_element_type=jnp.float32)


def whole(shape):
    return pl.BlockSpec(shape, lambda *_: (0,) * len(shape))


def kernel_call(kernel, grid, in_specs, out_specs, out_shape, flops, size, scratch=(), weight=1000):
    return pl.pallas_call(
        kernel,
        grid=grid,
        in_specs=in_specs,
        out_specs=out_specs,
        out_shape=out_shape,
        scratch_shapes=scratch,
        compiler_params=pltpu.CompilerParams(vmem_limit_bytes=48 * 2**20),
        cost_estimate=pl.CostEstimate(
            flops=flops // weight, bytes_accessed=size // weight, transcendentals=0
        ),
    )


def turn(values, cosine, sine):
    return values * cosine + pltpu.roll(values, HEAD_DIM // 2, 1) * sine


def attend_kernel(rows_ref, weight_ref, cos_ref, sin_ref, pos_col_ref, pos_row_ref, *refs):
    turned_ref, out_ref = refs[-2:]
    key_pos = pos_row_ref[...]
    rows = rows_ref.shape[0]

    @pl.loop(0, rows // CHUNK)
    def _(i):
        at = pl.ds(pl.multiple_of(i * CHUNK, CHUNK), CHUNK)
        proj = dot(rows_ref[at, :], weight_ref[0])
        cosine, sine = cos_ref[at, :], sin_ref[at, :]
        turned_ref[at, :HEAD_DIM] = low_bits(turn(proj[:, :HEAD_DIM], cosine, sine))
        turned_ref[at, HEAD_DIM : 2 * HEAD_DIM] = low_bits(
            turn(proj[:, HEAD_DIM : 2 * HEAD_DIM], cosine, sine)
        )
        turned_ref[at, 2 * HEAD_DIM :] = low_bits(proj[:, 2 * HEAD_DIM :])

    @pl.loop(0, rows // CHUNK)
    def _(i):
        at = pl.ds(pl.multiple_of(i * CHUNK, CHUNK), CHUNK)
        scores = dot(turned_ref[at, :HEAD_DIM], turned_ref[:, HEAD_DIM : 2 * HEAD_DIM], ACROSS)
        scores = scores * HEAD_DIM ** (-0.5)
        scores = jnp.where(pos_col_ref[at, :] >= key_pos, scores, -1e30)
        shifted = jnp.exp(scores - jnp.max(scores, axis=1, keepdims=True))
        soft = shifted * (1.0 / jnp.sum(shifted, axis=1, keepdims=True))
        out_ref[at, :] = low_bits(dot(low_bits(soft), turned_ref[:, 2 * HEAD_DIM :]))


def attend(rows, weight, tables, *held):
    count, width = rows.shape
    span = weight.shape[2]
    return kernel_call(
        attend_kernel,
        (2,),
        [
            whole(rows.shape),
            pl.BlockSpec((1, width, span), lambda h: (h, 0, 0)),
            *[whole(table.shape) for table in tables],
            *[pl.BlockSpec(memory_space=pl.ANY) for _ in held],
        ],
        (
            pl.BlockSpec((count, span), lambda h: (0, h)),
            pl.BlockSpec((count, HEAD_DIM), lambda h: (0, h)),
        ),
        (
            jax.ShapeDtypeStruct((count, 2 * span), jnp.bfloat16),
            jax.ShapeDtypeStruct((count, 2 * HEAD_DIM), jnp.bfloat16),
        ),
        2 * count * width * 2 * span + 8 * count * count * HEAD_DIM * 3,
        count * width * 2 + weight.size * 2,
        weight=1,
    )(rows, weight, *tables, *held)


def attend_back_kernel(
    grad_ref, weight_ref, turned_ref, cos_ref, sin_ref, pos_col_ref, pos_row_ref, *refs
):
    out_ref, key_acc, value_acc = refs[-3:]
    key_pos = pos_col_ref[...]
    rows, width = grad_ref.shape
    scale = HEAD_DIM ** (-0.5)
    keys = turned_ref[:, HEAD_DIM : 2 * HEAD_DIM]
    values = turned_ref[:, 2 * HEAD_DIM :]
    key_acc[...] = jnp.zeros_like(key_acc)
    value_acc[...] = jnp.zeros_like(value_acc)
    for start in range(0, rows, CHUNK):
        at = slice(start, start + CHUNK)
        queries = turned_ref[at, :HEAD_DIM]
        grads = low_bits(
            dot(grad_ref[at, : width // 2], weight_ref[0], ACROSS)
            + dot(grad_ref[at, width // 2 :], weight_ref[1], ACROSS)
        )
        scores = dot(keys, queries, ACROSS) * scale
        scores = jnp.where(pos_row_ref[:, at] >= key_pos, scores, -1e30)
        shifted = jnp.exp(scores - jnp.max(scores, axis=0, keepdims=True))
        soft = shifted * (1.0 / jnp.sum(shifted, axis=0, keepdims=True))
        grad_soft = dot(values, grads, ACROSS)
        centre = jnp.sum(soft * grad_soft, axis=0, keepdims=True)
        grad_scores = low_bits(soft * (grad_soft - centre) * scale)
        value_acc[...] += dot(low_bits(soft), grads)
        key_acc[...] += dot(grad_scores, queries)
        query_grad = dot(grad_scores, keys, DOWN)
        out_ref[at, :HEAD_DIM] = low_bits(turn(query_grad, cos_ref[at, :], -sin_ref[at, :]))
    out_ref[:, HEAD_DIM : 2 * HEAD_DIM] = low_bits(turn(key_acc[...], cos_ref[...], -sin_ref[...]))
    out_ref[:, 2 * HEAD_DIM :] = low_bits(value_acc[...])


def attend_back(grads, weight, turned, tables, *held):
    count, width = grads.shape
    span = turned.shape[1] // 2
    return kernel_call(
        attend_back_kernel,
        (2,),
        [
            whole(grads.shape),
            pl.BlockSpec((2, HEAD_DIM, width // 2), lambda h: (0, h, 0)),
            pl.BlockSpec((count, span), lambda h: (0, h)),
            *[whole(table.shape) for table in tables],
            *[pl.BlockSpec(memory_space=pl.ANY) for _ in held],
        ],
        pl.BlockSpec((count, span), lambda h: (0, h)),
        jax.ShapeDtypeStruct(turned.shape, jnp.bfloat16),
        2 * count * width * 2 * HEAD_DIM + 20 * count * count * HEAD_DIM * 2,
        count * width * 2 + turned.size * 4,
        [pltpu.VMEM((count, HEAD_DIM), jnp.float32)] * 2,
    )(grads, weight, turned, *tables, *held)


def hidden_kernel(rows_ref, grad_ref, wide_ref, down_ref, hidden_ref, out_ref):
    rows, width = rows_ref.shape
    span = hidden_ref.shape[1]

    @pl.loop(0, rows // CHUNK)
    def _(i):
        at = pl.ds(pl.multiple_of(i * CHUNK, CHUNK), CHUNK)
        both = dot(rows_ref[at, :], wide_ref[0])
        gate, up = both[:, :span], both[:, span:]
        grad_hidden = dot(grad_ref[at, : width // 2], down_ref[0], ACROSS) + dot(
            grad_ref[at, width // 2 :], down_ref[1], ACROSS
        )
        sigma = jax.nn.sigmoid(gate)
        silu = gate * sigma
        hidden_ref[at, :] = low_bits(silu * up)
        out_ref[at, :span] = low_bits(grad_hidden * up * (sigma * (1.0 + gate * (1.0 - sigma))))
        out_ref[at, span:] = low_bits(grad_hidden * silu)


def hidden_pass(rows, grads, wide, down):
    count, width = rows.shape
    tile = wide.shape[2] // 2
    return kernel_call(
        hidden_kernel,
        (2,),
        [
            whole(rows.shape),
            whole(grads.shape),
            pl.BlockSpec((1, width, 2 * tile), lambda w: (w, 0, 0)),
            pl.BlockSpec((2, tile, width // 2), lambda w: (0, w, 0)),
        ],
        (
            pl.BlockSpec((count, tile), lambda w: (0, w)),
            pl.BlockSpec((count, 2 * tile), lambda w: (0, w)),
        ),
        (
            jax.ShapeDtypeStruct((count, 2 * tile), jnp.bfloat16),
            jax.ShapeDtypeStruct((count, 4 * tile), jnp.bfloat16),
        ),
        2 * count * width * 6 * tile,
        count * width * 4 + wide.size * 3,
    )(rows, grads, wide, down)


def back_kernel(counts, *refs):
    out_ref = refs[-1]
    pairs, more = counts
    lefts, weights = refs[:pairs], refs[pairs : 2 * pairs]
    added = refs[2 * pairs : 2 * pairs + more]
    rows, depth = lefts[0].shape

    @pl.loop(0, rows // TALL)
    def _(i):
        at = pl.ds(pl.multiple_of(i * TALL, TALL), TALL)
        total = sum(
            dot(left_ref[at, : depth // 2], weight_ref[0], ACROSS)
            + dot(left_ref[at, depth // 2 :], weight_ref[1], ACROSS)
            for left_ref, weight_ref in zip(lefts, weights)
        )
        for added_ref in added:
            total += wide_bits(added_ref[at, :])
        out_ref[at, :] = low_bits(total)


def back_rows(lefts, weights, added=(), held=()):
    count, depth = lefts[0].shape
    width = weights[0].shape[1]
    tile = 256
    return kernel_call(
        functools.partial(back_kernel, (len(lefts), len(added))),
        (width // tile,),
        [
            *[whole(left.shape) for left in lefts],
            *[pl.BlockSpec((2, tile, depth // 2), lambda i: (0, i, 0)) for _ in weights],
            *[pl.BlockSpec((count, tile), lambda i: (0, i)) for _ in added],
            *[pl.BlockSpec(memory_space=pl.ANY) for _ in held],
        ],
        pl.BlockSpec((count, tile), lambda i: (0, i)),
        jax.ShapeDtypeStruct((count, width), jnp.bfloat16),
        2 * count * width * depth * len(lefts),
        len(lefts) * (count * (width + depth) * 2 + weights[0].size * 2),
    )(*lefts, *weights, *added, *held)


def ahead_kernel(counts, *refs):
    out_ref = refs[-1]
    pairs, more = counts
    lefts, weights = refs[:pairs], refs[pairs : 2 * pairs]
    added = refs[2 * pairs : 2 * pairs + more]
    rows = lefts[0].shape[0]

    @pl.loop(0, rows // TALL)
    def _(i):
        at = pl.ds(pl.multiple_of(i * TALL, TALL), TALL)
        total = sum(dot(left_ref[at, :], weight_ref[0]) for left_ref, weight_ref in zip(lefts, weights))
        for added_ref in added:
            total += wide_bits(added_ref[at, :])
        out_ref[at, :] = low_bits(total)


def ahead_rows(lefts, weights, added=()):
    count, depth = lefts[0].shape
    span = weights[0].shape[2]
    tile = 512
    tiles = span // tile
    return kernel_call(
        functools.partial(ahead_kernel, (len(lefts), len(added))),
        (2, tiles),
        [
            *[whole(left.shape) for left in lefts],
            *[pl.BlockSpec((1, depth, tile), lambda w, t: (w, 0, t)) for _ in weights],
            *[pl.BlockSpec((count, tile), lambda w, t: (0, w * tiles + t)) for _ in added],
        ],
        pl.BlockSpec((count, tile), lambda w, t: (0, w * tiles + t)),
        jax.ShapeDtypeStruct((count, 2 * span), jnp.bfloat16),
        2 * count * depth * 2 * span * len(lefts),
        len(lefts) * (count * (2 * span + depth) * 2 + weights[0].size * 2),
    )(*lefts, *weights, *added)


def outer_kernel(left_ref, left_other_ref, right_ref, right_other_ref, out_ref):
    out_ref[0] = low_bits(
        dot(left_ref[...], right_ref[...], DOWN) + dot(left_other_ref[...], right_other_ref[...], DOWN)
    )


def outer_rows(lefts, rights):
    count, depth = lefts[0].shape
    span = rights[0].shape[1] // 2
    tile = min(depth, 512)
    left_spec = pl.BlockSpec((count, tile), lambda w, i: (0, i))
    right_spec = pl.BlockSpec((count, span), lambda w, i: (0, w))
    return kernel_call(
        outer_kernel,
        (2, depth // tile),
        [left_spec, left_spec, right_spec, right_spec],
        pl.BlockSpec((1, tile, span), lambda w, i: (w, i, 0)),
        jax.ShapeDtypeStruct((2, depth, span), jnp.bfloat16),
        2 * 2 * count * depth * 2 * span,
        4 * count * (depth + 2 * span) + depth * span * 4,
    )(*lefts, *rights)


def row_tables(half_block, blocks, spots):
    block_at = jnp.arange(2 * half_block, dtype=jnp.int32)
    pieces = []
    for side, order in (("own", ((0, 0), (1, 0), (0, 1), (1, 1))), ("other", ((0, 0), (0, 1), (1, 0), (1, 1)))):
        far = spots["w"] if side == "own" else 1 - spots["w"]
        for flip_u, flip_v in order:
            block = far * 4 + (spots["u"] ^ flip_u) * 2 + (spots["v"] ^ flip_v)
            pieces.append(paired_positions(block * 2 * half_block + block_at, 2 * half_block, blocks))
    positions = jnp.concatenate(pieces)
    cosine, sine = rope_tables(positions)
    cosine, sine = cosine[:, 0], sine[:, 0]
    return (
        jnp.concatenate([cosine, cosine], axis=1),
        jnp.concatenate([-sine, sine], axis=1),
        positions[:, None],
        positions[None, :],
    )


def paired_body(
    tokens,
    cotangent,
    counts,
    query_weight,
    key_weight,
    value_weight,
    output_weight,
    gate_weight,
    up_weight,
    down_weight,
):
    tok_rows = tokens.shape[1]
    spots = {name: lax.axis_index(name) for name in PAIRS}
    c, w, x, u, v = (spots[name] for name in ("c", "w", "x", "u", "v"))
    tables = row_tables(tok_rows // 2, 8, spots)
    live = (w < counts[0]).astype(jnp.float32)
    tile = 256
    head_columns = 3 * HEAD_DIM
    wide_columns = gate_weight.shape[1] // 2
    output_span, down_span = output_weight.shape[0] // 4, down_weight.shape[0] // 4

    token_kept, token_sent = both_halves(tokens, w, 0)
    cotangent_kept, cotangent_sent = both_halves(cotangent, w, 0)
    columns_kept, columns_sent = column_halves(
        [query_weight, key_weight, value_weight, gate_weight, up_weight], c
    )
    parts = jnp.concatenate(
        [output_weight.reshape(2, 2, output_span, -1), down_weight.reshape(2, 2, down_span, -1)],
        axis=2,
    )
    parts_kept, parts_sent = both_halves(parts, v, 0)
    token_got, columns_got, parts_got = (
        swap(token_sent[0], "w"),
        swap(columns_sent, "c"),
        swap(parts_sent[0], "v"),
    )
    inputs = wide_bits(jnp.concatenate([token_kept[0], token_got], axis=0))
    normed_in, norm_in_back = jax.vjp(layer_norm, inputs)
    norm_own = low_bits(normed_in)
    columns = join(columns_kept, columns_got, c, 0)
    qkv_piece = columns[:, :head_columns]
    wide_pieces = [
        jnp.concatenate(
            [
                columns[:, at + start : at + start + tile]
                for at in (head_columns, head_columns + wide_columns)
            ],
            axis=1,
        )
        for start in range(0, wide_columns, tile)
    ]
    size = wide_pieces[0].shape[0] // 2
    parts = join(parts_kept[0], parts_got, v, 2)
    parts_kept, parts_sent = both_halves(parts, c, 0)
    norm_u, norm_v, qkv_w, qkv_x, parts_got = stage(
        [(norm_own, "u"), (norm_own, "v"), (qkv_piece, "w"), (qkv_piece, "x"), (parts_sent[0], "c")]
    )
    parts = join(parts_kept, parts_got[None], c, 0)
    parts_kept, parts_sent = both_halves(parts, u, 0)
    norm_uv, qkv_wx, parts_got, cotangent_got = stage(
        [(norm_u, "v"), (qkv_w, "x"), (parts_sent[0], "u"), (cotangent_sent[0], "w")], [norm_v, qkv_x]
    )
    norm_in = weave(norm_own, norm_u, norm_v, norm_uv[:tok_rows], norm_uv[tok_rows:])
    full_qkv = square(qkv_piece, qkv_w, qkv_x, qkv_wx, spots)
    parts = join(parts_kept[0], parts_got, u, 1)
    output_piece, down_piece = parts[:output_span], parts[output_span:]
    down_pieces = [down_piece[: down_span // 2], down_piece[down_span // 2 :]]
    grad_out = wide_bits(jnp.concatenate([cotangent_kept[0], cotangent_got], axis=0)) * live
    grad_own = low_bits(grad_out)

    output_x, output_w, grad_u, grad_v, norm_other = stage(
        [
            (output_piece, "x"),
            (output_piece, "w"),
            (grad_own, "u"),
            (grad_own, "v"),
            (norm_in, "c"),
        ],
        [qkv_wx, cotangent_got],
    )
    first = attend(norm_in, full_qkv, tables)
    output_w, norm_other, _ = lax.optimization_barrier((output_w, norm_other, first[0]))
    output_wx, wide_w0a = stage([(output_w, "x"), (wide_pieces[0][:size], "w")])
    second = attend(norm_other, full_qkv, tables)
    output_x, second, grad_u, grad_v, wide_w0a = lax.optimization_barrier(
        (output_x, second, grad_u, grad_v, wide_w0a)
    )
    norm_in = (norm_in, norm_other)
    turned, attended = zip(first, second)
    full_output = square(output_piece, output_w, output_x, output_wx, spots)
    other, grad_uv, grad_vu = stage(
        [(ahead_rows([attended[1]], [full_output]), "c")] + corners(grad_u, grad_v)
    )
    total = ahead_rows([attended[0]], [full_output], [other])
    grad_uv, grad_vu, total = lax.optimization_barrier((grad_uv, grad_vu, total))
    grad_all = weave(grad_own, grad_u, grad_v, grad_uv, grad_vu)
    from_v, from_u, wide_w0b, wide_x0, grad_other = stage(
        fold_sends(total)
        + [(wide_pieces[0][size:], "w"), (wide_pieces[0], "x"), (grad_all, "c")],
        [wide_w0a],
    )
    grad_all = (grad_all, grad_other)
    kept, sends = fold(total, from_v, from_u)
    from_u, from_v, down_w0, wide_wx0 = stage(
        sends
        + [(down_pieces[0], "w"), (jnp.concatenate([wide_w0a, wide_w0b], axis=0), "x")],
        [wide_x0, grad_other],
    )
    after_attn = inputs + fold_end(kept, from_u, from_v)
    normed_mid, norm_mid_back = jax.vjp(layer_norm, after_attn)
    mid_own = low_bits(normed_mid)
    mid_u, mid_v, wide_w1a, down_x = stage(
        [(mid_own, "u"), (mid_own, "v"), (wide_pieces[1][:size], "w"), (down_piece, "x")],
        [wide_wx0, down_w0],
    )
    mid_uv, mid_vu, down_w1, down_wx0, wide_wx1a = stage(
        corners(mid_u, mid_v) + [(down_pieces[1], "w"), (down_w0, "x"), (wide_w1a, "x")],
        [down_x],
    )
    norm_mid = weave(mid_own, mid_u, mid_v, mid_uv, mid_vu)
    full_wide = [
        square(wide_pieces[0], jnp.concatenate([wide_w0a, wide_w0b], axis=0), wide_x0, wide_wx0, spots)
    ]
    half_rows = down_span // 2
    full_down = [square(down_pieces[0], down_w0, down_x[:half_rows], down_wx0, spots)]
    norm_other, wide_w1b, wide_x1, down_wx1 = stage(
        [
            (norm_mid, "c"),
            (wide_pieces[1][size:], "w"),
            (wide_pieces[1], "x"),
            (down_w1, "x"),
        ],
        [mid_uv, wide_wx1a, down_wx0],
    )
    norm_mid = (norm_mid, norm_other)

    first = hidden_pass(norm_mid[0], grad_all[0], full_wide[0], full_down[0])
    second = hidden_pass(norm_other, grad_all[1], full_wide[0], full_down[0])
    second, wide_w1b = lax.optimization_barrier((second, wide_w1b))
    passes = [(first, second)]
    wide_outers = [outer_rows(norm_mid, [first[1], second[1]])]
    far0, far_kept0, near0, near_kept0 = corner_blocks(wide_outers[0], w, x)
    wide_wx1b = swap(wide_w1b, "x")
    far_got0 = swap(far0, "x")
    full_wide.append(
        square(
            wide_pieces[1],
            jnp.concatenate([wide_w1a, wide_w1b], axis=0),
            wide_x1,
            jnp.concatenate([wide_wx1a, wide_wx1b], axis=0),
            spots,
        )
    )
    full_down.append(square(down_pieces[1], down_w1, down_x[half_rows:], down_wx1, spots))
    first = hidden_pass(norm_mid[0], grad_all[0], full_wide[1], full_down[1])
    second = hidden_pass(norm_mid[1], grad_all[1], full_wide[1], full_down[1])
    passes.append((first, second))
    grad_wide = [[made[side][1] for made in passes] for side in (0, 1)]
    hidden = [[made[side][0] for made in passes] for side in (0, 1)]
    far_got0, grad_wide[1] = lax.optimization_barrier((far_got0, grad_wide[1]))
    far_sum0 = plus(far_kept0, far_got0)
    wide_g0a, near_got0 = stage([(far_sum0[:size], "w"), (near0, "x")])
    other = swap(back_rows(grad_wide[1], full_wide), "c")
    wide_outers.append(outer_rows(norm_mid, [first[1], second[1]]))
    other, wide_outers[1], wide_g0a, near_got0 = lax.optimization_barrier(
        (other, wide_outers[1], wide_g0a, near_got0)
    )
    far1, far_kept1, near1, near_kept1 = corner_blocks(wide_outers[1], w, x)
    total = back_rows(grad_wide[0], full_wide, [other])
    from_v, from_u, far_got1 = stage(fold_sends(total) + [(far1, "x")])
    ahead = ahead_rows(hidden[1], full_down)
    down_outers = [outer_rows([made[0][0], made[1][0]], grad_all) for made in passes]
    down_blocks = [corner_blocks(outer, w, x) for outer in down_outers]
    down_far, down_far_kept, down_near, down_near_kept = (
        jnp.concatenate(blocks, axis=0) for blocks in zip(*down_blocks)
    )
    far_sum1 = plus(far_kept1, far_got1)
    kept, sends = fold(total, from_v, from_u)
    from_u, from_v, wide_g0b, near_got1 = stage(
        sends + [(far_sum0[size:], "w"), (near1, "x")], [down_far, ahead, far_got1]
    )
    grad_norm_mid = fold_end(kept, from_u, from_v)
    grad_after = grad_out + norm_mid_back(grad_norm_mid)[0]
    after_own = low_bits(grad_after)
    after_u, after_v, other, wide_g1a, down_far_got = stage(
        [
            (after_own, "u"),
            (after_own, "v"),
            (ahead, "c"),
            (far_sum1[:size], "w"),
            (down_far, "x"),
        ],
        [wide_g0b, near_got1],
    )
    down_sum = plus(down_far_kept, down_far_got)
    after_uv, after_vu, wide_g1b, down_near_got = stage(
        corners(after_u, after_v) + [(far_sum1[size:], "w"), (down_near, "x")], [other, down_far_got, wide_g1a]
    )
    total = ahead_rows(hidden[0], full_down, [other])
    after_all = weave(after_own, after_u, after_v, after_uv, after_vu)

    from_v, from_u, down_g0, after_other = stage(
        fold_sends(total) + [(down_sum[:half_rows], "w"), (after_all, "c")], [wide_g1b, down_near_got]
    )
    after_all = (after_all, after_other)
    first = attend_back(after_all[0], full_output, turned[0], tables)
    output_outer = outer_rows(attended, after_all)
    output_far, output_far_kept, output_near, output_near_kept = corner_blocks(output_outer, w, x)
    kept, sends = fold(total, from_v, from_u)
    from_u, from_v, down_g1, output_got = stage(
        sends + [(down_sum[half_rows:], "w"), (output_far, "x")],
        [first, after_other, down_g0, output_outer],
    )
    second = attend_back(after_other, full_output, turned[1], tables)
    grad_qkv = (first, second)
    ahead = back_rows([second], [full_qkv])
    mixed = low_bits((after_attn + fold_end(kept, from_u, from_v)) * live)
    other, mixed_got, output_got, output_near_got = stage(
        [
            (ahead, "c"),
            (mixed[tok_rows:], "w"),
            (plus(output_far_kept, output_got), "w"),
            (output_near, "x"),
        ],
        [down_g1],
    )
    qkv_outer = outer_rows(norm_in, grad_qkv)
    other, qkv_outer = lax.optimization_barrier((other, qkv_outer))
    qkv_far, qkv_far_kept, qkv_near, qkv_near_kept = corner_blocks(qkv_outer, w, x)
    qkv_got = swap(qkv_far, "x")
    total = back_rows([first], [full_qkv], [other])
    qkv_got, total = lax.optimization_barrier((qkv_got, total))
    from_v, from_u, qkv_got = stage(
        fold_sends(total) + [(plus(qkv_far_kept, qkv_got), "w")]
    )
    kept, sends = fold(total, from_v, from_u)
    from_u, from_v, qkv_near_got = stage(sends + [(qkv_near, "x")])
    grad_norm_in = fold_end(kept, from_u, from_v)
    token_grad = grad_after + norm_in_back(grad_norm_in)[0]
    token_got = swap(low_bits(token_grad[tok_rows:]), "w")

    def add_up(*values):
        return sum(wide_bits(value) for value in values)

    held = (
        (near_kept0, near_got0, wide_g0a, wide_g0b),
        (near_kept1, near_got1, wide_g1a, wide_g1b),
        (down_near_kept, down_near_got, down_g0, down_g1),
    )
    held, _ = lax.optimization_barrier((held, from_u))
    wide_totals = [
        add_up(kept, got, jnp.concatenate([top, bottom], axis=0)) for kept, got, top, bottom in held
    ]
    down_total = low_bits(wide_totals.pop())
    qkv_total = add_up(qkv_near_kept, qkv_near_got, qkv_got)
    output_total = low_bits(add_up(output_near_kept, output_near_got, output_got))

    wide_total = jnp.concatenate(
        [part[:, at : at + tile] for at in (0, tile) for part in wide_totals], axis=1
    )

    def columns_home(total, sizes):
        kept, sent = both_halves(total, c, 0)
        return join_columns(kept, swap(low_bits(sent), "c"), c, sizes)

    def rows_home(total):
        count = total.shape[1] // 4
        even = jnp.concatenate([total[:, :count], total[:, 2 * count : 3 * count]], axis=1)
        odd = jnp.concatenate([total[:, count : 2 * count], total[:, 3 * count :]], axis=1)
        sent = jnp.where(v == 0, odd, even)
        parts = join(jnp.where(v == 0, even, odd)[None], swap(sent, "v")[None], v, 0)
        kept, sent = both_halves(parts, u, 2)
        parts = join(kept[None], swap(sent, "u")[None], u, 0)
        kept, sent = both_halves(parts, c, 0)
        return wide_bits(join(kept[0][:, None], swap(sent, "c")[0][:, None], c, 1))

    gate_grad, up_grad = columns_home(wide_total, (wide_columns,) * 2)
    query_grad, key_grad, value_grad = columns_home(qkv_total, (HEAD_DIM,) * 3)
    output_grad, down_grad = rows_home(output_total), rows_home(down_total)
    token_got, gate_grad, up_grad, down_grad, output_grad = lax.optimization_barrier(
        (token_got, gate_grad, up_grad, down_grad, output_grad)
    )
    return (
        join(mixed[None, :tok_rows], mixed_got[None], w, 0),
        join(token_grad[None, :tok_rows], wide_bits(token_got)[None], w, 0),
        query_grad,
        key_grad,
        value_grad,
        output_grad.reshape(output_weight.shape),
        gate_grad,
        up_grad,
        down_grad.reshape(down_weight.shape),
    )


def paired_solution(mesh):
    pairs = Mesh(mesh.devices.reshape((2,) * 5), PAIRS)
    rows, columns = ("x", "c"), ("w", "u", "v")
    slots = P(rows, columns, None)
    weight = P(rows, columns)
    return jax.shard_map(
        paired_body,
        mesh=pairs,
        in_specs=(slots, slots, P(rows)) + (weight,) * 7,
        out_specs=(slots, slots) + (weight,) * 7,
        check_vma=False,
    )


def solution(mesh):
    if mesh.shape["ctx"] == 8 and mesh.shape["dp"] == 4:
        return paired_solution(mesh)
    in_specs = (
        P("dp", "ctx", None),
        P("dp", "ctx", None),
        P("dp"),
        P("dp", "ctx"),
        P("dp", "ctx"),
        P("dp", "ctx"),
        P("dp", "ctx"),
        P("dp", "ctx"),
        P("dp", "ctx"),
        P("dp", "ctx"),
    )
    out_specs = (
        P("dp", "ctx", None),
        P("dp", "ctx", None),
        P("dp", "ctx"),
        P("dp", "ctx"),
        P("dp", "ctx"),
        P("dp", "ctx"),
        P("dp", "ctx"),
        P("dp", "ctx"),
        P("dp", "ctx"),
    )
    return jax.shard_map(body, mesh=mesh, in_specs=in_specs, out_specs=out_specs, check_vma=False)
```

```python
import functools

import jax
import jax.numpy as jnp
from jax import lax
from jax.experimental import pallas as pl
from jax.experimental.pallas import tpu as pltpu
from jax.sharding import Mesh
from jax.sharding import PartitionSpec as P

HEADS = 16
HEAD_DIM = 128
FF = 8192


epsilon = 1e-05
rope_base = 10000.0


def layer_norm(values):
    centred = values - jnp.mean(values, axis=-1, keepdims=True)
    variance = jnp.mean(centred * centred, axis=-1, keepdims=True)
    return centred * lax.rsqrt(variance + epsilon)


def paired_positions(row_index, tok_rows, blocks):
    half_block = tok_rows // 2
    device = row_index // tok_rows
    offset = row_index % tok_rows
    return jnp.where(
        offset < half_block,
        device * half_block + offset,
        (2 * blocks - 1 - device) * half_block + offset - half_block,
    )


def rope_tables(positions):
    half_dim = HEAD_DIM // 2
    frequency = rope_base ** (-jnp.arange(half_dim, dtype=jnp.float32) / half_dim)
    angles = positions.astype(jnp.float32)[:, None] * frequency[None, :]
    return (jnp.cos(angles)[:, None, :], jnp.sin(angles)[:, None, :])


def rotate(values, cosine_table, sine_table):
    half_dim = values.shape[-1] // 2
    first_half = values[..., :half_dim]
    second_half = values[..., half_dim:]
    return jnp.concatenate(
        [
            first_half * cosine_table - second_half * sine_table,
            second_half * cosine_table + first_half * sine_table,
        ],
        axis=-1,
    )


def outer_sum(left, right):
    return lax.dot_general(
        left, right, (((0,), (0,)), ((), ())), preferred_element_type=jnp.float32
    )


def back_product(grad_rows, weight):
    return lax.dot_general(
        grad_rows, weight, (((1,), (1,)), ((), ())), preferred_element_type=jnp.float32
    )


def block_start(block, tile_span, blocks):
    upper_side = (block >= blocks // tile_span).astype(jnp.int32)
    lead_tile = jnp.where(
        upper_side == 0, block * tile_span, 2 * blocks - (block + 1) * tile_span
    ).astype(jnp.int32)
    return (lead_tile, upper_side)


def tile_starts(tiles, lead_tile, upper_side):
    zero_index = jnp.zeros((), jnp.int32)
    return (lead_tile, upper_side) + (zero_index,) * (tiles.ndim - 2)


def take_block(tiles, lead_tile, upper_side, tile_span):
    piece = lax.dynamic_slice(
        tiles, tile_starts(tiles, lead_tile, upper_side), (tile_span, 1) + tiles.shape[2:]
    )
    return piece.reshape((tile_span * tiles.shape[2],) + tiles.shape[3:])


def add_block(tiles, part, lead_tile, upper_side, tile_span):
    starts = tile_starts(tiles, lead_tile, upper_side)
    piece_shape = (tile_span, 1) + tiles.shape[2:]
    before = lax.dynamic_slice(tiles, starts, piece_shape)
    return lax.dynamic_update_slice(tiles, before + part.reshape(piece_shape), starts)


def block_scores(query_half, query_pos, key_block, key_pos):
    scores = jnp.einsum(
        "qhd,khd->hqk", query_half, key_block, preferred_element_type=jnp.float32
    ) * HEAD_DIM ** (-0.5)
    allowed = query_pos[:, None] >= key_pos[None, :]
    return jnp.where(allowed[None, :, :], scores, -1e30)


def attend_half(query_half, query_pos, tables, needed, tile_span, blocks):
    key_tiles, value_tiles, pos_tiles = tables
    row_count = query_half.shape[0]

    def scores_at(block):
        lead_tile, upper_side = block_start(block, tile_span, blocks)
        key_block = take_block(key_tiles, lead_tile, upper_side, tile_span)
        key_pos = take_block(pos_tiles, lead_tile, upper_side, tile_span)
        return (block_scores(query_half, query_pos, key_block, key_pos), lead_tile, upper_side)

    def total_step(block, carried):
        highest, total_mass = carried
        scores = scores_at(block)[0]
        new_highest = jnp.maximum(highest, jnp.max(scores, axis=-1))
        total_mass = total_mass * jnp.exp(highest - new_highest) + jnp.sum(
            jnp.exp(scores - new_highest[..., None]), axis=-1
        )
        return (new_highest, total_mass)

    start_high = jnp.full((HEADS, row_count), -1e30, jnp.float32)
    highest, total_mass = lax.fori_loop(
        0, needed, total_step, (start_high, jnp.zeros((HEADS, row_count), jnp.float32))
    )
    log_total = highest + jnp.log(total_mass)

    def value_step(block, output_rows):
        scores, lead_tile, upper_side = scores_at(block)
        soft_low = jnp.exp(scores - log_total[..., None]).astype(jnp.bfloat16)
        value_block = take_block(value_tiles, lead_tile, upper_side, tile_span)
        return output_rows + jnp.einsum(
            "hqk,khd->qhd", soft_low, value_block, preferred_element_type=jnp.float32
        )

    output_rows = lax.fori_loop(
        0, needed, value_step, jnp.zeros((row_count, HEADS, HEAD_DIM), jnp.float32)
    )
    return (output_rows, log_total)


def attend_half_back(
    query_half,
    query_pos,
    grad_half,
    log_total,
    centre,
    tables,
    needed,
    tile_span,
    blocks,
    key_grad,
    value_grad,
):
    key_tiles, value_tiles, pos_tiles = tables
    score_scale = HEAD_DIM ** (-0.5)

    def back_step(block, state):
        query_grad, key_acc, value_acc = state
        lead_tile, upper_side = block_start(block, tile_span, blocks)
        key_block = take_block(key_tiles, lead_tile, upper_side, tile_span)
        value_block = take_block(value_tiles, lead_tile, upper_side, tile_span)
        key_pos = take_block(pos_tiles, lead_tile, upper_side, tile_span)
        soft = jnp.exp(
            block_scores(query_half, query_pos, key_block, key_pos) - log_total[..., None]
        )
        value_part = jnp.einsum(
            "hqk,qhd->khd", soft.astype(jnp.bfloat16), grad_half, preferred_element_type=jnp.float32
        )
        grad_soft = jnp.einsum(
            "qhd,khd->hqk", grad_half, value_block, preferred_element_type=jnp.float32
        )
        grad_scores = (soft * (grad_soft - centre[..., None]) * score_scale).astype(jnp.bfloat16)
        query_grad = query_grad + jnp.einsum(
            "hqk,khd->qhd", grad_scores, key_block, preferred_element_type=jnp.float32
        )
        key_part = jnp.einsum(
            "hqk,qhd->khd", grad_scores, query_half, preferred_element_type=jnp.float32
        )
        key_acc = add_block(key_acc, key_part, lead_tile, upper_side, tile_span)
        value_acc = add_block(value_acc, value_part, lead_tile, upper_side, tile_span)
        return (query_grad, key_acc, value_acc)

    initial = (jnp.zeros(query_half.shape, jnp.float32), key_grad, value_grad)
    return lax.fori_loop(0, needed, back_step, initial)


def gather_weights(
    query_weight, key_weight, value_weight, output_weight, gate_weight, up_weight, down_weight
):
    row_parts = (
        lax.all_gather(query_weight, "dp", axis=0, tiled=True),
        lax.all_gather(key_weight, "dp", axis=0, tiled=True),
        lax.all_gather(value_weight, "dp", axis=0, tiled=True),
        lax.all_gather(output_weight, "dp", axis=0, tiled=True),
        lax.all_gather(gate_weight, "dp", axis=0, tiled=True),
        lax.all_gather(up_weight, "dp", axis=0, tiled=True),
        lax.all_gather(down_weight, "dp", axis=0, tiled=True),
    )
    return (
        lax.all_gather(row_parts[0], "ctx", axis=1, tiled=True),
        lax.all_gather(row_parts[1], "ctx", axis=1, tiled=True),
        lax.all_gather(row_parts[2], "ctx", axis=1, tiled=True),
        lax.all_gather(row_parts[3], "ctx", axis=1, tiled=True),
        lax.all_gather(row_parts[4], "ctx", axis=1, tiled=True),
        lax.all_gather(row_parts[5], "ctx", axis=1, tiled=True),
        lax.all_gather(row_parts[6], "ctx", axis=1, tiled=True),
    )


def fold_columns(running, operands, grads):
    norm_in_low, attended_low, norm_mid_low, hidden_low = operands
    columns = (
        lax.all_to_all(grads[0], "ctx", split_axis=1, concat_axis=0, tiled=True),
        lax.all_to_all(grads[1], "ctx", split_axis=1, concat_axis=0, tiled=True),
        lax.all_to_all(grads[2], "ctx", split_axis=1, concat_axis=0, tiled=True),
        lax.all_to_all(grads[3], "ctx", split_axis=1, concat_axis=0, tiled=True),
        lax.all_to_all(grads[4], "ctx", split_axis=1, concat_axis=0, tiled=True),
        lax.all_to_all(grads[5], "ctx", split_axis=1, concat_axis=0, tiled=True),
        lax.all_to_all(grads[6], "ctx", split_axis=1, concat_axis=0, tiled=True),
    )
    totals = tuple(running)
    norm_in_piece = lax.all_gather(norm_in_low, "ctx", axis=0, tiled=True)
    attended_piece = lax.all_gather(attended_low, "ctx", axis=0, tiled=True)
    norm_mid_piece = lax.all_gather(norm_mid_low, "ctx", axis=0, tiled=True)
    hidden_piece = lax.all_gather(hidden_low, "ctx", axis=0, tiled=True)
    lefts = (
        norm_in_piece,
        norm_in_piece,
        norm_in_piece,
        attended_piece,
        norm_mid_piece,
        norm_mid_piece,
        hidden_piece,
    )
    return list(
        tuple(
            (total + outer_sum(left, column) for total, left, column in zip(totals, lefts, columns))
        )
    )


def body(
    tokens,
    cotangent,
    counts,
    query_weight,
    key_weight,
    value_weight,
    output_weight,
    gate_weight,
    up_weight,
    down_weight,
):
    slot_count, tok_rows, model_width = tokens.shape
    blocks = lax.axis_size("ctx")
    ctx_index = lax.axis_index("ctx")
    seq_rows = tok_rows * blocks
    half_rows = tok_rows // 2
    proj_width = HEADS * HEAD_DIM
    tile_span = min(512, seq_rows // 2) // half_rows
    first_needed = ctx_index // tile_span + 1
    second_needed = (2 * blocks - 1 - ctx_index) // tile_span + 1
    own_positions = paired_positions(
        ctx_index * tok_rows + jnp.arange(tok_rows, dtype=jnp.int32), tok_rows, blocks
    )
    pos_tiles = paired_positions(jnp.arange(seq_rows, dtype=jnp.int32), tok_rows, blocks).reshape(
        blocks, 2, half_rows
    )
    cosine_table, sine_table = rope_tables(own_positions)

    def rotate_heads(projected):
        return rotate(
            projected.reshape(tok_rows, HEADS, HEAD_DIM), cosine_table, sine_table
        ).reshape(tok_rows, proj_width)

    running = [
        jnp.zeros((model_width, proj_width // blocks), jnp.float32),
        jnp.zeros((model_width, proj_width // blocks), jnp.float32),
        jnp.zeros((model_width, proj_width // blocks), jnp.float32),
        jnp.zeros((proj_width, model_width // blocks), jnp.float32),
        jnp.zeros((model_width, FF // blocks), jnp.float32),
        jnp.zeros((model_width, FF // blocks), jnp.float32),
        jnp.zeros((FF, model_width // blocks), jnp.float32),
    ]
    outputs = []
    token_grads = []
    for slot_index in range(slot_count):
        gathered = gather_weights(
            query_weight,
            key_weight,
            value_weight,
            output_weight,
            gate_weight,
            up_weight,
            down_weight,
        )
        full_query, full_key, full_value, full_output, full_gate, full_up, full_down = gathered
        live_mask = (slot_index < counts[0]).astype(jnp.float32)
        inputs = tokens[slot_index].astype(jnp.float32)
        normed_in, norm_in_back = jax.vjp(layer_norm, inputs)
        norm_in_low = normed_in.astype(jnp.bfloat16)
        query_proj = jnp.dot(norm_in_low, full_query, preferred_element_type=jnp.float32)
        key_proj = jnp.dot(norm_in_low, full_key, preferred_element_type=jnp.float32)
        value_proj = jnp.dot(norm_in_low, full_value, preferred_element_type=jnp.float32)
        query_rot, query_turn_back = jax.vjp(rotate_heads, query_proj)
        key_rot, key_turn_back = jax.vjp(rotate_heads, key_proj)
        query_heads = query_rot.astype(jnp.bfloat16).reshape(tok_rows, HEADS, HEAD_DIM)
        key_rows, value_rows = (
            lax.all_gather(key_rot.astype(jnp.bfloat16), "ctx", axis=0, tiled=True),
            lax.all_gather(value_proj.astype(jnp.bfloat16), "ctx", axis=0, tiled=True),
        )
        tables = (
            key_rows.reshape(blocks, 2, half_rows, HEADS, HEAD_DIM),
            value_rows.reshape(blocks, 2, half_rows, HEADS, HEAD_DIM),
            pos_tiles,
        )
        first_out, first_total = attend_half(
            query_heads[:half_rows],
            own_positions[:half_rows],
            tables,
            first_needed,
            tile_span,
            blocks,
        )
        second_out, second_total = attend_half(
            query_heads[half_rows:],
            own_positions[half_rows:],
            tables,
            second_needed,
            tile_span,
            blocks,
        )
        attended_wide = jnp.concatenate([first_out, second_out], axis=0)
        attended_low = attended_wide.reshape(tok_rows, proj_width).astype(jnp.bfloat16)
        after_attn = inputs + jnp.dot(attended_low, full_output, preferred_element_type=jnp.float32)
        normed_mid, norm_mid_back = jax.vjp(layer_norm, after_attn)
        norm_mid_low = normed_mid.astype(jnp.bfloat16)
        gate_proj = jnp.dot(norm_mid_low, full_gate, preferred_element_type=jnp.float32)
        up_proj = jnp.dot(norm_mid_low, full_up, preferred_element_type=jnp.float32)
        hidden, hidden_back = jax.vjp(
            lambda gate_in, up_in: jax.nn.silu(gate_in) * up_in, gate_proj, up_proj
        )
        hidden_low = hidden.astype(jnp.bfloat16)
        layer_out = after_attn + jnp.dot(hidden_low, full_down, preferred_element_type=jnp.float32)
        outputs.append((layer_out * live_mask).astype(jnp.bfloat16))
        grad_out = cotangent[slot_index].astype(jnp.float32) * live_mask
        grad_out_low = grad_out.astype(jnp.bfloat16)
        grad_gate_in, grad_up_in = hidden_back(back_product(grad_out_low, full_down))
        grad_gate_low = grad_gate_in.astype(jnp.bfloat16)
        grad_up_low = grad_up_in.astype(jnp.bfloat16)
        grad_norm_mid = back_product(grad_gate_low, full_gate) + back_product(grad_up_low, full_up)
        grad_after = grad_out + norm_mid_back(grad_norm_mid)[0]
        grad_after_low = grad_after.astype(jnp.bfloat16)
        grad_attended_low = back_product(grad_after_low, full_output).astype(jnp.bfloat16)
        grad_heads = grad_attended_low.reshape(tok_rows, HEADS, HEAD_DIM)
        centre = jnp.einsum("qhd,qhd->hq", grad_heads.astype(jnp.float32), attended_wide)
        empty_tiles = jnp.zeros((blocks, 2, half_rows, HEADS, HEAD_DIM), jnp.float32)
        first_query, key_acc, value_acc = attend_half_back(
            query_heads[:half_rows],
            own_positions[:half_rows],
            grad_heads[:half_rows],
            first_total,
            centre[:, :half_rows],
            tables,
            first_needed,
            tile_span,
            blocks,
            empty_tiles,
            empty_tiles,
        )
        second_query, key_acc, value_acc = attend_half_back(
            query_heads[half_rows:],
            own_positions[half_rows:],
            grad_heads[half_rows:],
            second_total,
            centre[:, half_rows:],
            tables,
            second_needed,
            tile_span,
            blocks,
            key_acc,
            value_acc,
        )
        grad_query_rot = jnp.concatenate([first_query, second_query], axis=0).reshape(
            tok_rows, proj_width
        )
        key_share, value_share = (
            lax.psum_scatter(
                key_acc.reshape(seq_rows, proj_width).astype(jnp.bfloat16),
                "ctx",
                scatter_dimension=0,
                tiled=True,
            ).astype(jnp.float32),
            lax.psum_scatter(
                value_acc.reshape(seq_rows, proj_width).astype(jnp.bfloat16),
                "ctx",
                scatter_dimension=0,
                tiled=True,
            ).astype(jnp.float32),
        )
        grad_query_low = query_turn_back(grad_query_rot)[0].astype(jnp.bfloat16)
        grad_key_low = key_turn_back(key_share)[0].astype(jnp.bfloat16)
        grad_value_low = value_share.astype(jnp.bfloat16)
        grad_norm_in = (
            back_product(grad_query_low, full_query)
            + back_product(grad_key_low, full_key)
            + back_product(grad_value_low, full_value)
        )
        token_grads.append(grad_after + norm_in_back(grad_norm_in)[0])
        grads = (
            grad_query_low,
            grad_key_low,
            grad_value_low,
            grad_after_low,
            grad_gate_low,
            grad_up_low,
            grad_out_low,
        )
        running = fold_columns(
            running, (norm_in_low, attended_low, norm_mid_low, hidden_low), grads
        )
    row_sums = (
        lax.psum_scatter(
            running[0].astype(jnp.bfloat16), "dp", scatter_dimension=0, tiled=True
        ).astype(jnp.float32),
        lax.psum_scatter(
            running[1].astype(jnp.bfloat16), "dp", scatter_dimension=0, tiled=True
        ).astype(jnp.float32),
        lax.psum_scatter(
            running[2].astype(jnp.bfloat16), "dp", scatter_dimension=0, tiled=True
        ).astype(jnp.float32),
        lax.psum_scatter(
            running[3].astype(jnp.bfloat16), "dp", scatter_dimension=0, tiled=True
        ).astype(jnp.float32),
        lax.psum_scatter(
            running[4].astype(jnp.bfloat16), "dp", scatter_dimension=0, tiled=True
        ).astype(jnp.float32),
        lax.psum_scatter(
            running[5].astype(jnp.bfloat16), "dp", scatter_dimension=0, tiled=True
        ).astype(jnp.float32),
        lax.psum_scatter(
            running[6].astype(jnp.bfloat16), "dp", scatter_dimension=0, tiled=True
        ).astype(jnp.float32),
    )
    return (
        jnp.stack(outputs),
        jnp.stack(token_grads),
        row_sums[0],
        row_sums[1],
        row_sums[2],
        row_sums[3],
        row_sums[4],
        row_sums[5],
        row_sums[6],
    )


PAIRS = ("x", "c", "w", "u", "v")
SWAP = ((0, 1), (1, 0))


def swap(value, axis):
    return lax.ppermute(value, axis, SWAP)


def join(own, other, bit, axis):
    low = jnp.where(bit == 0, own, other)
    high = jnp.where(bit == 0, other, own)
    return jnp.concatenate([low, high], axis=axis)


def low_bits(value):
    return value.astype(jnp.bfloat16)


def wide_bits(value):
    return value.astype(jnp.float32)


def half(value, bit, axis):
    size = value.shape[axis] // 2
    return lax.dynamic_slice_in_dim(value, bit * size, size, axis)


def stage(sends, waits=()):
    values, _ = lax.optimization_barrier((tuple(value for value, _ in sends), tuple(waits)))
    return [swap(value, axis) for value, (_, axis) in zip(values, sends)]


def both_halves(value, bit, axis):
    return half(value, bit, axis), half(value, 1 - bit, axis)


def column_halves(weights, c):
    return tuple(
        jnp.concatenate([half(weight, bit, 1) for weight in weights], axis=1) for bit in (c, 1 - c)
    )


def join_columns(kept, other, c, counts):
    grads, at = [], 0
    for count in counts:
        grads.append(join(wide_bits(kept[:, at : at + count]), wide_bits(other[:, at : at + count]), c, 1))
        at += count
    return grads


def square(own, beside, across, both, spots):
    first = join(own, across, spots["x"], 0)
    second = join(beside, both, spots["x"], 0)
    return join(first[None], second[None], spots["w"], 0)


def corner_blocks(grad, w, x):
    _, rows, columns = grad.shape
    rows //= 2
    parts = grad.reshape(2, 2, rows, columns)
    return [
        lax.dynamic_slice(parts, (at_w, at_x, 0, 0), (1, 1, rows, columns))[0, 0]
        for at_w, at_x in ((1 - w, 1 - x), (1 - w, x), (w, 1 - x), (w, x))
    ]


def plus(left, right):
    return low_bits(wide_bits(left) + wide_bits(right))


def weave(own, from_u, from_v, first_uv, second_uv):
    size = own.shape[0] // 2
    return jnp.concatenate(
        [
            own[:size],
            from_u[:size],
            from_v[:size],
            first_uv,
            own[size:],
            from_v[size:],
            from_u[size:],
            second_uv,
        ],
        axis=0,
    )


def corners(from_u, from_v):
    size = from_u.shape[0] // 2
    return [(from_u[:size], "v"), (from_v[size:], "u")]


def fold_sends(total):
    size = total.shape[0] // 8
    return [(total[2 * size : 4 * size], "v"), (total[6 * size :], "u")]


def fold(total, from_v, from_u):
    size = total.shape[0] // 8
    first = wide_bits(total[: 2 * size]) + wide_bits(from_v)
    second = wide_bits(total[4 * size : 6 * size]) + wide_bits(from_u)
    kept = jnp.concatenate([first[:size], second[:size]], axis=0)
    return kept, [(low_bits(first[size:]), "u"), (low_bits(second[size:]), "v")]


def fold_end(kept, from_u, from_v):
    return kept + jnp.concatenate([wide_bits(from_u), wide_bits(from_v)], axis=0)


ACROSS = (((1,), (1,)), ((), ()))
DOWN = (((0,), (0,)), ((), ()))
CHUNK = 256
TALL = 1024


def dot(left, right, dims=(((1,), (0,)), ((), ()))):
    return lax.dot_general(left, right, dims, preferred_element_type=jnp.float32)


def whole(shape):
    return pl.BlockSpec(shape, lambda *_: (0,) * len(shape))


def kernel_call(kernel, grid, in_specs, out_specs, out_shape, flops, size, scratch=(), weight=1000):
    return pl.pallas_call(
        kernel,
        grid=grid,
        in_specs=in_specs,
        out_specs=out_specs,
        out_shape=out_shape,
        scratch_shapes=scratch,
        compiler_params=pltpu.CompilerParams(vmem_limit_bytes=48 * 2**20),
        cost_estimate=pl.CostEstimate(
            flops=flops // weight, bytes_accessed=size // weight, transcendentals=0
        ),
    )


def turn(values, cosine, sine):
    return values * cosine + pltpu.roll(values, HEAD_DIM // 2, 1) * sine


def attend_kernel(rows_ref, weight_ref, cos_ref, sin_ref, pos_col_ref, pos_row_ref, *refs):
    turned_ref, out_ref = refs[-2:]
    key_pos = pos_row_ref[...]
    rows = rows_ref.shape[0]

    @pl.loop(0, rows // CHUNK)
    def _(i):
        at = pl.ds(pl.multiple_of(i * CHUNK, CHUNK), CHUNK)
        proj = dot(rows_ref[at, :], weight_ref[0])
        cosine, sine = cos_ref[at, :], sin_ref[at, :]
        turned_ref[at, :HEAD_DIM] = low_bits(turn(proj[:, :HEAD_DIM], cosine, sine))
        turned_ref[at, HEAD_DIM : 2 * HEAD_DIM] = low_bits(
            turn(proj[:, HEAD_DIM : 2 * HEAD_DIM], cosine, sine)
        )
        turned_ref[at, 2 * HEAD_DIM :] = low_bits(proj[:, 2 * HEAD_DIM :])

    @pl.loop(0, rows // CHUNK)
    def _(i):
        at = pl.ds(pl.multiple_of(i * CHUNK, CHUNK), CHUNK)
        scores = dot(turned_ref[at, :HEAD_DIM], turned_ref[:, HEAD_DIM : 2 * HEAD_DIM], ACROSS)
        scores = scores * HEAD_DIM ** (-0.5)
        scores = jnp.where(pos_col_ref[at, :] >= key_pos, scores, -1e30)
        shifted = jnp.exp(scores - jnp.max(scores, axis=1, keepdims=True))
        soft = shifted * (1.0 / jnp.sum(shifted, axis=1, keepdims=True))
        out_ref[at, :] = low_bits(dot(low_bits(soft), turned_ref[:, 2 * HEAD_DIM :]))


def attend(rows, weight, tables, *held):
    count, width = rows.shape
    span = weight.shape[2]
    return kernel_call(
        attend_kernel,
        (2,),
        [
            whole(rows.shape),
            pl.BlockSpec((1, width, span), lambda h: (h, 0, 0)),
            *[whole(table.shape) for table in tables],
            *[pl.BlockSpec(memory_space=pl.ANY) for _ in held],
        ],
        (
            pl.BlockSpec((count, span), lambda h: (0, h)),
            pl.BlockSpec((count, HEAD_DIM), lambda h: (0, h)),
        ),
        (
            jax.ShapeDtypeStruct((count, 2 * span), jnp.bfloat16),
            jax.ShapeDtypeStruct((count, 2 * HEAD_DIM), jnp.bfloat16),
        ),
        2 * count * width * 2 * span + 8 * count * count * HEAD_DIM * 3,
        count * width * 2 + weight.size * 2,
        weight=1,
    )(rows, weight, *tables, *held)


def attend_back_kernel(
    grad_ref, weight_ref, turned_ref, cos_ref, sin_ref, pos_col_ref, pos_row_ref, *refs
):
    out_ref, key_acc, value_acc = refs[-3:]
    key_pos = pos_col_ref[...]
    rows, width = grad_ref.shape
    scale = HEAD_DIM ** (-0.5)
    keys = turned_ref[:, HEAD_DIM : 2 * HEAD_DIM]
    values = turned_ref[:, 2 * HEAD_DIM :]
    key_acc[...] = jnp.zeros_like(key_acc)
    value_acc[...] = jnp.zeros_like(value_acc)
    for start in range(0, rows, CHUNK):
        at = slice(start, start + CHUNK)
        queries = turned_ref[at, :HEAD_DIM]
        grads = low_bits(
            dot(grad_ref[at, : width // 2], weight_ref[0], ACROSS)
            + dot(grad_ref[at, width // 2 :], weight_ref[1], ACROSS)
        )
        scores = dot(keys, queries, ACROSS) * scale
        scores = jnp.where(pos_row_ref[:, at] >= key_pos, scores, -1e30)
        shifted = jnp.exp(scores - jnp.max(scores, axis=0, keepdims=True))
        soft = shifted * (1.0 / jnp.sum(shifted, axis=0, keepdims=True))
        grad_soft = dot(values, grads, ACROSS)
        centre = jnp.sum(soft * grad_soft, axis=0, keepdims=True)
        grad_scores = low_bits(soft * (grad_soft - centre) * scale)
        value_acc[...] += dot(low_bits(soft), grads)
        key_acc[...] += dot(grad_scores, queries)
        query_grad = dot(grad_scores, keys, DOWN)
        out_ref[at, :HEAD_DIM] = low_bits(turn(query_grad, cos_ref[at, :], -sin_ref[at, :]))
    out_ref[:, HEAD_DIM : 2 * HEAD_DIM] = low_bits(turn(key_acc[...], cos_ref[...], -sin_ref[...]))
    out_ref[:, 2 * HEAD_DIM :] = low_bits(value_acc[...])


def attend_back(grads, weight, turned, tables, *held):
    count, width = grads.shape
    span = turned.shape[1] // 2
    return kernel_call(
        attend_back_kernel,
        (2,),
        [
            whole(grads.shape),
            pl.BlockSpec((2, HEAD_DIM, width // 2), lambda h: (0, h, 0)),
            pl.BlockSpec((count, span), lambda h: (0, h)),
            *[whole(table.shape) for table in tables],
            *[pl.BlockSpec(memory_space=pl.ANY) for _ in held],
        ],
        pl.BlockSpec((count, span), lambda h: (0, h)),
        jax.ShapeDtypeStruct(turned.shape, jnp.bfloat16),
        2 * count * width * 2 * HEAD_DIM + 20 * count * count * HEAD_DIM * 2,
        count * width * 2 + turned.size * 4,
        [pltpu.VMEM((count, HEAD_DIM), jnp.float32)] * 2,
    )(grads, weight, turned, *tables, *held)


def hidden_kernel(rows_ref, grad_ref, wide_ref, down_ref, hidden_ref, out_ref):
    rows, width = rows_ref.shape
    span = hidden_ref.shape[1]

    @pl.loop(0, rows // CHUNK)
    def _(i):
        at = pl.ds(pl.multiple_of(i * CHUNK, CHUNK), CHUNK)
        both = dot(rows_ref[at, :], wide_ref[0])
        gate, up = both[:, :span], both[:, span:]
        grad_hidden = dot(grad_ref[at, : width // 2], down_ref[0], ACROSS) + dot(
            grad_ref[at, width // 2 :], down_ref[1], ACROSS
        )
        sigma = jax.nn.sigmoid(gate)
        silu = gate * sigma
        hidden_ref[at, :] = low_bits(silu * up)
        out_ref[at, :span] = low_bits(grad_hidden * up * (sigma * (1.0 + gate * (1.0 - sigma))))
        out_ref[at, span:] = low_bits(grad_hidden * silu)


def hidden_pass(rows, grads, wide, down):
    count, width = rows.shape
    tile = wide.shape[2] // 2
    return kernel_call(
        hidden_kernel,
        (2,),
        [
            whole(rows.shape),
            whole(grads.shape),
            pl.BlockSpec((1, width, 2 * tile), lambda w: (w, 0, 0)),
            pl.BlockSpec((2, tile, width // 2), lambda w: (0, w, 0)),
        ],
        (
            pl.BlockSpec((count, tile), lambda w: (0, w)),
            pl.BlockSpec((count, 2 * tile), lambda w: (0, w)),
        ),
        (
            jax.ShapeDtypeStruct((count, 2 * tile), jnp.bfloat16),
            jax.ShapeDtypeStruct((count, 4 * tile), jnp.bfloat16),
        ),
        2 * count * width * 6 * tile,
        count * width * 4 + wide.size * 3,
    )(rows, grads, wide, down)


def back_kernel(counts, *refs):
    out_ref = refs[-1]
    pairs, more = counts
    lefts, weights = refs[:pairs], refs[pairs : 2 * pairs]
    added = refs[2 * pairs : 2 * pairs + more]
    rows, depth = lefts[0].shape

    @pl.loop(0, rows // TALL)
    def _(i):
        at = pl.ds(pl.multiple_of(i * TALL, TALL), TALL)
        total = sum(
            dot(left_ref[at, : depth // 2], weight_ref[0], ACROSS)
            + dot(left_ref[at, depth // 2 :], weight_ref[1], ACROSS)
            for left_ref, weight_ref in zip(lefts, weights)
        )
        for added_ref in added:
            total += wide_bits(added_ref[at, :])
        out_ref[at, :] = low_bits(total)


def back_rows(lefts, weights, added=(), held=()):
    count, depth = lefts[0].shape
    width = weights[0].shape[1]
    tile = 256
    return kernel_call(
        functools.partial(back_kernel, (len(lefts), len(added))),
        (width // tile,),
        [
            *[whole(left.shape) for left in lefts],
            *[pl.BlockSpec((2, tile, depth // 2), lambda i: (0, i, 0)) for _ in weights],
            *[pl.BlockSpec((count, tile), lambda i: (0, i)) for _ in added],
            *[pl.BlockSpec(memory_space=pl.ANY) for _ in held],
        ],
        pl.BlockSpec((count, tile), lambda i: (0, i)),
        jax.ShapeDtypeStruct((count, width), jnp.bfloat16),
        2 * count * width * depth * len(lefts),
        len(lefts) * (count * (width + depth) * 2 + weights[0].size * 2),
    )(*lefts, *weights, *added, *held)


def ahead_kernel(counts, *refs):
    out_ref = refs[-1]
    pairs, more = counts
    lefts, weights = refs[:pairs], refs[pairs : 2 * pairs]
    added = refs[2 * pairs : 2 * pairs + more]
    rows = lefts[0].shape[0]

    @pl.loop(0, rows // TALL)
    def _(i):
        at = pl.ds(pl.multiple_of(i * TALL, TALL), TALL)
        total = sum(dot(left_ref[at, :], weight_ref[0]) for left_ref, weight_ref in zip(lefts, weights))
        for added_ref in added:
            total += wide_bits(added_ref[at, :])
        out_ref[at, :] = low_bits(total)


def ahead_rows(lefts, weights, added=()):
    count, depth = lefts[0].shape
    span = weights[0].shape[2]
    tile = 512
    tiles = span // tile
    return kernel_call(
        functools.partial(ahead_kernel, (len(lefts), len(added))),
        (2, tiles),
        [
            *[whole(left.shape) for left in lefts],
            *[pl.BlockSpec((1, depth, tile), lambda w, t: (w, 0, t)) for _ in weights],
            *[pl.BlockSpec((count, tile), lambda w, t: (0, w * tiles + t)) for _ in added],
        ],
        pl.BlockSpec((count, tile), lambda w, t: (0, w * tiles + t)),
        jax.ShapeDtypeStruct((count, 2 * span), jnp.bfloat16),
        2 * count * depth * 2 * span * len(lefts),
        len(lefts) * (count * (2 * span + depth) * 2 + weights[0].size * 2),
    )(*lefts, *weights, *added)


def outer_kernel(left_ref, left_other_ref, right_ref, right_other_ref, out_ref):
    out_ref[0] = low_bits(
        dot(left_ref[...], right_ref[...], DOWN) + dot(left_other_ref[...], right_other_ref[...], DOWN)
    )


def outer_rows(lefts, rights):
    count, depth = lefts[0].shape
    span = rights[0].shape[1] // 2
    tile = min(depth, 1024)
    left_spec = pl.BlockSpec((count, tile), lambda w, i: (0, i))
    right_spec = pl.BlockSpec((count, span), lambda w, i: (0, w))
    return kernel_call(
        outer_kernel,
        (2, depth // tile),
        [left_spec, left_spec, right_spec, right_spec],
        pl.BlockSpec((1, tile, span), lambda w, i: (w, i, 0)),
        jax.ShapeDtypeStruct((2, depth, span), jnp.bfloat16),
        2 * 2 * count * depth * 2 * span,
        4 * count * (depth + 2 * span) + depth * span * 4,
    )(*lefts, *rights)


def row_tables(half_block, blocks, spots):
    block_at = jnp.arange(2 * half_block, dtype=jnp.int32)
    pieces = []
    for side, order in (("own", ((0, 0), (1, 0), (0, 1), (1, 1))), ("other", ((0, 0), (0, 1), (1, 0), (1, 1)))):
        far = spots["w"] if side == "own" else 1 - spots["w"]
        for flip_u, flip_v in order:
            block = far * 4 + (spots["u"] ^ flip_u) * 2 + (spots["v"] ^ flip_v)
            pieces.append(paired_positions(block * 2 * half_block + block_at, 2 * half_block, blocks))
    positions = jnp.concatenate(pieces)
    cosine, sine = rope_tables(positions)
    cosine, sine = cosine[:, 0], sine[:, 0]
    return (
        jnp.concatenate([cosine, cosine], axis=1),
        jnp.concatenate([-sine, sine], axis=1),
        positions[:, None],
        positions[None, :],
    )


def paired_body(
    tokens,
    cotangent,
    counts,
    query_weight,
    key_weight,
    value_weight,
    output_weight,
    gate_weight,
    up_weight,
    down_weight,
):
    tok_rows = tokens.shape[1]
    spots = {name: lax.axis_index(name) for name in PAIRS}
    c, w, x, u, v = (spots[name] for name in ("c", "w", "x", "u", "v"))
    tables = row_tables(tok_rows // 2, 8, spots)
    live = (w < counts[0]).astype(jnp.float32)
    tile = 256
    head_columns = 3 * HEAD_DIM
    wide_columns = gate_weight.shape[1] // 2
    output_span, down_span = output_weight.shape[0] // 4, down_weight.shape[0] // 4

    token_kept, token_sent = both_halves(tokens, w, 0)
    cotangent_kept, cotangent_sent = both_halves(cotangent, w, 0)
    columns_kept, columns_sent = column_halves(
        [query_weight, key_weight, value_weight, gate_weight, up_weight], c
    )
    parts = jnp.concatenate(
        [output_weight.reshape(2, 2, output_span, -1), down_weight.reshape(2, 2, down_span, -1)],
        axis=2,
    )
    parts_kept, parts_sent = both_halves(parts, v, 0)
    token_got, columns_got, parts_got = (
        swap(token_sent[0], "w"),
        swap(columns_sent, "c"),
        swap(parts_sent[0], "v"),
    )
    inputs = wide_bits(jnp.concatenate([token_kept[0], token_got], axis=0))
    normed_in, norm_in_back = jax.vjp(layer_norm, inputs)
    norm_own = low_bits(normed_in)
    columns = join(columns_kept, columns_got, c, 0)
    qkv_piece = columns[:, :head_columns]
    wide_pieces = [
        jnp.concatenate(
            [
                columns[:, at + start : at + start + tile]
                for at in (head_columns, head_columns + wide_columns)
            ],
            axis=1,
        )
        for start in range(0, wide_columns, tile)
    ]
    size = wide_pieces[0].shape[0] // 2
    parts = join(parts_kept[0], parts_got, v, 2)
    parts_kept, parts_sent = both_halves(parts, c, 0)
    norm_u, norm_v, qkv_w, qkv_x, parts_got = stage(
        [(norm_own, "u"), (norm_own, "v"), (qkv_piece, "w"), (qkv_piece, "x"), (parts_sent[0], "c")]
    )
    parts = join(parts_kept, parts_got[None], c, 0)
    parts_kept, parts_sent = both_halves(parts, u, 0)
    norm_uv, qkv_wx, parts_got, cotangent_got = stage(
        [(norm_u, "v"), (qkv_w, "x"), (parts_sent[0], "u"), (cotangent_sent[0], "w")], [norm_v, qkv_x]
    )
    norm_in = weave(norm_own, norm_u, norm_v, norm_uv[:tok_rows], norm_uv[tok_rows:])
    full_qkv = square(qkv_piece, qkv_w, qkv_x, qkv_wx, spots)
    parts = join(parts_kept[0], parts_got, u, 1)
    output_piece, down_piece = parts[:output_span], parts[output_span:]
    down_pieces = [down_piece[: down_span // 2], down_piece[down_span // 2 :]]
    grad_out = wide_bits(jnp.concatenate([cotangent_kept[0], cotangent_got], axis=0)) * live
    grad_own = low_bits(grad_out)

    output_x, output_w, grad_u, grad_v, norm_other = stage(
        [
            (output_piece, "x"),
            (output_piece, "w"),
            (grad_own, "u"),
            (grad_own, "v"),
            (norm_in, "c"),
        ],
        [qkv_wx, cotangent_got],
    )
    first = attend(norm_in, full_qkv, tables)
    output_w, norm_other, _ = lax.optimization_barrier((output_w, norm_other, first[0]))
    output_wx, wide_w0a = stage([(output_w, "x"), (wide_pieces[0][:size], "w")])
    second = attend(norm_other, full_qkv, tables)
    output_x, second, grad_u, grad_v, wide_w0a = lax.optimization_barrier(
        (output_x, second, grad_u, grad_v, wide_w0a)
    )
    norm_in = (norm_in, norm_other)
    turned, attended = zip(first, second)
    full_output = square(output_piece, output_w, output_x, output_wx, spots)
    other, grad_uv, grad_vu = stage(
        [(ahead_rows([attended[1]], [full_output]), "c")] + corners(grad_u, grad_v)
    )
    total = ahead_rows([attended[0]], [full_output], [other])
    grad_uv, grad_vu, total = lax.optimization_barrier((grad_uv, grad_vu, total))
    grad_all = weave(grad_own, grad_u, grad_v, grad_uv, grad_vu)
    from_v, from_u, wide_w0b, wide_x0, grad_other = stage(
        fold_sends(total)
        + [(wide_pieces[0][size:], "w"), (wide_pieces[0], "x"), (grad_all, "c")],
        [wide_w0a],
    )
    grad_all = (grad_all, grad_other)
    kept, sends = fold(total, from_v, from_u)
    from_u, from_v, down_w0, wide_wx0 = stage(
        sends
        + [(down_pieces[0], "w"), (jnp.concatenate([wide_w0a, wide_w0b], axis=0), "x")],
        [wide_x0, grad_other],
    )
    after_attn = inputs + fold_end(kept, from_u, from_v)
    normed_mid, norm_mid_back = jax.vjp(layer_norm, after_attn)
    mid_own = low_bits(normed_mid)
    mid_u, mid_v, wide_w1a, down_x = stage(
        [(mid_own, "u"), (mid_own, "v"), (wide_pieces[1][:size], "w"), (down_piece, "x")],
        [wide_wx0, down_w0],
    )
    mid_uv, mid_vu, down_w1, down_wx0, wide_wx1a = stage(
        corners(mid_u, mid_v) + [(down_pieces[1], "w"), (down_w0, "x"), (wide_w1a, "x")],
        [down_x],
    )
    norm_mid = weave(mid_own, mid_u, mid_v, mid_uv, mid_vu)
    full_wide = [
        square(wide_pieces[0], jnp.concatenate([wide_w0a, wide_w0b], axis=0), wide_x0, wide_wx0, spots)
    ]
    half_rows = down_span // 2
    full_down = [square(down_pieces[0], down_w0, down_x[:half_rows], down_wx0, spots)]
    norm_other, wide_w1b, wide_x1, down_wx1 = stage(
        [
            (norm_mid, "c"),
            (wide_pieces[1][size:], "w"),
            (wide_pieces[1], "x"),
            (down_w1, "x"),
        ],
        [mid_uv, wide_wx1a, down_wx0],
    )
    norm_mid = (norm_mid, norm_other)

    first = hidden_pass(norm_mid[0], grad_all[0], full_wide[0], full_down[0])
    second = hidden_pass(norm_other, grad_all[1], full_wide[0], full_down[0])
    second, wide_w1b = lax.optimization_barrier((second, wide_w1b))
    passes = [(first, second)]
    wide_outers = [outer_rows(norm_mid, [first[1], second[1]])]
    far0, far_kept0, near0, near_kept0 = corner_blocks(wide_outers[0], w, x)
    wide_wx1b = swap(wide_w1b, "x")
    far_got0 = swap(far0, "x")
    full_wide.append(
        square(
            wide_pieces[1],
            jnp.concatenate([wide_w1a, wide_w1b], axis=0),
            wide_x1,
            jnp.concatenate([wide_wx1a, wide_wx1b], axis=0),
            spots,
        )
    )
    full_down.append(square(down_pieces[1], down_w1, down_x[half_rows:], down_wx1, spots))
    first = hidden_pass(norm_mid[0], grad_all[0], full_wide[1], full_down[1])
    second = hidden_pass(norm_mid[1], grad_all[1], full_wide[1], full_down[1])
    passes.append((first, second))
    grad_wide = [[made[side][1] for made in passes] for side in (0, 1)]
    hidden = [[made[side][0] for made in passes] for side in (0, 1)]
    far_got0, grad_wide[1] = lax.optimization_barrier((far_got0, grad_wide[1]))
    far_sum0 = plus(far_kept0, far_got0)
    wide_g0a, near_got0 = stage([(far_sum0[:size], "w"), (near0, "x")])
    other = swap(back_rows(grad_wide[1], full_wide), "c")
    wide_outers.append(outer_rows(norm_mid, [first[1], second[1]]))
    other, wide_outers[1], wide_g0a, near_got0 = lax.optimization_barrier(
        (other, wide_outers[1], wide_g0a, near_got0)
    )
    far1, far_kept1, near1, near_kept1 = corner_blocks(wide_outers[1], w, x)
    total = back_rows(grad_wide[0], full_wide, [other])
    from_v, from_u, far_got1 = stage(fold_sends(total) + [(far1, "x")])
    ahead = ahead_rows(hidden[1], full_down)
    down_outers = [outer_rows([made[0][0], made[1][0]], grad_all) for made in passes]
    down_blocks = [corner_blocks(outer, w, x) for outer in down_outers]
    down_far, down_far_kept, down_near, down_near_kept = (
        jnp.concatenate(blocks, axis=0) for blocks in zip(*down_blocks)
    )
    far_sum1 = plus(far_kept1, far_got1)
    kept, sends = fold(total, from_v, from_u)
    from_u, from_v, wide_g0b, near_got1 = stage(
        sends + [(far_sum0[size:], "w"), (near1, "x")], [down_far, ahead, far_got1]
    )
    grad_norm_mid = fold_end(kept, from_u, from_v)
    grad_after = grad_out + norm_mid_back(grad_norm_mid)[0]
    after_own = low_bits(grad_after)
    after_u, after_v, other, wide_g1a, down_far_got = stage(
        [
            (after_own, "u"),
            (after_own, "v"),
            (ahead, "c"),
            (far_sum1[:size], "w"),
            (down_far, "x"),
        ],
        [wide_g0b, near_got1],
    )
    down_sum = plus(down_far_kept, down_far_got)
    after_uv, after_vu, wide_g1b, down_near_got = stage(
        corners(after_u, after_v) + [(far_sum1[size:], "w"), (down_near, "x")], [other, down_far_got, wide_g1a]
    )
    total = ahead_rows(hidden[0], full_down, [other])
    after_all = weave(after_own, after_u, after_v, after_uv, after_vu)

    from_v, from_u, down_g0, after_other = stage(
        fold_sends(total) + [(down_sum[:half_rows], "w"), (after_all, "c")], [wide_g1b, down_near_got]
    )
    after_all = (after_all, after_other)
    first = attend_back(after_all[0], full_output, turned[0], tables)
    output_outer = outer_rows(attended, after_all)
    output_far, output_far_kept, output_near, output_near_kept = corner_blocks(output_outer, w, x)
    kept, sends = fold(total, from_v, from_u)
    from_u, from_v, down_g1, output_got = stage(
        sends + [(down_sum[half_rows:], "w"), (output_far, "x")],
        [first, after_other, down_g0, output_outer],
    )
    second = attend_back(after_other, full_output, turned[1], tables)
    grad_qkv = (first, second)
    ahead = back_rows([second], [full_qkv])
    mixed = low_bits((after_attn + fold_end(kept, from_u, from_v)) * live)
    other, mixed_got, output_got, output_near_got = stage(
        [
            (ahead, "c"),
            (mixed[tok_rows:], "w"),
            (plus(output_far_kept, output_got), "w"),
            (output_near, "x"),
        ],
        [down_g1],
    )
    qkv_outer = outer_rows(norm_in, grad_qkv)
    other, qkv_outer = lax.optimization_barrier((other, qkv_outer))
    qkv_far, qkv_far_kept, qkv_near, qkv_near_kept = corner_blocks(qkv_outer, w, x)
    qkv_got = swap(qkv_far, "x")
    total = back_rows([first], [full_qkv], [other])
    qkv_got, total = lax.optimization_barrier((qkv_got, total))
    from_v, from_u, qkv_got = stage(
        fold_sends(total) + [(plus(qkv_far_kept, qkv_got), "w")]
    )
    kept, sends = fold(total, from_v, from_u)
    from_u, from_v, qkv_near_got = stage(sends + [(qkv_near, "x")])
    grad_norm_in = fold_end(kept, from_u, from_v)
    token_grad = grad_after + norm_in_back(grad_norm_in)[0]
    token_got = swap(low_bits(token_grad[tok_rows:]), "w")

    def add_up(*values):
        return sum(wide_bits(value) for value in values)

    held = (
        (near_kept0, near_got0, wide_g0a, wide_g0b),
        (near_kept1, near_got1, wide_g1a, wide_g1b),
        (down_near_kept, down_near_got, down_g0, down_g1),
    )
    held, _ = lax.optimization_barrier((held, from_u))
    wide_totals = [
        add_up(kept, got, jnp.concatenate([top, bottom], axis=0)) for kept, got, top, bottom in held
    ]
    down_total = low_bits(wide_totals.pop())
    qkv_total = add_up(qkv_near_kept, qkv_near_got, qkv_got)
    output_total = low_bits(add_up(output_near_kept, output_near_got, output_got))

    wide_total = jnp.concatenate(
        [part[:, at : at + tile] for at in (0, tile) for part in wide_totals], axis=1
    )

    def columns_home(total, sizes):
        kept, sent = both_halves(total, c, 0)
        return join_columns(kept, swap(low_bits(sent), "c"), c, sizes)

    def rows_home(total):
        count = total.shape[1] // 4
        even = jnp.concatenate([total[:, :count], total[:, 2 * count : 3 * count]], axis=1)
        odd = jnp.concatenate([total[:, count : 2 * count], total[:, 3 * count :]], axis=1)
        sent = jnp.where(v == 0, odd, even)
        parts = join(jnp.where(v == 0, even, odd)[None], swap(sent, "v")[None], v, 0)
        kept, sent = both_halves(parts, u, 2)
        parts = join(kept[None], swap(sent, "u")[None], u, 0)
        kept, sent = both_halves(parts, c, 0)
        return wide_bits(join(kept[0][:, None], swap(sent, "c")[0][:, None], c, 1))

    gate_grad, up_grad = columns_home(wide_total, (wide_columns,) * 2)
    query_grad, key_grad, value_grad = columns_home(qkv_total, (HEAD_DIM,) * 3)
    output_grad, down_grad = rows_home(output_total), rows_home(down_total)
    token_got, gate_grad, up_grad, down_grad, output_grad = lax.optimization_barrier(
        (token_got, gate_grad, up_grad, down_grad, output_grad)
    )
    return (
        join(mixed[None, :tok_rows], mixed_got[None], w, 0),
        join(token_grad[None, :tok_rows], wide_bits(token_got)[None], w, 0),
        query_grad,
        key_grad,
        value_grad,
        output_grad.reshape(output_weight.shape),
        gate_grad,
        up_grad,
        down_grad.reshape(down_weight.shape),
    )


def paired_solution(mesh):
    pairs = Mesh(mesh.devices.reshape((2,) * 5), PAIRS)
    rows, columns = ("x", "c"), ("w", "u", "v")
    slots = P(rows, columns, None)
    weight = P(rows, columns)
    return jax.shard_map(
        paired_body,
        mesh=pairs,
        in_specs=(slots, slots, P(rows)) + (weight,) * 7,
        out_specs=(slots, slots) + (weight,) * 7,
        check_vma=False,
    )


def solution(mesh):
    if mesh.shape["ctx"] == 8 and mesh.shape["dp"] == 4:
        return paired_solution(mesh)
    in_specs = (
        P("dp", "ctx", None),
        P("dp", "ctx", None),
        P("dp"),
        P("dp", "ctx"),
        P("dp", "ctx"),
        P("dp", "ctx"),
        P("dp", "ctx"),
        P("dp", "ctx"),
        P("dp", "ctx"),
        P("dp", "ctx"),
    )
    out_specs = (
        P("dp", "ctx", None),
        P("dp", "ctx", None),
        P("dp", "ctx"),
        P("dp", "ctx"),
        P("dp", "ctx"),
        P("dp", "ctx"),
        P("dp", "ctx"),
        P("dp", "ctx"),
        P("dp", "ctx"),
    )
    return jax.shard_map(body, mesh=mesh, in_specs=in_specs, out_specs=out_specs, check_vma=False)
```
